32 devices in a mesh: graph: 16 (over z, y, x), head: 2 (over core).
Axes of the slice: x: 2, y: 2, z: 4, core: 2. Of those that a mesh axis runs over, the one named last changes fastest.
Arguments:
- node_input: bfloat16 [32768, 512], P('graph', 'head'), may hold values from -6 to 6
- cotangent: bfloat16 [32768, 512], P('graph', 'head'), may hold values from -6 to 6
- norm_gain: bfloat16 [512], P('head'), may hold values from 0.5 to 1.5
- norm_bias: bfloat16 [512], P('head'), may hold values from -3 to 3
- query_weight: bfloat16 [512, 512], P(None, 'head'), may hold values from -0.25 to 0.25
- key_weight: bfloat16 [512, 512], P(None, 'head'), may hold values from -0.25 to 0.25
- value_weight: bfloat16 [512, 512], P(None, 'head'), may hold values from -0.25 to 0.25
- gate_weight: bfloat16 [512, 512], P(None, 'head'), may hold values from -0.25 to 0.25
- out_weight: bfloat16 [512, 512], P(None, 'head'), may hold values from -0.5 to 0.5
- adjacent_vertices: int32 [32768, 16], P('graph'), may hold values from 0 to 127, as said below
- active_vertex_tally: int32 [256], P('graph'), may hold values from 32 to 128, as said below
- training_period: int32 [256], P('graph'), may hold values 0 or 1
Outputs:
- layer_output: bfloat16 [32768, 512], P('graph', 'head')
- input_grad: bfloat16 [32768, 512], P('graph', 'head')
- gain_grad: float32 [512], P('head')
- bias_grad: float32 [512], P('head')
- query_grad: float32 [512, 512], P(None, 'head')
- key_grad: float32 [512, 512], P(None, 'head')
- value_grad: float32 [512, 512], P(None, 'head')
- gate_grad: float32 [512, 512], P(None, 'head')
- out_grad: float32 [512, 512], P(None, 'head')
The draws below stay inside these ranges and needn't reach their ends.
Inputs may be any that keep to these rules, and one draw needn't show every extreme that they name: `active_vertex_tally`: each index of graph holds one subgraph of 128 live nodes. `adjacent_vertices`: every entry names a live node of the row's own subgraph (below its node count).
All inputs are finite; a program needn't handle non-finite values. No bound on the sum of `training_period` on one device may be relied on, other than what follows from the above.
Results may differ from the reference program's by a relative error of at most 0.0025.
The reference program's roundings to bfloat16 on the way count: a program that leaves them out, or rounds other values in their place, can miss the bound.
Values may be sent and summed in bfloat16 or wider, within the bound.
A program may use at most 128 MiB of HBM per device.

```python
import jax
import jax.numpy as jnp
from jax import lax

D = 512
FOCUS_CHANNELS = 8
CHANNEL_DIM = 64
ADJACENT_NUMBER = 16
CLUSTER_VERTICES = 128
CLUSTER_PLACES = 16
CLUSTER_NUMBER = 256
VERTEX_PLACES = 32768


def counts_of(key):
    former_portion, latter_portion = jax.random.split(jax.random.fold_in(key, 7))
    cluster_sizes = jax.random.randint(former_portion, (CLUSTER_NUMBER,), CLUSTER_VERTICES // 4, CLUSTER_VERTICES + 1)
    chosen_vertices = jax.random.randint(latter_portion, (CLUSTER_NUMBER // CLUSTER_PLACES,), 0, CLUSTER_PLACES)
    fetched_vectors = jnp.arange(CLUSTER_NUMBER) % CLUSTER_PLACES == jnp.repeat(chosen_vertices, CLUSTER_PLACES)
    return jnp.where(fetched_vectors, CLUSTER_VERTICES, cluster_sizes).astype(jnp.int32)


def draw_active_vertex_tally(key, part):
    return counts_of(key)


def draw_adjacent_vertices(key, part):
    cluster_sizes = counts_of(key)
    upper_cutoff = jnp.repeat(cluster_sizes, CLUSTER_VERTICES)[:, None]
    return jax.random.randint(jax.random.fold_in(key, 11), (VERTEX_PLACES, ADJACENT_NUMBER), 0, upper_cutoff).astype(jnp.int32)


def touch_ends(values, own_key, least, top_value):
    longest = values.shape.index(max(values.shape))
    spots = []
    for shift in (0, 1):
        where = [jax.random.randint(jax.random.fold_in(own_key, axis), (), 0, length) for axis, length in enumerate(values.shape)]
        where[longest] = (where[longest] + shift) % values.shape[longest]
        spots.append(tuple(where))
    return values.at[spots[0]].set(least).at[spots[1]].set(top_value)


def shard_levels(stream_key, shape, pieces, low, high):
    loudness = 1.0
    for dim, shards_of in pieces:
        steps = jax.random.uniform(jax.random.fold_in(jax.random.fold_in(stream_key, 6), dim), (shards_of,), jnp.float32, low / len(pieces), high / len(pieces))
        loudness = loudness * jnp.repeat(jnp.exp(steps), shape[dim] // shards_of).reshape((-1,) + (1,) * (len(shape) - 1 - dim))
    return loudness


def bell_draw(rng, shape, deviation, bound, shards=(), kind=jnp.bfloat16):
    factor_of = shard_levels(rng, shape, shards, -0.22, 0.18) if shards else 1.0
    array = jax.random.normal(rng, shape, jnp.float32) * deviation * factor_of
    return jnp.minimum(jnp.maximum(array, -bound), bound).astype(kind)


def setup_inputs(seed: int = 0) -> dict:
    key_list = jax.random.split(jax.random.key(seed), 13)
    return {
        "node_input": bell_draw(key_list[0], (VERTEX_PLACES, D), 1.0, 6.0, ((0, 16), (1, 2))),
        "cotangent": bell_draw(key_list[1], (VERTEX_PLACES, D), 1.0, 6.0, ((0, 16), (1, 2))),
        "norm_gain": jnp.clip(1.0 + 0.1 * jax.random.normal(key_list[2], (D,), jnp.float32), 0.5, 1.5).astype(jnp.bfloat16),
        "norm_bias": bell_draw(key_list[3], (D,), 0.5, 3.0, ((0, 2),)),
        "query_weight": bell_draw(key_list[4], (D, D), D ** -0.5, 0.25, ((1, 2),)),
        "key_weight": bell_draw(key_list[5], (D, D), D ** -0.5, 0.25, ((1, 2),)),
        "value_weight": bell_draw(key_list[6], (D, D), D ** -0.5, 0.25, ((1, 2),)),
        "gate_weight": bell_draw(key_list[7], (D, D), D ** -0.5, 0.25, ((1, 2),)),
        "out_weight": bell_draw(key_list[8], (D, D), (D // 4) ** -0.5, 0.5, ((1, 2),)),
        "adjacent_vertices": draw_adjacent_vertices(jax.random.fold_in(key_list[12], 71), 0),
        "active_vertex_tally": draw_active_vertex_tally(jax.random.fold_in(key_list[12], 71), 0),
        "training_period": touch_ends((jax.random.randint(key_list[11], (CLUSTER_NUMBER,), 0, 4) < 1).astype(jnp.int32), jax.random.fold_in(key_list[11], 1), 0, 1),
    }


EPS = 1e-05
BETA = 0.9
HIGH_ACCURACY = lax.Precision.HIGHEST

@jax.custom_vjp
def low(v):
    return lax.optimization_barrier(v.astype(jnp.bfloat16)).astype(jnp.float32)

@jax.custom_vjp
def low_back(v):
    return v

def low_keep(v):
    return (low(v), None)

def low_pass(kept, grad):
    return (grad,)

def back_keep(v):
    return (v, None)

def back_low(kept, grad):
    return (low(grad),)
low.defvjp(low_keep, low_pass)
low_back.defvjp(back_keep, back_low)

def neighbour_attention(query_rows, key_rows, value_rows, adjacency_table):
    near_keys = key_rows[adjacency_table]
    near_values = value_rows[adjacency_table]
    attention_logits = jnp.einsum('phd,pjhd->phj', query_rows, near_keys, precision=HIGH_ACCURACY) * query_rows.shape[-1] ** (-0.5)
    attention_probabilities = jax.nn.softmax(attention_logits, axis=-1)
    return jnp.einsum('phj,pjhd->phd', attention_probabilities, near_values, precision=HIGH_ACCURACY)

def forward(node_input, gain, bias, wq, wk, wv, wg, wo, adjacency_table, active_vertex, retain_flag, frozen):
    feature_mean = lax.optimization_barrier(jnp.mean(node_input, axis=-1, keepdims=True))
    centred_input = node_input - feature_mean
    var = lax.optimization_barrier(jnp.mean(centred_input * centred_input, axis=-1, keepdims=True))
    normed_input = low(centred_input * lax.rsqrt(var + EPS) * gain + bias)
    query = low_back(jnp.dot(normed_input, wq, precision=HIGH_ACCURACY))
    key = low_back(jnp.dot(normed_input, wk, precision=HIGH_ACCURACY))
    value = low_back(jnp.dot(normed_input, wv, precision=HIGH_ACCURACY))
    gate = low_back(jnp.dot(normed_input, wg, precision=HIGH_ACCURACY))
    regrouped_source = (CLUSTER_NUMBER, CLUSTER_VERTICES, FOCUS_CHANNELS, CHANNEL_DIM)
    local = lax.map(jax.checkpoint(lambda t: neighbour_attention(*t)), (query.reshape(regrouped_source), key.reshape(regrouped_source), value.reshape(regrouped_source), adjacency_table))
    local = local.reshape(VERTEX_PLACES, D)
    q_pos = jax.nn.sigmoid(query).reshape(VERTEX_PLACES, FOCUS_CHANNELS, CHANNEL_DIM)
    k_pos = jax.nn.sigmoid(key).reshape(VERTEX_PLACES, FOCUS_CHANNELS, CHANNEL_DIM) * active_vertex[:, None, None]
    vals = value.reshape(VERTEX_PLACES, FOCUS_CHANNELS, CHANNEL_DIM)
    summary = jnp.einsum('nha,nhb->hab', k_pos, vals, precision=HIGH_ACCURACY)
    key_total = lax.optimization_barrier(jnp.sum(k_pos, axis=0))
    numer = jnp.einsum('nha,hab->nhb', q_pos, summary, precision=HIGH_ACCURACY)
    denom = jnp.einsum('nha,ha->nh', q_pos, key_total, precision=HIGH_ACCURACY)
    glob = (numer / denom[..., None]).reshape(VERTEX_PLACES, D)
    attended = local + retain_flag[:, None] * glob + (1.0 - retain_flag[:, None]) * frozen
    mixed = low((1.0 - BETA) * gate * attended + BETA * attended)
    return (node_input + jnp.dot(mixed, wo, precision=HIGH_ACCURACY), glob)

def reference(node_input, cotangent, norm_gain, norm_bias, query_weight, key_weight, value_weight, gate_weight, out_weight, adjacent_vertices, active_vertex_tally, training_period):
    active_vertex = (jnp.arange(CLUSTER_VERTICES, dtype=jnp.int32)[None, :] < active_vertex_tally[:, None]).reshape(VERTEX_PLACES).astype(jnp.float32)
    retain_flag = jnp.repeat((1 - training_period).astype(jnp.float32), CLUSTER_VERTICES)
    adjacency_table = adjacent_vertices.reshape(CLUSTER_NUMBER, CLUSTER_VERTICES, ADJACENT_NUMBER)
    inputs = (node_input, norm_gain, norm_bias, query_weight, key_weight, value_weight, gate_weight, out_weight)
    inputs = tuple((t.astype(jnp.float32) for t in inputs))
    ones = jnp.ones((VERTEX_PLACES,), jnp.float32)
    zeros = jnp.zeros((VERTEX_PLACES, D), jnp.float32)
    first_out, frozen = forward(*inputs, adjacency_table, active_vertex, ones, zeros)

    def apply(x, ga, bi, a, b, c, d, e):
        return forward(x, ga, bi, a, b, c, d, e, adjacency_table, active_vertex, retain_flag, frozen)
    result, pullback, unused_glob = jax.vjp(apply, *inputs, has_aux=True)
    grads = pullback(cotangent.astype(jnp.float32))
    return (result.astype(jnp.bfloat16), grads[0].astype(jnp.bfloat16), grads[1], grads[2], grads[3], grads[4], grads[5], grads[6], grads[7])
```

```python
import functools

import jax
import jax.numpy as jnp
from jax import lax
from jax.experimental import pallas as pl
from jax.experimental.pallas import tpu as pltpu
from jax.sharding import PartitionSpec as P

EPS = 1e-05
BETA = 0.9
LOG2E = 1.4426950408889634
BF = jnp.bfloat16
F32 = jnp.float32
MESH = pl.DeviceIdType.MESH
NODES = 128
CHUNKS = 16
QUERY, KEY, VALUE, GATE, OUT = 0, 1, 2, 3, 4


def nn(a, b):
    return lax.dot_general(a, b, (((1,), (0,)), ((), ())), preferred_element_type=F32)


def nt(a, b):
    return lax.dot_general(a, b, (((1,), (1,)), ((), ())), preferred_element_type=F32)


def tn(a, b):
    return lax.dot_general(a, b, (((0,), (0,)), ((), ())), preferred_element_type=F32)


def split(a):
    high = a.astype(BF)
    return high, (a - high.astype(F32)).astype(BF)


def rows_cat(*parts):
    return jnp.concatenate(parts, axis=0)


def lanes_cat(*parts):
    return jnp.concatenate(parts, axis=1)


def block(start, size):
    return pl.ds(pl.multiple_of(start * size, size), size)


def layer_kernel(
    groups,
    x,
    c,
    gain,
    bias,
    wq,
    wk,
    wv,
    wg,
    wo,
    adjacent,
    tally,
    period,
    layer_out,
    input_grad,
    small_grad,
    fin,
    xo,
    co,
    gbs,
    gbo,
    woo,
    wall,
    normed,
    mean_keep,
    rstd_keep,
    q,
    k,
    v,
    g,
    dmix,
    datt,
    att,
    prob,
    dq,
    dk,
    dv,
    low4,
    mix,
    mixo,
    dn_own,
    dn_send,
    dn_recv,
    st_send,
    st_recv,
    sum_part,
    sum_recv,
    sum_red,
    sum_hi,
    sum_full,
    part,
    psend,
    precv,
    zpart,
    zrecv,
    hrecv,
    gb_part,
    gb_recv,
    gb_hi,
    core_sems,
    mix_sems,
    dn_sems,
    ar_sems,
    arh_sems,
    w_sems,
    wh_sems,
    gb_sems,
    gbh_sems,
):
    A, B, C = groups
    L = A * B
    R, W = x.shape
    NB = R // NODES
    PAIRS = W // 128
    me = lax.axis_index("graph")
    head = lax.axis_index("head")
    other = 1 - head
    lo = lax.rem(me, L)
    hi = me // L
    al = lax.rem(lo, A)
    bl = lo // A

    def dev(h_, b_, a_):
        return (h_ * L + b_ * A + a_, head)

    lo_peers = [(hi * L + lax.rem(lo + d, L), head) for d in range(1, L)]
    hi_peers = [(lax.rem(hi + d, C) * L + lo, head) for d in range(1, C)]
    a_peers = [(lax.rem(al + d, A), dev(hi, bl, lax.rem(al + d, A))) for d in range(1, A)]
    b_peers = [(lax.rem(bl + d, B), dev(hi, lax.rem(bl + d, B), al)) for d in range(1, B)]
    partner = (me, other)
    own_rows = block(head, W)
    oth_rows = block(other, W)

    def send(src, dst, sems, index, to):
        copy = pltpu.make_async_remote_copy(
            src_ref=src,
            dst_ref=dst,
            send_sem=sems.at[(0,) + index],
            recv_sem=sems.at[(1,) + index],
            device_id=to,
            device_id_type=MESH,
        )
        copy.start()
        return copy

    barrier = pltpu.get_barrier_semaphore()
    greeted = [partner] + lo_peers + hi_peers
    for to in greeted:
        pl.semaphore_signal(barrier, inc=1, device_id=to, device_id_type=MESH)

    for i, w in enumerate((wq, wk, wv, wg)):
        wall[0:W, i * W : (i + 1) * W] = w[own_rows, :]
        wall[W : 2 * W, i * W : (i + 1) * W] = w[oth_rows, :]
    gbs[0:8, :] = jnp.broadcast_to(gain[...].astype(F32), (8, W))
    gbs[8:16, :] = jnp.broadcast_to(bias[...].astype(F32), (8, W))
    pl.semaphore_wait(barrier, len(greeted))

    XC = 4
    CC = 2
    core_copies = [send(gbs, gbo, core_sems, (0,), partner)]
    for i in range(XC):
        piece = pl.ds(i * (R // XC), R // XC)
        core_copies.append(send(x.at[piece], xo.at[piece], core_sems, (1 + i,), partner))
    core_copies.append(send(wo.at[oth_rows], woo, core_sems, (1 + XC,), partner))
    for i in range(CC):
        piece = pl.ds(i * (R // CC), R // CC)
        core_copies.append(send(c.at[piece], co.at[piece], core_sems, (2 + XC + i,), partner))

    RB = 256
    NR = R // RB

    def own_dmix(b, _):
        r = block(b, RB)
        dmix[r, :] = nt(c[r, :], wo[own_rows, :])
        return 0

    lax.fori_loop(0, NR, own_dmix, 0)

    sum_part[...] = jnp.zeros_like(sum_part)
    core_copies[0].wait_recv()
    gain_own, bias_own = gbs[0:1, :], gbs[8:9, :]
    gain_oth, bias_oth = gbo[0:1, :], gbo[8:9, :]
    lane_half = lax.broadcasted_iota(jnp.int32, (1, 128), 1) < 64
    node_of = lax.broadcasted_iota(jnp.int32, (NODES, 128), 0)

    def live_mask(s):
        return node_of < tally[s]

    def norm_block(b, carry):
        r = block(b, RB)
        xa = x[r, :].astype(F32)
        xb = xo[r, :].astype(F32)
        mean = (
            jnp.sum(xa, axis=1, keepdims=True) + jnp.sum(xb, axis=1, keepdims=True)
        ) * (1.0 / (2 * W))
        xa = xa - mean
        xb = xb - mean
        var = (
            jnp.sum(xa * xa, axis=1, keepdims=True) + jnp.sum(xb * xb, axis=1, keepdims=True)
        ) * (1.0 / (2 * W))
        rstd = lax.rsqrt(var + EPS)
        mean_keep[r, :] = jnp.broadcast_to(mean, (RB, 128))
        rstd_keep[r, :] = jnp.broadcast_to(rstd, (RB, 128))
        na = (xa * rstd * gain_own + bias_own).astype(BF)
        nb = (xb * rstd * gain_oth + bias_oth).astype(BF)
        normed[r, 0:W] = na
        normed[r, W : 2 * W] = nb
        kv = nn(lanes_cat(na, nb), wall[:, W : 3 * W])
        kk = kv[:, 0:W]
        vv = kv[:, W : 2 * W]
        k[r, :] = kk
        v[r, :] = vv
        sums, totals = carry
        new_sums, new_totals = [], []
        for p in range(PAIRS):
            ls = slice(p * 128, (p + 1) * 128)
            sig = jax.nn.sigmoid(kk[:, ls])
            kp = rows_cat(
                *[
                    jnp.where(live_mask(b * (RB // NODES) + i), sig[i * NODES : (i + 1) * NODES], 0.0)
                    for i in range(RB // NODES)
                ]
            )
            new_sums.append(sums[p] + tn(kp.astype(BF), vv[:, ls].astype(BF)))
            new_totals.append(totals[p] + jnp.sum(kp, axis=0, keepdims=True))
        return tuple(new_sums), tuple(new_totals)

    def zero_sums():
        return (
            tuple(jnp.zeros((128, 128), F32) for _ in range(PAIRS)),
            tuple(jnp.zeros((1, 128), F32) for _ in range(PAIRS)),
        )

    carry = zero_sums()
    for i in range(XC):
        core_copies[1 + i].wait_recv()
        carry = lax.fori_loop(i * (NR // XC), (i + 1) * (NR // XC), norm_block, carry)

    def pack_sums(slot, carry):
        sums, totals = carry
        for p in range(PAIRS):
            packed = jnp.where(lane_half, sums[p][0:64], sums[p][64:128])
            for j in range(8):
                sum_part[slot, p * 8 + j, 0:8, :] = packed[j * 8 : (j + 1) * 8]
            for j in range(CHUNKS):
                sum_part[slot, j, 8 + p : 9 + p, :] = totals[p]

    PER = CHUNKS // L

    def ar_scatter(slot):
        mine = block(lo, PER)
        sum_recv[slot, pl.ds(lo, 1)] = sum_part[slot, mine].reshape((1,) + sum_part.shape[1:][:0] + (PER,) + sum_part.shape[2:])
        copies = []
        for d in range(1, L):
            to = lax.rem(lo + d, L)
            copies.append(
                send(
                    sum_part.at[slot, block(to, PER)],
                    sum_recv.at[slot, lo],
                    ar_sems,
                    (slot, 0, d - 1),
                    lo_peers[d - 1],
                )
            )
        return copies

    def ar_reduce(slot, copies):
        for cp in copies:
            cp.wait()
        total = sum_recv[slot, 0]
        for i in range(1, L):
            total = total + sum_recv[slot, i]
        if C > 1:
            sum_hi[slot, pl.ds(hi, 1)] = total[None]
            sum_red[slot] = total
            hc = [
                send(sum_red.at[slot], sum_hi.at[slot, hi], arh_sems, (slot, d - 1), hi_peers[d - 1])
                for d in range(1, C)
            ]
            for cp in hc:
                cp.wait()
            total = sum_hi[slot, 0]
            for i in range(1, C):
                total = total + sum_hi[slot, i]
        sum_red[slot] = total
        sum_full[slot, block(lo, PER)] = total[:, 0:8, :]
        return [
            send(
                sum_red.at[slot, :, pl.ds(0, 8)],
                sum_full.at[slot, block(lo, PER)],
                ar_sems,
                (slot, 1, d - 1),
                lo_peers[d - 1],
            )
            for d in range(1, L)
        ]

    def ar_result(slot, copies):
        for cp in copies:
            cp.wait()
        mats, totals = [], []
        for p in range(PAIRS):
            packed = rows_cat(*[sum_full[slot, p * 8 + j] for j in range(8)])
            mats.append(
                rows_cat(jnp.where(lane_half, packed, 0.0), jnp.where(lane_half, 0.0, packed))
            )
            totals.append(sum_red[slot, 0, 8 + p : 9 + p, :])
        return mats, totals

    pack_sums(0, carry)
    ar0 = ar_scatter(0)

    for cp in core_copies[1 + XC :]:
        cp.wait_recv()

    def gate_block(b, _):
        r = block(b, RB)
        n = normed[r, :]
        q[r, :] = nn(n, wall[:, 0:W])
        gg = nn(n, wall[:, 3 * W : 4 * W])
        g[r, :] = gg
        dm = dmix[r, :] + nt(co[r, :], woo[...])
        dmix[r, :] = dm
        datt[r, :] = dm * ((1.0 - BETA) * gg + BETA)
        return 0

    lax.fori_loop(0, NR, gate_block, 0)
    ar0 = ar_reduce(0, ar0)

    half_row = jnp.where(lane_half, 1.0, 0.0)
    half_a = jnp.broadcast_to(half_row, (NODES, 128)).astype(BF)
    half_b = jnp.broadcast_to(1.0 - half_row, (NODES, 128)).astype(BF)

    def apart(a):
        return rows_cat(a * half_a, a * half_b)

    def joined(a):
        return jnp.where(lane_half, a[0:NODES], a[NODES : 2 * NODES])

    def forward_block(s, _):
        r = block(s, NODES)
        listed = adjacent[:, r]
        count = jnp.zeros((NODES, NODES), F32)
        for j in range(listed.shape[0]):
            count = count + jnp.where(listed[j : j + 1, :] == node_of, 1.0, 0.0)
        weight = jnp.where(count > 0.0, jnp.log(jnp.maximum(count, 1.0)) * LOG2E, -1e30)
        weight = lanes_cat(weight, weight)
        for p in range(PAIRS):
            ls = slice(p * 128, (p + 1) * 128)
            qh, ql = split(q[r, ls] * (0.125 * LOG2E))
            kh, kl = split(k[r, ls])
            vh, vl = split(v[r, ls])
            qbh = apart(qh)
            score = nt(lanes_cat(kh, kl, kh), lanes_cat(qbh, qbh, apart(ql))) + weight
            e = jnp.exp2(score - jnp.max(score, axis=0, keepdims=True))
            pr = e * (1.0 / jnp.sum(e, axis=0, keepdims=True))
            ph, plow = split(pr)
            prob[s, p, 0] = ph
            prob[s, p, 1] = plow
            o = tn(
                rows_cat(ph, plow),
                rows_cat(lanes_cat(vh, vl), lanes_cat(vh, jnp.zeros_like(vh))),
            )
            att[r, ls] = joined(o[:, 0:128] + o[:, 128:256])
        return 0

    lax.fori_loop(0, NB, forward_block, 0)

    mats, totals = ar_result(0, ar0)
    square = (2, 128, 128)
    same_head = (lax.broadcasted_iota(jnp.int32, (128, 128), 0) < 64) == (
        lax.broadcasted_iota(jnp.int32, (128, 128), 1) < 64
    )
    ones_bd = jnp.where(same_head, 1.0, 0.0).astype(BF)
    num_w, den_w, back_w = [], [], []
    for p in range(PAIRS):
        sh, sl = split(mats[p])
        th, tl = split(jnp.where(same_head, jnp.broadcast_to(totals[p], (128, 128)), 0.0))
        num_w.append(lanes_cat(sh, sl))
        den_w.append(rows_cat(th, tl))
        back_w.append(lanes_cat(sh, sh, sl))

    def glob_block(s, carry):
        r = block(s, NODES)
        keep = (1 - period[s]).astype(F32)
        sums, tots = carry
        new_sums, new_tots = [], []
        for p in range(PAIRS):
            ls = slice(p * 128, (p + 1) * 128)
            qp = jax.nn.sigmoid(q[r, ls])
            qpb = qp.astype(BF)
            num = nn(qpb, num_w[p])
            den = nt(qpb, den_w[p])
            inv = 1.0 / (den[:, 0:128] + den[:, 128:256])
            glob = (num[:, 0:128] + num[:, 128:256]) * inv
            at = att[r, ls] + glob
            mix[r, ls] = ((1.0 - BETA) * g[r, ls] * at + BETA * at).astype(BF)
            low4[GATE, r, ls] = (dmix[r, ls] * (1.0 - BETA) * at).astype(BF)
            dnum = (keep * datt[r, ls]) * inv
            dh, dl = split(dnum)
            th, tl = split(dnum * glob)
            dden = -nn(lanes_cat(th, tl), rows_cat(ones_bd, ones_bd))
            dqp = nt(lanes_cat(dh, dl, dh), back_w[p]) + dden * totals[p]
            dq[r, ls] = dqp * qp * (1.0 - qp)
            new_sums.append(sums[p] + tn(qpb, dh))
            new_tots.append(tots[p] + jnp.sum(dden * qp, axis=0, keepdims=True))
        return tuple(new_sums), tuple(new_tots)

    carry = lax.fori_loop(0, NB, glob_block, zero_sums())
    pack_sums(1, carry)
    ar1 = ar_scatter(1)
    mix_copy = send(mix, mixo, mix_sems, (0,), partner)

    KB = 512

    def weight_grads(kinds):
        def step(i, _):
            r = block(i, KB)
            n = normed[r, :]
            for kind in kinds:
                got = tn(n, low4[kind, r, :])
                part[kind, own_rows, :] += got[0:W]
                part[kind, oth_rows, :] += got[W : 2 * W]
            return 0

        for kind in kinds:
            part[kind] = jnp.zeros(part.shape[1:], F32)
        lax.fori_loop(0, R // KB, step, 0)

    def out_grads():
        def step(i, _):
            r = block(i, KB)
            cc = c[r, :]
            part[OUT, own_rows, :] += tn(mix[r, :], cc)
            part[OUT, oth_rows, :] += tn(mixo[r, :], cc)
            return 0

        part[OUT] = jnp.zeros(part.shape[1:], F32)
        lax.fori_loop(0, R // KB, step, 0)

    D = 2 * W
    PA = D // A
    PB = PA // B

    def w_scatter(w):
        psend[w] = part[w].astype(BF)
        return [
            send(psend.at[w, block(to, PA)], precv.at[w, i], w_sems, (w, 0, i), dv_)
            for i, (to, dv_) in enumerate(a_peers)
        ]

    def w_middle(w, copies):
        for cp in copies:
            cp.wait()
        total = part[w, block(al, PA), :]
        for i in range(A - 1):
            total = total + precv[w, i].astype(F32)
        zpart[w] = total
        return [
            send(zpart.at[w, block(to, PB)], zrecv.at[w, i], w_sems, (w, 1, i), dv_)
            for i, (to, dv_) in enumerate(b_peers)
        ]

    def w_spread(w, copies):
        for cp in copies:
            cp.wait()
        total = zpart[w, block(bl, PB), :]
        for i in range(B - 1):
            total = total + zrecv[w, i]
        here = pl.ds(pl.multiple_of(al * PA + bl * PB, PB), PB)
        if C > 1:
            hrecv[w, pl.ds(hi, 1)] = total[None]
            zpart[w, block(bl, PB), :] = total
            hc = [
                send(
                    zpart.at[w, block(bl, PB)], hrecv.at[w, hi], wh_sems, (w, d - 1), hi_peers[d - 1]
                )
                for d in range(1, C)
            ]
            for cp in hc:
                cp.wait()
            total = hrecv[w, 0]
            for i in range(1, C):
                total = total + hrecv[w, i]
        fin[w, here, :] = total.astype(BF)
        return [
            send(fin.at[w, here], fin.at[w, here], w_sems, (w, 2, i), dv_)
            for i, (_, dv_) in enumerate(b_peers)
        ]

    def w_gather(w, copies):
        for cp in copies:
            cp.wait()
        here = block(al, PA)
        return [
            send(fin.at[w, here], fin.at[w, here], w_sems, (w, 3, i), dv_)
            for i, (_, dv_) in enumerate(a_peers)
        ]

    def w_end(copies):
        for cp in copies:
            cp.wait()

    weight_grads((GATE,))
    gate_copies = w_scatter(GATE)
    mix_copy.wait_recv()
    out_grads()
    out_copies = w_scatter(OUT)

    def backward_block(s, _):
        r = block(s, NODES)
        for p in range(PAIRS):
            ls = slice(p * 128, (p + 1) * 128)
            qh, ql = split(q[r, ls])
            kh, kl = split(k[r, ls])
            vh, vl = split(v[r, ls])
            oh, ol = split(datt[r, ls])
            qbh, qbl = apart(qh), apart(ql)
            obh, obl = apart(oh), apart(ol)
            ph = prob[s, p, 0]
            plow = prob[s, p, 1]
            pr = ph.astype(F32) + plow.astype(F32)
            dp = nt(lanes_cat(vh, vl, vh), lanes_cat(obh, obh, obl))
            ds = pr * (dp - jnp.sum(pr * dp, axis=0, keepdims=True)) * 0.125
            dsh, dsl = split(ds)
            got = nn(ph, lanes_cat(obh, obl))
            dv[r, ls] = got[:, 0:128] + got[:, 128:256] + nn(plow, obh)
            got = nn(dsh, lanes_cat(qbh, qbl))
            dk[r, ls] = got[:, 0:128] + got[:, 128:256] + nn(dsl, qbh)
            got = tn(
                rows_cat(dsh, dsl),
                rows_cat(lanes_cat(kh, kl), lanes_cat(kh, jnp.zeros_like(kh))),
            )
            low4[QUERY, r, ls] = (dq[r, ls] + joined(got[:, 0:128] + got[:, 128:256])).astype(BF)
        return 0

    FIRST = NB // 2
    lax.fori_loop(0, FIRST, backward_block, 0)
    ar1 = ar_reduce(1, ar1)
    gate_copies = w_middle(GATE, gate_copies)
    out_copies = w_middle(OUT, out_copies)
    lax.fori_loop(FIRST, NB, backward_block, 0)
    gate_copies = w_spread(GATE, gate_copies)
    out_copies = w_spread(OUT, out_copies)
    weight_grads((QUERY,))
    query_copies = w_scatter(QUERY)
    gate_copies = w_gather(GATE, gate_copies)
    out_copies = w_gather(OUT, out_copies)

    mats, totals = ar_result(1, ar1)
    dsum = [m.astype(BF) for m in mats]

    def key_block(s, _):
        r = block(s, NODES)
        mask = live_mask(s)
        for p in range(PAIRS):
            ls = slice(p * 128, (p + 1) * 128)
            sig = jax.nn.sigmoid(k[r, ls])
            kp = jnp.where(mask, sig, 0.0)
            dkp = nt(v[r, ls].astype(BF), dsum[p]) + totals[p]
            low4[KEY, r, ls] = (dk[r, ls] + dkp * kp * (1.0 - sig)).astype(BF)
            low4[VALUE, r, ls] = (dv[r, ls] + nn(kp.astype(BF), dsum[p])).astype(BF)
        return 0

    lax.fori_loop(0, NB, key_block, 0)
    weight_grads((KEY, VALUE))
    key_copies = w_scatter(KEY)
    value_copies = w_scatter(VALUE)
    query_copies = w_middle(QUERY, query_copies)

    def normed_block(b, _):
        r = block(b, RB)
        grads = lanes_cat(*[low4[kind, r, :] for kind in (QUERY, KEY, VALUE, GATE)])
        dn = nt(grads, wall[...])
        dn_own[r, :] = dn[:, 0:W]
        dn_send[r, :] = dn[:, W : 2 * W]
        mean = mean_keep[r, 0:1]
        rstd = rstd_keep[r, 0:1]
        sa = dn[:, 0:W] * gain_own
        sb = dn[:, W : 2 * W] * gain_oth
        ha = (x[r, :].astype(F32) - mean) * rstd
        hb = (xo[r, :].astype(F32) - mean) * rstd
        s1 = jnp.sum(sa, axis=1, keepdims=True) + jnp.sum(sb, axis=1, keepdims=True)
        s2 = jnp.sum(sa * ha, axis=1, keepdims=True) + jnp.sum(sb * hb, axis=1, keepdims=True)
        st_send[r, :] = jnp.where(lane_half, s1, s2)
        return 0

    DC = 4
    dn_copies = []
    for i in range(DC):
        lax.fori_loop(i * (NR // DC), (i + 1) * (NR // DC), normed_block, 0)
        piece = pl.ds(i * (R // DC), R // DC)
        dn_copies.append(
            (
                send(dn_send.at[piece], dn_recv.at[piece], dn_sems, (0, i), partner),
                send(st_send.at[piece], st_recv.at[piece], dn_sems, (1, i), partner),
            )
        )
    query_copies = w_spread(QUERY, query_copies)
    key_copies = w_middle(KEY, key_copies)
    value_copies = w_middle(VALUE, value_copies)

    def out_block(b, _):
        r = block(b, RB)
        got = nn(mix[r, :], wo[own_rows, :]) + nn(mixo[r, :], wo[oth_rows, :])
        layer_out[r, :] = (x[r, :].astype(F32) + got).astype(BF)
        return 0

    lax.fori_loop(0, NR, out_block, 0)
    query_copies = w_gather(QUERY, query_copies)
    key_copies = w_spread(KEY, key_copies)
    value_copies = w_spread(VALUE, value_copies)

    def input_block(b, carry):
        gain_sum, bias_sum = carry
        r = block(b, RB)
        dn = dn_own[r, :] + dn_recv[r, :]
        st = st_send[r, :] + st_recv[r, :]
        mean = mean_keep[r, 0:1]
        rstd = rstd_keep[r, 0:1]
        s1 = st[:, 0:1] * (1.0 / (2 * W))
        s2 = st[:, 64:65] * (1.0 / (2 * W))
        ha = (x[r, :].astype(F32) - mean) * rstd
        inner = rstd * (dn * gain_own - s1 - ha * s2)
        input_grad[r, :] = (c[r, :].astype(F32) + inner).astype(BF)
        return (
            gain_sum + jnp.sum(dn * ha, axis=0, keepdims=True),
            bias_sum + jnp.sum(dn, axis=0, keepdims=True),
        )

    carry = (jnp.zeros((1, W), F32), jnp.zeros((1, W), F32))
    for i in range(DC):
        for cp in dn_copies[i]:
            cp.wait_recv()
        carry = lax.fori_loop(i * (NR // DC), (i + 1) * (NR // DC), input_block, carry)

    row = lax.broadcasted_iota(jnp.int32, (8, W), 0)
    terms = jnp.where(row == 0, carry[0], jnp.where(row == 1, carry[1], 0.0))
    gb_part[...] = terms
    gb_recv[pl.ds(lo, 1)] = terms[None]
    gb_copies = [
        send(gb_part, gb_recv.at[lo], gb_sems, (d - 1,), lo_peers[d - 1]) for d in range(1, L)
    ]
    key_copies = w_gather(KEY, key_copies)
    value_copies = w_gather(VALUE, value_copies)
    for cp in gb_copies:
        cp.wait()
    total = gb_recv[0]
    for i in range(1, L):
        total = total + gb_recv[i]
    if C > 1:
        gb_part[...] = total
        gb_hi[pl.ds(hi, 1)] = total[None]
        hc = [send(gb_part, gb_hi.at[hi], gbh_sems, (d - 1,), hi_peers[d - 1]) for d in range(1, C)]
        for cp in hc:
            cp.wait()
        total = gb_hi[0]
        for i in range(1, C):
            total = total + gb_hi[i]
    small_grad[...] = total
    for copies in (gate_copies, out_copies, query_copies, key_copies, value_copies):
        w_end(copies)
    for cp in core_copies:
        cp.wait_send()
    mix_copy.wait_send()
    for pair in dn_copies:
        for cp in pair:
            cp.wait_send()


def shards(
    groups,
    node_input,
    cotangent,
    norm_gain,
    norm_bias,
    query_weight,
    key_weight,
    value_weight,
    gate_weight,
    out_weight,
    adjacent_vertices,
    active_vertex_tally,
    training_period,
):
    A, B, C = groups
    L = A * B
    R, W = node_input.shape
    D = 2 * W
    NB = R // NODES
    PAIRS = W // 128
    PER = CHUNKS // L
    PA = D // A
    PB = PA // B
    VM = pltpu.VMEM
    dma = pltpu.SemaphoreType.DMA
    vmem = pl.BlockSpec(memory_space=pltpu.VMEM)
    smem = pl.BlockSpec(memory_space=pltpu.SMEM)
    layer_output, input_grad, small, fin = pl.pallas_call(
        functools.partial(layer_kernel, groups),
        name="layer_kernel",
        out_shape=(
            jax.ShapeDtypeStruct((R, W), BF),
            jax.ShapeDtypeStruct((R, W), BF),
            jax.ShapeDtypeStruct((8, W), F32),
            jax.ShapeDtypeStruct((5, D, W), BF),
        ),
        in_specs=[vmem] * 10 + [smem] * 2,
        out_specs=(vmem, vmem, vmem, vmem),
        scratch_shapes=[
            VM((R, W), BF),
            VM((R, W), BF),
            VM((16, W), F32),
            VM((16, W), F32),
            VM((W, W), BF),
            VM((D, 4 * W), BF),
            VM((R, D), BF),
            VM((R, 128), F32),
            VM((R, 128), F32),
            VM((R, W), F32),
            VM((R, W), F32),
            VM((R, W), F32),
            VM((R, W), F32),
            VM((R, W), F32),
            VM((R, W), F32),
            VM((R, W), F32),
            VM((NB, PAIRS, 2, NODES, 2 * NODES), BF),
            VM((R, W), F32),
            VM((R, W), F32),
            VM((R, W), F32),
            VM((4, R, W), BF),
            VM((R, W), BF),
            VM((R, W), BF),
            VM((R, W), F32),
            VM((R, W), F32),
            VM((R, W), F32),
            VM((R, 128), F32),
            VM((R, 128), F32),
            VM((2, CHUNKS, 16, 128), F32),
            VM((2, L, PER, 16, 128), F32),
            VM((2, PER, 16, 128), F32),
            VM((2, C, PER, 16, 128), F32),
            VM((2, CHUNKS, 8, 128), F32),
            VM((5, D, W), F32),
            VM((5, D, W), BF),
            VM((5, A - 1, PA, W), BF),
            VM((5, PA, W), F32),
            VM((5, B - 1, PB, W), F32),
            VM((5, C, PB, W), F32),
            VM((8, W), F32),
            VM((L, 8, W), F32),
            VM((C, 8, W), F32),
            dma((2, 8)),
            dma((2, 1)),
            dma((2, 2, 4)),
            dma((2, 2, 2, L - 1)),
            dma((2, 2, max(C - 1, 1))),
            dma((2, 5, 4, max(A, B) - 1)),
            dma((2, 5, max(C - 1, 1))),
            dma((2, L - 1)),
            dma((2, max(C - 1, 1))),
        ],
        compiler_params=pltpu.CompilerParams(
            collective_id=0, has_side_effects=True, vmem_limit_bytes=63 << 20
        ),
    )(
        node_input,
        cotangent,
        norm_gain.reshape(1, W),
        norm_bias.reshape(1, W),
        query_weight,
        key_weight,
        value_weight,
        gate_weight,
        out_weight,
        adjacent_vertices.T,
        active_vertex_tally,
        training_period,
    )
    full = fin.astype(F32)
    return (
        layer_output,
        input_grad,
        small[0],
        small[1],
        full[QUERY],
        full[KEY],
        full[VALUE],
        full[GATE],
        full[OUT],
    )


def factors(count):
    a = 4 if count % 4 == 0 else count
    b = 4 if count % (a * 4) == 0 else count // a
    return a, b, count // (a * b)


def solution(mesh):
    rows = P("graph", "head")
    cols = P(None, "head")
    return jax.shard_map(
        functools.partial(shards, factors(mesh.shape["graph"])),
        mesh=mesh,
        in_specs=(rows, rows, P("head"), P("head"))
        + (cols,) * 5
        + (P("graph", None), P("graph"), P("graph")),
        out_specs=(rows, rows, P("head"), P("head")) + (cols,) * 5,
        check_vma=False,
    )
```

```python
import functools

import jax
import jax.numpy as jnp
from jax import lax
from jax.experimental import pallas as pl
from jax.experimental.pallas import tpu as pltpu
from jax.sharding import PartitionSpec as P

EPS = 1e-05
BETA = 0.9
LOG2E = 1.4426950408889634
BF = jnp.bfloat16
F32 = jnp.float32
MESH = pl.DeviceIdType.MESH
NODES = 128
CHUNKS = 16
QUERY, KEY, VALUE, GATE, OUT = 0, 1, 2, 3, 4


def nn(a, b):
    return lax.dot_general(a, b, (((1,), (0,)), ((), ())), preferred_element_type=F32)


def nt(a, b):
    return lax.dot_general(a, b, (((1,), (1,)), ((), ())), preferred_element_type=F32)


def tn(a, b):
    return lax.dot_general(a, b, (((0,), (0,)), ((), ())), preferred_element_type=F32)


def split(a):
    high = a.astype(BF)
    return high, (a - high.astype(F32)).astype(BF)


def rows_cat(*parts):
    return jnp.concatenate(parts, axis=0)


def lanes_cat(*parts):
    return jnp.concatenate(parts, axis=1)


def block(start, size):
    return pl.ds(pl.multiple_of(start * size, size), size)


def layer_kernel(
    groups,
    x_hbm,
    c_hbm,
    gain,
    bias,
    wq,
    wk,
    wv,
    wg,
    wo_hbm,
    adjacent_hbm,
    tally,
    period,
    layer_out,
    input_grad,
    gain_grad,
    bias_grad,
    fin_hbm,
    x,
    xo,
    c,
    co,
    wo,
    adjacent,
    fin,
    gbs,
    gbo,
    woo,
    wall,
    normed,
    mean_keep,
    rstd_keep,
    q_sig,
    k_sig,
    qh,
    ql,
    kh,
    kl,
    vh,
    vl,
    g,
    dmix,
    datt,
    att,
    prob,
    dq,
    low4,
    mix,
    mixo,
    dn_recv,
    st_send,
    st_recv,
    sum_part,
    sum_recv,
    sum_red,
    sum_hi,
    sum_full,
    part,
    psend,
    precv,
    zpart,
    zrecv,
    hrecv,
    gb_part,
    gb_recv,
    gb_hi,
    load_sems,
    store_sems,
    core_sems,
    mix_sems,
    dn_sems,
    ar_sems,
    arh_sems,
    w_sems,
    wh_sems,
    gb_sems,
    gbh_sems,
):
    A, B, C = groups
    L = A * B
    R, W = x.shape
    NB = R // NODES
    PAIRS = W // 128
    me = lax.axis_index("graph")
    head = lax.axis_index("head")
    other = 1 - head
    lo = lax.rem(me, L)
    hi = me // L
    al = lax.rem(lo, A)
    bl = lo // A

    def dev(h_, b_, a_):
        return (h_ * L + b_ * A + a_, head)

    lo_peers = [(hi * L + lax.rem(lo + d, L), head) for d in range(1, L)]
    hi_peers = [(lax.rem(hi + d, C) * L + lo, head) for d in range(1, C)]
    a_peers = [(lax.rem(al + d, A), dev(hi, bl, lax.rem(al + d, A))) for d in range(1, A)]
    b_peers = [(lax.rem(bl + d, B), dev(hi, lax.rem(bl + d, B), al)) for d in range(1, B)]
    partner = (me, other)
    own_rows = block(head, W)
    oth_rows = block(other, W)

    def send(src, dst, sems, index, to):
        copy = pltpu.make_async_remote_copy(
            src_ref=src,
            dst_ref=dst,
            send_sem=sems.at[(0,) + index],
            recv_sem=sems.at[(1,) + index],
            device_id=to,
            device_id_type=MESH,
        )
        copy.start()
        return copy

    dk, dv, dn_own, dn_send = att, q_sig, g, dmix

    barrier = pltpu.get_barrier_semaphore()
    greeted = [partner] + lo_peers + hi_peers
    for to in greeted:
        pl.semaphore_signal(barrier, inc=1, device_id=to, device_id_type=MESH)

    loads = []

    def load(src, dst):
        copy = pltpu.make_async_copy(src, dst, load_sems.at[len(loads)])
        copy.start()
        loads.append(copy)
        return copy

    XC = 4
    x_loads = []
    for i in range(XC):
        piece = pl.ds(i * (R // XC), R // XC)
        x_loads.append(load(x_hbm.at[piece], x.at[piece]))
    wo_load = load(wo_hbm, wo)
    c_load = load(c_hbm, c)
    w_loads = []
    for i, w in ((1, wk), (2, wv), (0, wq), (3, wg)):
        cols = pl.ds(i * W, W)
        w_loads.append(load(w.at[own_rows], wall.at[pl.ds(0, W), cols]))
        w_loads.append(load(w.at[oth_rows], wall.at[pl.ds(W, W), cols]))
    adjacent_load = load(adjacent_hbm, adjacent)

    stores = []

    def store(src, dst):
        copy = pltpu.make_async_copy(src, dst, store_sems.at[len(stores)])
        copy.start()
        stores.append(copy)

    gbs[0:8, :] = jnp.broadcast_to(gain[...].astype(F32).reshape(1, W), (8, W))
    gbs[8:16, :] = jnp.broadcast_to(bias[...].astype(F32).reshape(1, W), (8, W))
    pl.semaphore_wait(barrier, len(greeted))

    CC = 2
    core_copies = [send(gbs, gbo, core_sems, (0,), partner)]
    for i in range(XC):
        piece = pl.ds(i * (R // XC), R // XC)
        x_loads[i].wait()
        core_copies.append(send(x.at[piece], xo.at[piece], core_sems, (1 + i,), partner))
    wo_load.wait()
    core_copies.append(send(wo.at[oth_rows], woo, core_sems, (1 + XC,), partner))
    c_load.wait()
    for i in range(CC):
        piece = pl.ds(i * (R // CC), R // CC)
        core_copies.append(send(c.at[piece], co.at[piece], core_sems, (2 + XC + i,), partner))

    RB = 256
    NR = R // RB

    def own_dmix(b, _):
        r = block(b, RB)
        dmix[r, :] = nt(c[r, :], wo[own_rows, :])
        return 0

    lax.fori_loop(0, NR, own_dmix, 0)

    sum_part[...] = jnp.zeros_like(sum_part)
    core_copies[0].wait_recv()
    gain_own, bias_own = gbs[0:1, :], gbs[8:9, :]
    gain_oth, bias_oth = gbo[0:1, :], gbo[8:9, :]
    lane_half = lax.broadcasted_iota(jnp.int32, (1, 128), 1) < 64
    node_of = lax.broadcasted_iota(jnp.int32, (NODES, 128), 0)

    def live_rows(first, a, count):
        node = lax.broadcasted_iota(jnp.int32, (NODES, a.shape[1]), 0)
        return rows_cat(
            *[
                jnp.where(node < tally[first + i], a[i * NODES : (i + 1) * NODES], 0.0)
                for i in range(count)
            ]
        )

    def norm_block(b, carry):
        r = block(b, RB)
        xa = x[r, :].astype(F32)
        xb = xo[r, :].astype(F32)
        mean = (
            jnp.sum(xa, axis=1, keepdims=True) + jnp.sum(xb, axis=1, keepdims=True)
        ) * (1.0 / (2 * W))
        xa = xa - mean
        xb = xb - mean
        var = (
            jnp.sum(xa * xa, axis=1, keepdims=True) + jnp.sum(xb * xb, axis=1, keepdims=True)
        ) * (1.0 / (2 * W))
        rstd = lax.rsqrt(var + EPS)
        mean_keep[r, :] = jnp.broadcast_to(mean, (RB, 128))
        rstd_keep[r, :] = jnp.broadcast_to(rstd, (RB, 128))
        na = (xa * rstd * gain_own + bias_own).astype(BF)
        nb = (xb * rstd * gain_oth + bias_oth).astype(BF)
        normed[r, 0:W] = na
        normed[r, W : 2 * W] = nb
        kv = nn(lanes_cat(na, nb), wall[:, W : 3 * W])
        kk = kv[:, 0:W]
        vv = kv[:, W : 2 * W]
        kh[r, :], kl[r, :] = split(kk)
        vbf, vlow = split(vv)
        vh[r, :] = vbf
        vl[r, :] = vlow
        sig = jax.nn.sigmoid(kk)
        k_sig[r, :] = sig
        kp = live_rows(b * (RB // NODES), sig, RB // NODES)
        kpb = kp.astype(BF)
        sums, totals = carry
        new_sums, new_totals = [], []
        for p in range(PAIRS):
            ls = slice(p * 128, (p + 1) * 128)
            new_sums.append(sums[p] + tn(kpb[:, ls], vbf[:, ls]))
            new_totals.append(totals[p] + jnp.sum(kp[:, ls], axis=0, keepdims=True))
        return tuple(new_sums), tuple(new_totals)

    def zero_sums():
        return (
            tuple(jnp.zeros((128, 128), F32) for _ in range(PAIRS)),
            tuple(jnp.zeros((1, 128), F32) for _ in range(PAIRS)),
        )

    for cp in w_loads[0:4]:
        cp.wait()
    carry = zero_sums()
    for i in range(XC):
        core_copies[1 + i].wait_recv()
        carry = lax.fori_loop(i * (NR // XC), (i + 1) * (NR // XC), norm_block, carry)

    def pack_sums(slot, carry):
        sums, totals = carry
        for p in range(PAIRS):
            packed = jnp.where(lane_half, sums[p][0:64], sums[p][64:128])
            for j in range(8):
                sum_part[slot, p * 8 + j, 0:8, :] = packed[j * 8 : (j + 1) * 8]
            for j in range(CHUNKS):
                sum_part[slot, j, 8 + p : 9 + p, :] = totals[p]

    PER = CHUNKS // L

    def ar_scatter(slot):
        mine = block(lo, PER)
        sum_recv[slot, pl.ds(lo, 1)] = sum_part[slot, mine].reshape((1,) + sum_part.shape[1:][:0] + (PER,) + sum_part.shape[2:])
        copies = []
        for d in range(1, L):
            to = lax.rem(lo + d, L)
            copies.append(
                send(
                    sum_part.at[slot, block(to, PER)],
                    sum_recv.at[slot, lo],
                    ar_sems,
                    (slot, 0, d - 1),
                    lo_peers[d - 1],
                )
            )
        return copies

    def ar_reduce(slot, copies):
        for cp in copies:
            cp.wait()
        total = sum_recv[slot, 0]
        for i in range(1, L):
            total = total + sum_recv[slot, i]
        if C > 1:
            sum_hi[slot, pl.ds(hi, 1)] = total[None]
            sum_red[slot] = total
            hc = [
                send(sum_red.at[slot], sum_hi.at[slot, hi], arh_sems, (slot, d - 1), hi_peers[d - 1])
                for d in range(1, C)
            ]
            for cp in hc:
                cp.wait()
            total = sum_hi[slot, 0]
            for i in range(1, C):
                total = total + sum_hi[slot, i]
        sum_red[slot] = total
        sum_full[slot, block(lo, PER)] = total[:, 0:8, :]
        return [
            send(
                sum_red.at[slot, :, pl.ds(0, 8)],
                sum_full.at[slot, block(lo, PER)],
                ar_sems,
                (slot, 1, d - 1),
                lo_peers[d - 1],
            )
            for d in range(1, L)
        ]

    def ar_result(slot, copies):
        for cp in copies:
            cp.wait()
        mats, totals = [], []
        for p in range(PAIRS):
            packed = rows_cat(*[sum_full[slot, p * 8 + j] for j in range(8)])
            mats.append(
                rows_cat(jnp.where(lane_half, packed, 0.0), jnp.where(lane_half, 0.0, packed))
            )
            totals.append(sum_red[slot, 0, 8 + p : 9 + p, :])
        return mats, totals

    pack_sums(0, carry)
    ar0 = ar_scatter(0)

    for cp in w_loads[4:]:
        cp.wait()
    for cp in core_copies[1 + XC :]:
        cp.wait_recv()

    def gate_block(b, _):
        r = block(b, RB)
        n = normed[r, :]
        qq = nn(n, wall[:, 0:W])
        q_sig[r, :] = jax.nn.sigmoid(qq)
        qh[r, :], ql[r, :] = split(qq * (0.125 * LOG2E))
        gg = nn(n, wall[:, 3 * W : 4 * W])
        g[r, :] = gg
        dm = dmix[r, :] + nt(co[r, :], woo[...])
        dmix[r, :] = dm
        datt[r, :] = dm * ((1.0 - BETA) * gg + BETA)
        return 0

    lax.fori_loop(0, NR, gate_block, 0)
    ar0 = ar_reduce(0, ar0)

    half_row = jnp.where(lane_half, 1.0, 0.0)
    half_a = jnp.broadcast_to(half_row, (NODES, 128)).astype(BF)
    half_b = jnp.broadcast_to(1.0 - half_row, (NODES, 128)).astype(BF)

    def apart(a):
        return rows_cat(a * half_a, a * half_b)

    def joined(a):
        return jnp.where(lane_half, a[0:NODES], a[NODES : 2 * NODES])

    FU = 4
    lanes = [slice(p * 128, (p + 1) * 128) for p in range(PAIRS)]

    def forward_block(i, _):
        chains = [(i * FU + u, p) for u in range(FU) for p in range(PAIRS)]
        weights = []
        for u in range(FU):
            listed = adjacent[:, block(i * FU + u, NODES)]
            count = jnp.zeros((NODES, NODES), F32)
            for j in range(listed.shape[0]):
                count = count + jnp.where(listed[j : j + 1, :] == node_of, 1.0, 0.0)
            weight = jnp.where(count > 0.0, jnp.log(jnp.maximum(count, 1.0)) * LOG2E, -1e30)
            weights.append(lanes_cat(weight, weight))
        scores = []
        for s, p in chains:
            r, ls = block(s, NODES), lanes[p]
            high, low = kh[r, ls], kl[r, ls]
            qbh = apart(qh[r, ls])
            scores.append(
                nt(lanes_cat(high, low, high), lanes_cat(qbh, qbh, apart(ql[r, ls])))
            )
        probs = []
        for j, score in enumerate(scores):
            score = score + weights[j // PAIRS]
            e = jnp.exp2(score - jnp.max(score, axis=0, keepdims=True))
            probs.append(split(e * (1.0 / jnp.sum(e, axis=0, keepdims=True))))
        for (s, p), (high, low) in zip(chains, probs):
            prob[s, p, 0] = high
            prob[s, p, 1] = low
        for (s, p), (high, low) in zip(chains, probs):
            r, ls = block(s, NODES), lanes[p]
            vhigh = vh[r, ls]
            o = tn(
                rows_cat(high, low),
                rows_cat(lanes_cat(vhigh, vl[r, ls]), lanes_cat(vhigh, jnp.zeros_like(vhigh))),
            )
            att[r, ls] = joined(o[:, 0:128] + o[:, 128:256])
        return 0

    adjacent_load.wait()
    lax.fori_loop(0, NB // FU, forward_block, 0)

    mats, totals = ar_result(0, ar0)
    square = (2, 128, 128)
    same_head = (lax.broadcasted_iota(jnp.int32, (128, 128), 0) < 64) == (
        lax.broadcasted_iota(jnp.int32, (128, 128), 1) < 64
    )
    ones_bd = jnp.where(same_head, 1.0, 0.0).astype(BF)
    num_w, den_w, back_w = [], [], []
    for p in range(PAIRS):
        sh, sl = split(mats[p])
        th, tl = split(jnp.where(same_head, jnp.broadcast_to(totals[p], (128, 128)), 0.0))
        num_w.append(lanes_cat(sh, sl))
        den_w.append(rows_cat(th, tl))
        back_w.append(lanes_cat(sh, sh, sl))

    GU = 4

    def glob_block(i, carry):
        r = block(i, GU * NODES)
        keep = [(1 - period[i * GU + u]).astype(F32) for u in range(GU)]
        sums, tots = carry
        new_sums, new_tots = [], []
        for p in range(PAIRS):
            ls = lanes[p]
            qp = q_sig[r, ls]
            qpb = qp.astype(BF)
            num = nn(qpb, num_w[p])
            den = nt(qpb, den_w[p])
            inv = 1.0 / (den[:, 0:128] + den[:, 128:256])
            glob = (num[:, 0:128] + num[:, 128:256]) * inv
            at = att[r, ls] + glob
            mix[r, ls] = ((1.0 - BETA) * g[r, ls] * at + BETA * at).astype(BF)
            low4[GATE, r, ls] = (dmix[r, ls] * (1.0 - BETA) * at).astype(BF)
            da = datt[r, ls]
            dnum = rows_cat(*[keep[u] * da[u * NODES : (u + 1) * NODES] for u in range(GU)]) * inv
            dh, dl = split(dnum)
            th, tl = split(dnum * glob)
            dden = -nn(lanes_cat(th, tl), rows_cat(ones_bd, ones_bd))
            dqp = nt(lanes_cat(dh, dl, dh), back_w[p]) + dden * totals[p]
            dq[r, ls] = dqp * qp * (1.0 - qp)
            new_sums.append(sums[p] + tn(qpb, dh))
            new_tots.append(tots[p] + jnp.sum(dden * qp, axis=0, keepdims=True))
        return tuple(new_sums), tuple(new_tots)

    carry = lax.fori_loop(0, NB // GU, glob_block, zero_sums())
    pack_sums(1, carry)
    ar1 = ar_scatter(1)
    mix_copy = send(mix, mixo, mix_sems, (0,), partner)

    KB = 512

    def weight_grads(kinds):
        def step(i, _):
            r = block(i, KB)
            n = normed[r, :]
            for kind in kinds:
                got = tn(n, low4[kind, r, :])
                part[kind, own_rows, :] += got[0:W]
                part[kind, oth_rows, :] += got[W : 2 * W]
            return 0

        for kind in kinds:
            part[kind] = jnp.zeros(part.shape[1:], F32)
        lax.fori_loop(0, R // KB, step, 0)

    def out_grads():
        def step(i, _):
            r = block(i, KB)
            cc = c[r, :]
            part[OUT, own_rows, :] += tn(mix[r, :], cc)
            part[OUT, oth_rows, :] += tn(mixo[r, :], cc)
            return 0

        part[OUT] = jnp.zeros(part.shape[1:], F32)
        lax.fori_loop(0, R // KB, step, 0)

    D = 2 * W
    PA = D // A
    PB = PA // B

    def w_scatter(w):
        psend[w] = part[w].astype(BF)
        return [
            send(psend.at[w, block(to, PA)], precv.at[w, i], w_sems, (w, 0, i), dv_)
            for i, (to, dv_) in enumerate(a_peers)
        ]

    def w_middle(w, copies):
        for cp in copies:
            cp.wait()
        total = part[w, block(al, PA), :]
        for i in range(A - 1):
            total = total + precv[w, i].astype(F32)
        zpart[w] = total
        return [
            send(zpart.at[w, block(to, PB)], zrecv.at[w, i], w_sems, (w, 1, i), dv_)
            for i, (to, dv_) in enumerate(b_peers)
        ]

    def w_spread(w, copies):
        for cp in copies:
            cp.wait()
        total = zpart[w, block(bl, PB), :]
        for i in range(B - 1):
            total = total + zrecv[w, i]
        here = pl.ds(pl.multiple_of(al * PA + bl * PB, PB), PB)
        if C > 1:
            hrecv[w, pl.ds(hi, 1)] = total[None]
            zpart[w, block(bl, PB), :] = total
            hc = [
                send(
                    zpart.at[w, block(bl, PB)], hrecv.at[w, hi], wh_sems, (w, d - 1), hi_peers[d - 1]
                )
                for d in range(1, C)
            ]
            for cp in hc:
                cp.wait()
            total = hrecv[w, 0]
            for i in range(1, C):
                total = total + hrecv[w, i]
        fin[w, here, :] = total.astype(BF)
        return [
            send(fin.at[w, here], fin.at[w, here], w_sems, (w, 2, i), dv_)
            for i, (_, dv_) in enumerate(b_peers)
        ]

    def w_gather(w, copies):
        for cp in copies:
            cp.wait()
        here = block(al, PA)
        return [
            send(fin.at[w, here], fin.at[w, here], w_sems, (w, 3, i), dv_)
            for i, (_, dv_) in enumerate(a_peers)
        ]

    def w_keep(w, copies):
        for cp in copies:
            cp.wait()
        store(fin.at[w], fin_hbm.at[w])

    weight_grads((GATE,))
    gate_copies = w_scatter(GATE)
    mix_copy.wait_recv()
    out_grads()
    out_copies = w_scatter(OUT)

    BU = 4

    def backward_block(i, _):
        chains = [(block(i * BU + u, NODES), i * BU + u, p) for u in range(BU) for p in range(PAIRS)]
        outs, dps = [], []
        for r, s, p in chains:
            ls = lanes[p]
            oh, ol = split(datt[r, ls])
            oh, ol = apart(oh), apart(ol)
            outs.append((oh, ol))
            high = vh[r, ls]
            dps.append(nt(lanes_cat(high, vl[r, ls], high), lanes_cat(oh, oh, ol)))
        dss = []
        for (r, s, p), dp in zip(chains, dps):
            pr = prob[s, p, 0].astype(F32) + prob[s, p, 1].astype(F32)
            dss.append(split(pr * (dp - jnp.sum(pr * dp, axis=0, keepdims=True))))
        for (r, s, p), (oh, ol) in zip(chains, outs):
            got = nn(prob[s, p, 0], lanes_cat(oh, ol))
            dv[r, lanes[p]] = got[:, 0:128] + got[:, 128:256] + nn(prob[s, p, 1], oh)
        for (r, s, p), (high, low) in zip(chains, dss):
            ls = lanes[p]
            qbh = apart(qh[r, ls])
            got = nn(high, lanes_cat(qbh, apart(ql[r, ls])))
            dk[r, ls] = (got[:, 0:128] + got[:, 128:256] + nn(low, qbh)) * (1.0 / LOG2E)
        for (r, s, p), (high, low) in zip(chains, dss):
            ls = lanes[p]
            khigh = kh[r, ls]
            got = tn(
                rows_cat(high, low),
                rows_cat(lanes_cat(khigh, kl[r, ls]), lanes_cat(khigh, jnp.zeros_like(khigh))),
            )
            got = joined(got[:, 0:128] + got[:, 128:256]) * 0.125
            low4[QUERY, r, ls] = (dq[r, ls] + got).astype(BF)
        return 0

    FIRST = NB // BU // 2
    lax.fori_loop(0, FIRST, backward_block, 0)
    ar1 = ar_reduce(1, ar1)
    lax.fori_loop(FIRST, NB // BU, backward_block, 0)
    gate_copies = w_middle(GATE, gate_copies)
    out_copies = w_middle(OUT, out_copies)
    weight_grads((QUERY,))
    query_copies = w_scatter(QUERY)

    mats, totals = ar_result(1, ar1)
    dsum = [m.astype(BF) for m in mats]

    KU = 4

    def key_block(i, _):
        r = block(i, KU * NODES)
        for p in range(PAIRS):
            ls = lanes[p]
            sig = k_sig[r, ls]
            kp = live_rows(i * KU, sig, KU)
            dkp = nt(vh[r, ls], dsum[p]) + totals[p]
            low4[KEY, r, ls] = (dk[r, ls] + dkp * kp * (1.0 - sig)).astype(BF)
            low4[VALUE, r, ls] = (dv[r, ls] + nn(kp.astype(BF), dsum[p])).astype(BF)
        return 0

    lax.fori_loop(0, NB // KU, key_block, 0)
    weight_grads((KEY, VALUE))
    key_copies = w_scatter(KEY)
    value_copies = w_scatter(VALUE)
    gate_copies = w_spread(GATE, gate_copies)
    out_copies = w_spread(OUT, out_copies)

    def normed_block(b, _):
        r = block(b, RB)
        grads = lanes_cat(*[low4[kind, r, :] for kind in (QUERY, KEY, VALUE, GATE)])
        dn = nt(grads, wall[...])
        dn_own[r, :] = dn[:, 0:W]
        dn_send[r, :] = dn[:, W : 2 * W]
        mean = mean_keep[r, 0:1]
        rstd = rstd_keep[r, 0:1]
        sa = dn[:, 0:W] * gain_own
        sb = dn[:, W : 2 * W] * gain_oth
        ha = (x[r, :].astype(F32) - mean) * rstd
        hb = (xo[r, :].astype(F32) - mean) * rstd
        s1 = jnp.sum(sa, axis=1, keepdims=True) + jnp.sum(sb, axis=1, keepdims=True)
        s2 = jnp.sum(sa * ha, axis=1, keepdims=True) + jnp.sum(sb * hb, axis=1, keepdims=True)
        st_send[r, :] = jnp.where(lane_half, s1, s2)
        return 0

    DC = 4
    dn_copies = []
    for i in range(DC):
        lax.fori_loop(i * (NR // DC), (i + 1) * (NR // DC), normed_block, 0)
        piece = pl.ds(i * (R // DC), R // DC)
        dn_copies.append(
            (
                send(dn_send.at[piece], dn_recv.at[piece], dn_sems, (0, i), partner),
                send(st_send.at[piece], st_recv.at[piece], dn_sems, (1, i), partner),
            )
        )
        if i == 1:
            query_copies = w_middle(QUERY, query_copies)
    key_copies = w_middle(KEY, key_copies)
    value_copies = w_middle(VALUE, value_copies)
    query_copies = w_spread(QUERY, query_copies)
    gate_copies = w_gather(GATE, gate_copies)
    out_copies = w_gather(OUT, out_copies)

    def out_block(b, _):
        r = block(b, RB)
        got = nn(mix[r, :], wo[own_rows, :]) + nn(mixo[r, :], wo[oth_rows, :])
        mixo[r, :] = (x[r, :].astype(F32) + got).astype(BF)
        return 0

    lax.fori_loop(0, NR, out_block, 0)
    store(mixo, layer_out)
    key_copies = w_spread(KEY, key_copies)
    value_copies = w_spread(VALUE, value_copies)
    query_copies = w_gather(QUERY, query_copies)

    def input_block(b, carry):
        gain_sum, bias_sum = carry
        r = block(b, RB)
        dn = dn_own[r, :] + dn_recv[r, :]
        st = st_send[r, :] + st_recv[r, :]
        mean = mean_keep[r, 0:1]
        rstd = rstd_keep[r, 0:1]
        s1 = st[:, 0:1] * (1.0 / (2 * W))
        s2 = st[:, 64:65] * (1.0 / (2 * W))
        ha = (x[r, :].astype(F32) - mean) * rstd
        inner = rstd * (dn * gain_own - s1 - ha * s2)
        co[r, :] = (c[r, :].astype(F32) + inner).astype(BF)
        return (
            gain_sum + jnp.sum(dn * ha, axis=0, keepdims=True),
            bias_sum + jnp.sum(dn, axis=0, keepdims=True),
        )

    carry = (jnp.zeros((1, W), F32), jnp.zeros((1, W), F32))
    for i in range(DC):
        for cp in dn_copies[i]:
            cp.wait_recv()
        carry = lax.fori_loop(i * (NR // DC), (i + 1) * (NR // DC), input_block, carry)
        piece = pl.ds(i * (R // DC), R // DC)
        store(co.at[piece], input_grad.at[piece])

    row = lax.broadcasted_iota(jnp.int32, (8, W), 0)
    terms = jnp.where(row == 0, carry[0], jnp.where(row == 1, carry[1], 0.0))
    gb_part[...] = terms
    gb_recv[pl.ds(lo, 1)] = terms[None]
    gb_copies = [
        send(gb_part, gb_recv.at[lo], gb_sems, (d - 1,), lo_peers[d - 1]) for d in range(1, L)
    ]
    key_copies = w_gather(KEY, key_copies)
    value_copies = w_gather(VALUE, value_copies)
    for cp in gb_copies:
        cp.wait()
    total = gb_recv[0]
    for i in range(1, L):
        total = total + gb_recv[i]
    if C > 1:
        gb_part[...] = total
        gb_hi[pl.ds(hi, 1)] = total[None]
        hc = [send(gb_part, gb_hi.at[hi], gbh_sems, (d - 1,), hi_peers[d - 1]) for d in range(1, C)]
        for cp in hc:
            cp.wait()
        total = gb_hi[0]
        for i in range(1, C):
            total = total + gb_hi[i]
    gain_grad[...] = total[0:1].reshape(W)
    bias_grad[...] = total[1:2].reshape(W)
    w_keep(GATE, gate_copies)
    w_keep(OUT, out_copies)
    w_keep(QUERY, query_copies)
    w_keep(KEY, key_copies)
    w_keep(VALUE, value_copies)
    for cp in stores:
        cp.wait()
    for cp in core_copies:
        cp.wait_send()
    mix_copy.wait_send()
    for pair in dn_copies:
        for cp in pair:
            cp.wait_send()


def shards(
    groups,
    node_input,
    cotangent,
    norm_gain,
    norm_bias,
    query_weight,
    key_weight,
    value_weight,
    gate_weight,
    out_weight,
    adjacent_vertices,
    active_vertex_tally,
    training_period,
):
    A, B, C = groups
    L = A * B
    R, W = node_input.shape
    D = 2 * W
    NB = R // NODES
    PAIRS = W // 128
    PER = CHUNKS // L
    PA = D // A
    PB = PA // B
    VM = pltpu.VMEM
    dma = pltpu.SemaphoreType.DMA
    vmem = pl.BlockSpec(memory_space=pltpu.VMEM)
    smem = pl.BlockSpec(memory_space=pltpu.SMEM)
    hbm = pl.BlockSpec(memory_space=pl.ANY)
    layer_output, input_grad, gain_grad, bias_grad, fin = pl.pallas_call(
        functools.partial(layer_kernel, groups),
        name="layer_kernel",
        out_shape=(
            jax.ShapeDtypeStruct((R, W), BF),
            jax.ShapeDtypeStruct((R, W), BF),
            jax.ShapeDtypeStruct((W,), F32),
            jax.ShapeDtypeStruct((W,), F32),
            jax.ShapeDtypeStruct((5, D, W), BF),
        ),
        in_specs=[hbm] * 2 + [vmem] * 2 + [hbm] * 6 + [smem] * 2,
        out_specs=(hbm, hbm, vmem, vmem, hbm),
        scratch_shapes=[
            VM((R, W), BF),
            VM((R, W), BF),
            VM((R, W), BF),
            VM((R, W), BF),
            VM((D, W), BF),
            VM((adjacent_vertices.shape[1], R), jnp.int32),
            VM((5, D, W), BF),
            VM((16, W), F32),
            VM((16, W), F32),
            VM((W, W), BF),
            VM((D, 4 * W), BF),
            VM((R, D), BF),
            VM((R, 128), F32),
            VM((R, 128), F32),
            VM((R, W), F32),
            VM((R, W), F32),
            VM((R, W), BF),
            VM((R, W), BF),
            VM((R, W), BF),
            VM((R, W), BF),
            VM((R, W), BF),
            VM((R, W), BF),
            VM((R, W), F32),
            VM((R, W), F32),
            VM((R, W), F32),
            VM((R, W), F32),
            VM((NB, PAIRS, 2, NODES, 2 * NODES), BF),
            VM((R, W), F32),
            VM((4, R, W), BF),
            VM((R, W), BF),
            VM((R, W), BF),
            VM((R, W), F32),
            VM((R, 128), F32),
            VM((R, 128), F32),
            VM((2, CHUNKS, 16, 128), F32),
            VM((2, L, PER, 16, 128), F32),
            VM((2, PER, 16, 128), F32),
            VM((2, C, PER, 16, 128), F32),
            VM((2, CHUNKS, 8, 128), F32),
            VM((5, D, W), F32),
            VM((5, D, W), BF),
            VM((5, A - 1, PA, W), BF),
            VM((5, PA, W), F32),
            VM((5, B - 1, PB, W), F32),
            VM((5, C, PB, W), F32),
            VM((8, W), F32),
            VM((L, 8, W), F32),
            VM((C, 8, W), F32),
            dma((15,)),
            dma((10,)),
            dma((2, 8)),
            dma((2, 1)),
            dma((2, 2, 4)),
            dma((2, 2, 2, L - 1)),
            dma((2, 2, max(C - 1, 1))),
            dma((2, 5, 4, max(A, B) - 1)),
            dma((2, 5, max(C - 1, 1))),
            dma((2, L - 1)),
            dma((2, max(C - 1, 1))),
        ],
        compiler_params=pltpu.CompilerParams(
            collective_id=0, has_side_effects=True, vmem_limit_bytes=63 << 20
        ),
    )(
        node_input,
        cotangent,
        norm_gain,
        norm_bias,
        query_weight,
        key_weight,
        value_weight,
        gate_weight,
        out_weight,
        adjacent_vertices.T,
        active_vertex_tally,
        training_period,
    )
    return pl.pallas_call(
        finish_kernel,
        name="finish_kernel",
        out_shape=(
            jax.ShapeDtypeStruct((R, W), BF),
            jax.ShapeDtypeStruct((R, W), BF),
            jax.ShapeDtypeStruct((W,), F32),
            jax.ShapeDtypeStruct((W,), F32),
        )
        + tuple(jax.ShapeDtypeStruct((D, W), F32) for _ in range(5)),
        in_specs=[hbm, hbm, vmem, vmem, hbm],
        out_specs=(hbm, hbm, vmem, vmem) + (hbm,) * 5,
        scratch_shapes=[VM((5, D, W), BF), VM((5, D, W), F32), VM((2, R, W), BF), dma((14,))],
    )(layer_output, input_grad, gain_grad, bias_grad, fin)


def finish_kernel(
    lo_in, ig_in, gain_in, bias_in, fin, lo, ig, gain, bias, gq, gk, gv, gg, go, low, full, wide, sems
):
    loads = []

    def begin(src, dst, into):
        copy = pltpu.make_async_copy(src, dst, sems.at[len(into) + (0 if into is loads else 7)])
        copy.start()
        into.append(copy)

    for i in range(5):
        begin(fin.at[i], low.at[i], loads)
    begin(lo_in, wide.at[0], loads)
    begin(ig_in, wide.at[1], loads)
    gain[...] = gain_in[...]
    bias[...] = bias_in[...]
    stores = []
    for i, out in enumerate((gq, gk, gv, gg, go)):
        loads[i].wait()
        full[i] = low[i].astype(F32)
        begin(full.at[i], out, stores)
    for i, out in enumerate((lo, ig)):
        loads[5 + i].wait()
        begin(wide.at[i], out, stores)
    for cp in stores:
        cp.wait()


def factors(count):
    a = 4 if count % 4 == 0 else count
    b = 4 if count % (a * 4) == 0 else count // a
    return a, b, count // (a * b)


def solution(mesh):
    rows = P("graph", "head")
    cols = P(None, "head")
    return jax.shard_map(
        functools.partial(shards, factors(mesh.shape["graph"])),
        mesh=mesh,
        in_specs=(rows, rows, P("head"), P("head"))
        + (cols,) * 5
        + (P("graph", None), P("graph"), P("graph")),
        out_specs=(rows, rows, P("head"), P("head")) + (cols,) * 5,
        check_vma=False,
    )
```

```python
import functools

import jax
import jax.numpy as jnp
from jax import lax
from jax.experimental import pallas as pl
from jax.experimental.pallas import tpu as pltpu
from jax.sharding import PartitionSpec as P

EPS = 1e-05
BETA = 0.9
LOG2E = 1.4426950408889634
BF = jnp.bfloat16
F32 = jnp.float32
MESH = pl.DeviceIdType.MESH
NODES = 128
QUERY, KEY, VALUE, GATE, OUT = 0, 1, 2, 3, 4


def nn(a, b):
    return lax.dot_general(a, b, (((1,), (0,)), ((), ())), preferred_element_type=F32)


def nt(a, b):
    return lax.dot_general(a, b, (((1,), (1,)), ((), ())), preferred_element_type=F32)


def tn(a, b):
    return lax.dot_general(a, b, (((0,), (0,)), ((), ())), preferred_element_type=F32)


def split(a):
    high = a.astype(BF)
    return high, (a - high.astype(F32)).astype(BF)


def rows_cat(*parts):
    return jnp.concatenate(parts, axis=0)


def lanes_cat(*parts):
    return jnp.concatenate(parts, axis=1)


def block(start, size):
    return pl.ds(pl.multiple_of(start * size, size), size)


def layer_kernel(
    groups,
    x_hbm,
    c_hbm,
    gain,
    bias,
    wq,
    wk,
    wv,
    wg,
    wo_hbm,
    adjacent_hbm,
    tally,
    period,
    layer_out,
    input_grad,
    gain_grad,
    bias_grad,
    fin_hbm,
    x,
    xo,
    c,
    co,
    wo,
    adjacent,
    fin,
    gbs,
    gbo,
    woo,
    wall,
    normed,
    mean_keep,
    rstd_keep,
    q_sig,
    k_sig,
    qh,
    ql,
    kh,
    kl,
    vh,
    vl,
    g,
    dmix,
    datt,
    att,
    prob,
    dq,
    low4,
    mix,
    mixo,
    dn_recv,
    st_send,
    st_recv,
    sum_part,
    sum_recv,
    sum_mid,
    sum_z,
    sum_hi,
    sum_full,
    part,
    psend,
    precv,
    zpart,
    zrecv,
    hrecv,
    gb_part,
    gb_recv,
    gb_z,
    gb_hi,
    load_sems,
    store_sems,
    core_sems,
    mix_sems,
    dn_sems,
    ar_sems,
    arh_sems,
    w_sems,
    wh_sems,
    gb_sems,
):
    A, B, C = groups
    L = A * B
    R, W = x.shape
    NB = R // NODES
    PAIRS = W // 128
    me = lax.axis_index("graph")
    head = lax.axis_index("head")
    other = 1 - head
    lo = lax.rem(me, L)
    hi = me // L
    al = lax.rem(lo, A)
    bl = lo // A

    def dev(h_, b_, a_):
        return (h_ * L + b_ * A + a_, head)

    a_peers = [(lax.rem(al + d, A), dev(hi, bl, lax.rem(al + d, A))) for d in range(1, A)]
    b_peers = [(lax.rem(bl + d, B), dev(hi, lax.rem(bl + d, B), al)) for d in range(1, B)]
    h_peers = [(lax.rem(hi + d, C), dev(lax.rem(hi + d, C), bl, al)) for d in range(1, C)]
    partner = (me, other)
    own_rows = block(head, W)
    oth_rows = block(other, W)

    def send(src, dst, send_sem, recv_sem, to):
        pltpu.make_async_remote_copy(
            src_ref=src,
            dst_ref=dst,
            send_sem=send_sem,
            recv_sem=recv_sem,
            device_id=to,
            device_id_type=MESH,
        ).start()

    def bytes_of(ref, sem):
        pltpu.make_async_copy(ref, ref, sem).wait()

    def wait_both(ref, sems, index):
        bytes_of(ref, sems.at[(0,) + index])
        bytes_of(ref, sems.at[(1,) + index])

    dk, dv, dn_own, dn_send = att, q_sig, g, dmix

    barrier = pltpu.get_barrier_semaphore()
    greeted = [partner] + [to for _, to in a_peers + b_peers + h_peers]
    for to in greeted:
        pl.semaphore_signal(barrier, inc=1, device_id=to, device_id_type=MESH)

    loads = []

    def load(src, dst):
        copy = pltpu.make_async_copy(src, dst, load_sems.at[len(loads)])
        copy.start()
        loads.append(copy)
        return copy

    XC = 4
    x_loads = []
    for i in range(XC):
        piece = pl.ds(i * (R // XC), R // XC)
        x_loads.append(load(x_hbm.at[piece], x.at[piece]))
    wo_load = load(wo_hbm, wo)
    c_load = load(c_hbm, c)
    w_loads = []
    for i, w in ((1, wk), (2, wv), (0, wq), (3, wg)):
        cols = pl.ds(i * W, W)
        w_loads.append(load(w.at[own_rows], wall.at[pl.ds(0, W), cols]))
        w_loads.append(load(w.at[oth_rows], wall.at[pl.ds(W, W), cols]))
    adjacent_load = load(adjacent_hbm, adjacent)

    stores = []

    def store(src, dst):
        copy = pltpu.make_async_copy(src, dst, store_sems.at[len(stores)])
        copy.start()
        stores.append(copy)

    gbs[0:8, :] = jnp.broadcast_to(gain[...].astype(F32).reshape(1, W), (8, W))
    gbs[8:16, :] = jnp.broadcast_to(bias[...].astype(F32).reshape(1, W), (8, W))
    pl.semaphore_wait(barrier, len(greeted))

    send(gbs, gbo, core_sems.at[0, 0], core_sems.at[1, 0], partner)
    pieces = [pl.ds(i * (R // XC), R // XC) for i in range(XC)]
    for i, piece in enumerate(pieces):
        x_loads[i].wait()
        send(x.at[piece], xo.at[piece], core_sems.at[0, 3], core_sems.at[1, 3 + i], partner)
    wo_load.wait()
    send(wo.at[oth_rows], woo, core_sems.at[0, 1], core_sems.at[1, 1], partner)
    c_load.wait()
    send(c, co, core_sems.at[0, 2], core_sems.at[1, 2], partner)

    RB = 256
    NR = R // RB

    def own_dmix(b, _):
        r = block(b, RB)
        dmix[r, :] = nt(c[r, :], wo[own_rows, :])
        return 0

    lax.fori_loop(0, NR, own_dmix, 0)

    sum_part[...] = jnp.zeros_like(sum_part)
    bytes_of(gbo, core_sems.at[1, 0])
    gain_own, bias_own = gbs[0:1, :], gbs[8:9, :]
    gain_oth, bias_oth = gbo[0:1, :], gbo[8:9, :]
    lane_half = lax.broadcasted_iota(jnp.int32, (1, 128), 1) < 64
    node_of = lax.broadcasted_iota(jnp.int32, (NODES, 128), 0)

    def live_rows(first, a, count):
        node = lax.broadcasted_iota(jnp.int32, (NODES, a.shape[1]), 0)
        return rows_cat(
            *[
                jnp.where(node < tally[first + i], a[i * NODES : (i + 1) * NODES], 0.0)
                for i in range(count)
            ]
        )

    def norm_block(b, carry):
        @pl.when(lax.rem(b, NR // XC) == 0)
        def _():
            i = b // (NR // XC)
            bytes_of(xo.at[block(i, R // XC)], core_sems.at[1, 3 + i])

        r = block(b, RB)
        xa = x[r, :].astype(F32)
        xb = xo[r, :].astype(F32)
        mean = (
            jnp.sum(xa, axis=1, keepdims=True) + jnp.sum(xb, axis=1, keepdims=True)
        ) * (1.0 / (2 * W))
        xa = xa - mean
        xb = xb - mean
        var = (
            jnp.sum(xa * xa, axis=1, keepdims=True) + jnp.sum(xb * xb, axis=1, keepdims=True)
        ) * (1.0 / (2 * W))
        rstd = lax.rsqrt(var + EPS)
        mean_keep[r, :] = jnp.broadcast_to(mean, (RB, 128))
        rstd_keep[r, :] = jnp.broadcast_to(rstd, (RB, 128))
        na = (xa * rstd * gain_own + bias_own).astype(BF)
        nb = (xb * rstd * gain_oth + bias_oth).astype(BF)
        normed[r, 0:W] = na
        normed[r, W : 2 * W] = nb
        kv = nn(lanes_cat(na, nb), wall[:, W : 3 * W])
        kk = kv[:, 0:W]
        vv = kv[:, W : 2 * W]
        kh[r, :], kl[r, :] = split(kk)
        vbf, vlow = split(vv)
        vh[r, :] = vbf
        vl[r, :] = vlow
        sig = jax.nn.sigmoid(kk)
        k_sig[r, :] = sig
        kp = live_rows(b * (RB // NODES), sig, RB // NODES)
        kpb = kp.astype(BF)
        sums, totals = carry
        new_sums, new_totals = [], []
        for p in range(PAIRS):
            ls = slice(p * 128, (p + 1) * 128)
            new_sums.append(sums[p] + tn(kpb[:, ls], vbf[:, ls]))
            new_totals.append(totals[p] + jnp.sum(kp[:, ls], axis=0, keepdims=True))
        return tuple(new_sums), tuple(new_totals)

    def zero_sums():
        return (
            tuple(jnp.zeros((128, 128), F32) for _ in range(PAIRS)),
            tuple(jnp.zeros((1, 128), F32) for _ in range(PAIRS)),
        )

    for cp in w_loads[0:4]:
        cp.wait()
    carry = lax.fori_loop(0, NR, norm_block, zero_sums())

    def pack_sums(slot, carry):
        sums, totals = carry
        packed = rows_cat(
            *[jnp.where(lane_half, sums[p][0:64], sums[p][64:128]) for p in range(PAIRS)]
        )
        for j in range(A):
            sum_part[slot, j, 0:SR, :] = packed[j * SR : (j + 1) * SR]
            for p in range(PAIRS):
                sum_part[slot, j, SR + p : SR + p + 1, :] = totals[p]

    SR = 64 * PAIRS // A

    def ar_scatter(slot):
        for i, (j, to) in enumerate(a_peers):
            send(
                sum_part.at[slot, j],
                sum_recv.at[slot, i],
                ar_sems.at[0, slot, 0],
                ar_sems.at[1, slot, 0],
                to,
            )

    def ar_middle(slot):
        wait_both(sum_recv.at[slot], ar_sems, (slot, 0))
        total = sum_part[slot, al]
        for i in range(A - 1):
            total = total + sum_recv[slot, i]
        sum_mid[slot] = total
        for i, (_, to) in enumerate(b_peers):
            send(
                sum_mid.at[slot],
                sum_z.at[slot, i],
                ar_sems.at[0, slot, 1],
                ar_sems.at[1, slot, 1],
                to,
            )

    def ar_gather(slot):
        wait_both(sum_z.at[slot], ar_sems, (slot, 1))
        total = sum_mid[slot]
        for i in range(B - 1):
            total = total + sum_z[slot, i]
        if C > 1:
            sum_mid[slot] = total
            for i, (_, to) in enumerate(h_peers):
                send(
                    sum_mid.at[slot],
                    sum_hi.at[slot, i],
                    arh_sems.at[0, slot],
                    arh_sems.at[1, slot],
                    to,
                )
            wait_both(sum_hi.at[slot], arh_sems, (slot,))
            for i in range(C - 1):
                total = total + sum_hi[slot, i]
        sum_full[slot, al] = total
        for i, (_, to) in enumerate(a_peers):
            send(
                sum_full.at[slot, al],
                sum_full.at[slot, al],
                ar_sems.at[0, slot, 2],
                ar_sems.at[1, slot, 2],
                to,
            )

    def ar_result(slot):
        wait_both(sum_recv.at[slot], ar_sems, (slot, 2))
        mats, totals = [], []
        packed = rows_cat(*[sum_full[slot, j, 0:SR, :] for j in range(A)])
        for p in range(PAIRS):
            own = packed[p * 64 : (p + 1) * 64]
            mats.append(rows_cat(jnp.where(lane_half, own, 0.0), jnp.where(lane_half, 0.0, own)))
            totals.append(sum_full[slot, 0, SR + p : SR + p + 1, :])
        return mats, totals

    pack_sums(0, carry)
    ar_scatter(0)

    for cp in w_loads[4:]:
        cp.wait()
    bytes_of(woo, core_sems.at[1, 1])
    bytes_of(co, core_sems.at[1, 2])

    def gate_block(b, _):
        r = block(b, RB)
        n = normed[r, :]
        qq = nn(n, wall[:, 0:W])
        q_sig[r, :] = jax.nn.sigmoid(qq)
        qh[r, :], ql[r, :] = split(qq * (0.125 * LOG2E))
        gg = nn(n, wall[:, 3 * W : 4 * W])
        g[r, :] = gg
        dm = dmix[r, :] + nt(co[r, :], woo[...])
        dmix[r, :] = dm
        datt[r, :] = dm * ((1.0 - BETA) * gg + BETA)
        return 0

    lax.fori_loop(0, NR, gate_block, 0)
    ar_middle(0)

    half_row = jnp.where(lane_half, 1.0, 0.0)
    half_a = jnp.broadcast_to(half_row, (NODES, 128)).astype(BF)
    half_b = jnp.broadcast_to(1.0 - half_row, (NODES, 128)).astype(BF)

    def apart(a):
        return rows_cat(a * half_a, a * half_b)

    def joined(a):
        return jnp.where(lane_half, a[0:NODES], a[NODES : 2 * NODES])

    FU = 4
    lanes = [slice(p * 128, (p + 1) * 128) for p in range(PAIRS)]

    def forward_block(i, _):
        @pl.when(i == NB // FU // 2)
        def _():
            ar_gather(0)

        chains = [(i * FU + u, p) for u in range(FU) for p in range(PAIRS)]
        weights = []
        for u in range(FU):
            listed = adjacent[:, block(i * FU + u, NODES)]
            count = jnp.zeros((NODES, NODES), F32)
            for j in range(listed.shape[0]):
                count = count + jnp.where(listed[j : j + 1, :] == node_of, 1.0, 0.0)
            weight = jnp.where(count > 0.0, jnp.log(jnp.maximum(count, 1.0)) * LOG2E, -1e30)
            weights.append(lanes_cat(weight, weight))
        scores = []
        for s, p in chains:
            r, ls = block(s, NODES), lanes[p]
            high, low = kh[r, ls], kl[r, ls]
            qbh = apart(qh[r, ls])
            scores.append(
                nt(lanes_cat(high, low, high), lanes_cat(qbh, qbh, apart(ql[r, ls])))
            )
        probs = []
        for j, score in enumerate(scores):
            score = score + weights[j // PAIRS]
            e = jnp.exp2(score - jnp.max(score, axis=0, keepdims=True))
            probs.append(split(e * (1.0 / jnp.sum(e, axis=0, keepdims=True))))
        for (s, p), (high, low) in zip(chains, probs):
            prob[s, p, 0] = high
            prob[s, p, 1] = low
        for (s, p), (high, low) in zip(chains, probs):
            r, ls = block(s, NODES), lanes[p]
            vhigh = vh[r, ls]
            o = tn(
                rows_cat(high, low),
                rows_cat(lanes_cat(vhigh, vl[r, ls]), lanes_cat(vhigh, jnp.zeros_like(vhigh))),
            )
            att[r, ls] = joined(o[:, 0:128] + o[:, 128:256])
        return 0

    adjacent_load.wait()
    lax.fori_loop(0, NB // FU, forward_block, 0)

    mats, totals = ar_result(0)
    square = (2, 128, 128)
    same_head = (lax.broadcasted_iota(jnp.int32, (128, 128), 0) < 64) == (
        lax.broadcasted_iota(jnp.int32, (128, 128), 1) < 64
    )
    ones_bd = jnp.where(same_head, 1.0, 0.0).astype(BF)
    num_w, den_w, back_w = [], [], []
    for p in range(PAIRS):
        sh, sl = split(mats[p])
        th, tl = split(jnp.where(same_head, jnp.broadcast_to(totals[p], (128, 128)), 0.0))
        num_w.append(lanes_cat(sh, sl))
        den_w.append(rows_cat(th, tl))
        back_w.append(lanes_cat(sh, sh, sl))

    GU = 4

    def glob_block(i, carry):
        r = block(i, GU * NODES)
        keep = [(1 - period[i * GU + u]).astype(F32) for u in range(GU)]
        sums, tots = carry
        new_sums, new_tots = [], []
        for p in range(PAIRS):
            ls = lanes[p]
            qp = q_sig[r, ls]
            qpb = qp.astype(BF)
            num = nn(qpb, num_w[p])
            den = nt(qpb, den_w[p])
            inv = 1.0 / (den[:, 0:128] + den[:, 128:256])
            glob = (num[:, 0:128] + num[:, 128:256]) * inv
            at = att[r, ls] + glob
            mix[r, ls] = ((1.0 - BETA) * g[r, ls] * at + BETA * at).astype(BF)
            low4[GATE, r, ls] = (dmix[r, ls] * (1.0 - BETA) * at).astype(BF)
            da = datt[r, ls]
            dnum = rows_cat(*[keep[u] * da[u * NODES : (u + 1) * NODES] for u in range(GU)]) * inv
            dh, dl = split(dnum)
            th, tl = split(dnum * glob)
            dden = -nn(lanes_cat(th, tl), rows_cat(ones_bd, ones_bd))
            dqp = nt(lanes_cat(dh, dl, dh), back_w[p]) + dden * totals[p]
            dq[r, ls] = dqp * qp * (1.0 - qp)
            new_sums.append(sums[p] + tn(qpb, dh))
            new_tots.append(tots[p] + jnp.sum(dden * qp, axis=0, keepdims=True))
        return tuple(new_sums), tuple(new_tots)

    carry = lax.fori_loop(0, NB // GU, glob_block, zero_sums())
    pack_sums(1, carry)
    ar_scatter(1)
    send(mix, mixo, mix_sems.at[0], mix_sems.at[1], partner)

    KB = 512

    def weight_grads(kinds):
        def step(i, _):
            r = block(i, KB)
            n = normed[r, :]
            for kind in kinds:
                got = tn(n, low4[kind, r, :])
                part[kind, own_rows, :] += got[0:W]
                part[kind, oth_rows, :] += got[W : 2 * W]
            return 0

        for kind in kinds:
            part[kind] = jnp.zeros(part.shape[1:], F32)
        lax.fori_loop(0, R // KB, step, 0)

    def out_grads():
        def step(i, _):
            r = block(i, KB)
            cc = c[r, :]
            part[OUT, own_rows, :] += tn(mix[r, :], cc)
            part[OUT, oth_rows, :] += tn(mixo[r, :], cc)
            return 0

        part[OUT] = jnp.zeros(part.shape[1:], F32)
        lax.fori_loop(0, R // KB, step, 0)

    D = 2 * W
    PA = D // A
    PB = PA // B

    QUERIES, KEYVALUE, GATEOUT = 0, 1, 2
    span = {QUERIES: pl.ds(0, 1), KEYVALUE: pl.ds(1, 2), GATEOUT: pl.ds(3, 2)}
    kinds_of = {QUERIES: (QUERY,), KEYVALUE: (KEY, VALUE), GATEOUT: (GATE, OUT)}

    def w_scatter(w):
        for kind in kinds_of[w]:
            psend[kind] = part[kind].astype(BF)
        for i, (j, to) in enumerate(a_peers):
            send(
                psend.at[span[w], block(j, PA)],
                precv.at[i, span[w]],
                w_sems.at[0, w, 0],
                w_sems.at[1, w, 0],
                to,
            )

    def w_middle(w):
        wait_both(precv.at[:, span[w]], w_sems, (w, 0))
        for kind in kinds_of[w]:
            total = part[kind, block(al, PA), :]
            for i in range(A - 1):
                total = total + precv[i, kind].astype(F32)
            zpart[kind] = total
        for i, (j, to) in enumerate(b_peers):
            send(
                zpart.at[span[w], block(j, PB)],
                zrecv.at[i, span[w]],
                w_sems.at[0, w, 1],
                w_sems.at[1, w, 1],
                to,
            )

    here = pl.ds(pl.multiple_of(al * PA + bl * PB, PB), PB)

    def w_spread(w):
        wait_both(zrecv.at[:, span[w]], w_sems, (w, 1))
        totals = {}
        for kind in kinds_of[w]:
            total = zpart[kind, block(bl, PB), :]
            for i in range(B - 1):
                total = total + zrecv[i, kind]
            totals[kind] = total
        if C > 1:
            for kind in kinds_of[w]:
                zpart[kind, block(bl, PB), :] = totals[kind]
            for i, (_, to) in enumerate(h_peers):
                send(
                    zpart.at[span[w], block(bl, PB)],
                    hrecv.at[i, span[w]],
                    wh_sems.at[0, w],
                    wh_sems.at[1, w],
                    to,
                )
            wait_both(hrecv.at[:, span[w]], wh_sems, (w,))
            for kind in kinds_of[w]:
                for i in range(C - 1):
                    totals[kind] = totals[kind] + hrecv[i, kind]
        for kind in kinds_of[w]:
            fin[kind, here, :] = totals[kind].astype(BF)
        for i, (_, to) in enumerate(b_peers):
            send(
                fin.at[span[w], here],
                fin.at[span[w], here],
                w_sems.at[0, w, 2],
                w_sems.at[1, w, 2],
                to,
            )

    def w_gather(w):
        wait_both(fin.at[span[w], pl.ds(0, (B - 1) * PB)], w_sems, (w, 2))
        for i, (_, to) in enumerate(a_peers):
            send(
                fin.at[span[w], block(al, PA)],
                fin.at[span[w], block(al, PA)],
                w_sems.at[0, w, 3],
                w_sems.at[1, w, 3],
                to,
            )

    def w_keep(w):
        wait_both(fin.at[span[w], pl.ds(0, (A - 1) * PA)], w_sems, (w, 3))
        store(fin.at[span[w]], fin_hbm.at[span[w]])

    weight_grads((GATE,))
    bytes_of(mixo, mix_sems.at[1])
    out_grads()
    w_scatter(GATEOUT)

    BU = 4

    def backward_block(i, _):
        @pl.when(i == 1)
        def _():
            ar_middle(1)

        @pl.when(i == 3)
        def _():
            ar_gather(1)

        chains = [(block(i * BU + u, NODES), i * BU + u, p) for u in range(BU) for p in range(PAIRS)]
        outs, dps = [], []
        for r, s, p in chains:
            ls = lanes[p]
            oh, ol = split(datt[r, ls])
            oh, ol = apart(oh), apart(ol)
            outs.append((oh, ol))
            high = vh[r, ls]
            dps.append(nt(lanes_cat(high, vl[r, ls], high), lanes_cat(oh, oh, ol)))
        dss = []
        for (r, s, p), dp in zip(chains, dps):
            pr = prob[s, p, 0].astype(F32) + prob[s, p, 1].astype(F32)
            dss.append(split(pr * (dp - jnp.sum(pr * dp, axis=0, keepdims=True))))
        for (r, s, p), (oh, ol) in zip(chains, outs):
            got = nn(prob[s, p, 0], lanes_cat(oh, ol))
            dv[r, lanes[p]] = got[:, 0:128] + got[:, 128:256] + nn(prob[s, p, 1], oh)
        for (r, s, p), (high, low) in zip(chains, dss):
            ls = lanes[p]
            qbh = apart(qh[r, ls])
            got = nn(high, lanes_cat(qbh, apart(ql[r, ls])))
            dk[r, ls] = (got[:, 0:128] + got[:, 128:256] + nn(low, qbh)) * (1.0 / LOG2E)
        for (r, s, p), (high, low) in zip(chains, dss):
            ls = lanes[p]
            khigh = kh[r, ls]
            got = tn(
                rows_cat(high, low),
                rows_cat(lanes_cat(khigh, kl[r, ls]), lanes_cat(khigh, jnp.zeros_like(khigh))),
            )
            got = joined(got[:, 0:128] + got[:, 128:256]) * 0.125
            low4[QUERY, r, ls] = (dq[r, ls] + got).astype(BF)
        return 0

    lax.fori_loop(0, NB // BU, backward_block, 0)
    w_middle(GATEOUT)
    weight_grads((QUERY,))
    w_scatter(QUERIES)

    mats, totals = ar_result(1)
    dsum = [m.astype(BF) for m in mats]

    KU = 4

    def key_block(i, _):
        r = block(i, KU * NODES)
        for p in range(PAIRS):
            ls = lanes[p]
            sig = k_sig[r, ls]
            kp = live_rows(i * KU, sig, KU)
            dkp = nt(vh[r, ls], dsum[p]) + totals[p]
            low4[KEY, r, ls] = (dk[r, ls] + dkp * kp * (1.0 - sig)).astype(BF)
            low4[VALUE, r, ls] = (dv[r, ls] + nn(kp.astype(BF), dsum[p])).astype(BF)
        return 0

    lax.fori_loop(0, NB // KU, key_block, 0)
    weight_grads((KEY, VALUE))
    w_scatter(KEYVALUE)
    w_spread(GATEOUT)

    DC = 4

    def normed_block(b, _):
        r = block(b, RB)
        grads = lanes_cat(*[low4[kind, r, :] for kind in (QUERY, KEY, VALUE, GATE)])
        dn = nt(grads, wall[...])
        dn_own[r, :] = dn[:, 0:W]
        dn_send[r, :] = dn[:, W : 2 * W]
        mean = mean_keep[r, 0:1]
        rstd = rstd_keep[r, 0:1]
        sa = dn[:, 0:W] * gain_own
        sb = dn[:, W : 2 * W] * gain_oth
        ha = (x[r, :].astype(F32) - mean) * rstd
        hb = (xo[r, :].astype(F32) - mean) * rstd
        s1 = jnp.sum(sa, axis=1, keepdims=True) + jnp.sum(sb, axis=1, keepdims=True)
        s2 = jnp.sum(sa * ha, axis=1, keepdims=True) + jnp.sum(sb * hb, axis=1, keepdims=True)
        st_send[r, :] = jnp.where(lane_half, s1, s2)

        @pl.when(lax.rem(b, NR // DC) == NR // DC - 1)
        def _():
            i = b // (NR // DC)
            piece = block(i, R // DC)
            send(dn_send.at[piece], dn_recv.at[piece], dn_sems.at[0, 0], dn_sems.at[0, 2 + i], partner)
            send(st_send.at[piece], st_recv.at[piece], dn_sems.at[0, 1], dn_sems.at[1, 2 + i], partner)

        @pl.when(b == NR // 2)
        def _():
            w_middle(QUERIES)

        return 0

    lax.fori_loop(0, NR, normed_block, 0)
    w_middle(KEYVALUE)
    w_spread(QUERIES)
    w_gather(GATEOUT)

    def out_block(b, _):
        r = block(b, RB)
        got = nn(mix[r, :], wo[own_rows, :]) + nn(mixo[r, :], wo[oth_rows, :])
        mixo[r, :] = (x[r, :].astype(F32) + got).astype(BF)
        return 0

    lax.fori_loop(0, NR, out_block, 0)
    store(mixo, layer_out)
    w_spread(KEYVALUE)
    w_gather(QUERIES)

    def input_block(b, carry):
        @pl.when(lax.rem(b, NR // DC) == 0)
        def _():
            i = b // (NR // DC)
            piece = block(i, R // DC)
            bytes_of(dn_recv.at[piece], dn_sems.at[0, 2 + i])
            bytes_of(st_recv.at[piece], dn_sems.at[1, 2 + i])

        gain_sum, bias_sum = carry
        r = block(b, RB)
        dn = dn_own[r, :] + dn_recv[r, :]
        st = st_send[r, :] + st_recv[r, :]
        mean = mean_keep[r, 0:1]
        rstd = rstd_keep[r, 0:1]
        s1 = st[:, 0:1] * (1.0 / (2 * W))
        s2 = st[:, 64:65] * (1.0 / (2 * W))
        ha = (x[r, :].astype(F32) - mean) * rstd
        inner = rstd * (dn * gain_own - s1 - ha * s2)
        co[r, :] = (c[r, :].astype(F32) + inner).astype(BF)
        return (
            gain_sum + jnp.sum(dn * ha, axis=0, keepdims=True),
            bias_sum + jnp.sum(dn, axis=0, keepdims=True),
        )

    carry = (jnp.zeros((1, W), F32), jnp.zeros((1, W), F32))
    carry = lax.fori_loop(0, NR, input_block, carry)
    store(co, input_grad)

    row = lax.broadcasted_iota(jnp.int32, (8, W), 0)
    total = jnp.where(row == 0, carry[0], jnp.where(row == 1, carry[1], 0.0))

    def in_order(total, step, held, index, count, peers):
        gb_part[step] = total
        held[pl.ds(index, 1)] = total[None]
        for _, to in peers:
            send(gb_part.at[step], held.at[index], gb_sems.at[0, step], gb_sems.at[1, step], to)
        return count

    def added(step, held, count):
        wait_both(held.at[pl.ds(0, count - 1)], gb_sems, (step,))
        total = held[0]
        for i in range(1, count):
            total = total + held[i]
        return total

    in_order(total, 0, gb_recv, al, A, a_peers)
    w_gather(KEYVALUE)
    in_order(added(0, gb_recv, A), 1, gb_z, bl, B, b_peers)
    w_keep(GATEOUT)
    w_keep(QUERIES)
    total = added(1, gb_z, B)
    if C > 1:
        in_order(total, 2, gb_hi, hi, C, h_peers)
        total = added(2, gb_hi, C)
    gain_grad[...] = total[0:1].reshape(W)
    bias_grad[...] = total[1:2].reshape(W)
    w_keep(KEYVALUE)
    for cp in stores:
        cp.wait()
    bytes_of(gbs, core_sems.at[0, 0])
    bytes_of(woo, core_sems.at[0, 1])
    bytes_of(c, core_sems.at[0, 2])
    bytes_of(x, core_sems.at[0, 3])
    bytes_of(mix, mix_sems.at[0])
    bytes_of(dn_send, dn_sems.at[0, 0])
    bytes_of(st_send, dn_sems.at[0, 1])


def shards(
    groups,
    node_input,
    cotangent,
    norm_gain,
    norm_bias,
    query_weight,
    key_weight,
    value_weight,
    gate_weight,
    out_weight,
    adjacent_vertices,
    active_vertex_tally,
    training_period,
):
    A, B, C = groups
    R, W = node_input.shape
    D = 2 * W
    NB = R // NODES
    PAIRS = W // 128
    SR = 64 * PAIRS // A + 8
    PA = D // A
    PB = PA // B
    VM = pltpu.VMEM
    dma = pltpu.SemaphoreType.DMA
    vmem = pl.BlockSpec(memory_space=pltpu.VMEM)
    smem = pl.BlockSpec(memory_space=pltpu.SMEM)
    hbm = pl.BlockSpec(memory_space=pl.ANY)
    layer_output, input_grad, gain_grad, bias_grad, fin = pl.pallas_call(
        functools.partial(layer_kernel, groups),
        name="layer_kernel",
        out_shape=(
            jax.ShapeDtypeStruct((R, W), BF),
            jax.ShapeDtypeStruct((R, W), BF),
            jax.ShapeDtypeStruct((W,), F32),
            jax.ShapeDtypeStruct((W,), F32),
            jax.ShapeDtypeStruct((5, D, W), BF),
        ),
        in_specs=[hbm] * 2 + [vmem] * 2 + [hbm] * 6 + [smem] * 2,
        out_specs=(hbm, hbm, vmem, vmem, hbm),
        scratch_shapes=[
            VM((R, W), BF),
            VM((R, W), BF),
            VM((R, W), BF),
            VM((R, W), BF),
            VM((D, W), BF),
            VM((adjacent_vertices.shape[1], R), jnp.int32),
            VM((5, D, W), BF),
            VM((16, W), F32),
            VM((16, W), F32),
            VM((W, W), BF),
            VM((D, 4 * W), BF),
            VM((R, D), BF),
            VM((R, 128), F32),
            VM((R, 128), F32),
            VM((R, W), F32),
            VM((R, W), F32),
            VM((R, W), BF),
            VM((R, W), BF),
            VM((R, W), BF),
            VM((R, W), BF),
            VM((R, W), BF),
            VM((R, W), BF),
            VM((R, W), F32),
            VM((R, W), F32),
            VM((R, W), F32),
            VM((R, W), F32),
            VM((NB, PAIRS, 2, NODES, 2 * NODES), BF),
            VM((R, W), F32),
            VM((4, R, W), BF),
            VM((R, W), BF),
            VM((R, W), BF),
            VM((R, W), F32),
            VM((R, 128), F32),
            VM((R, 128), F32),
            VM((2, A, SR, 128), F32),
            VM((2, A - 1, SR, 128), F32),
            VM((2, SR, 128), F32),
            VM((2, B - 1, SR, 128), F32),
            VM((2, max(C - 1, 1), SR, 128), F32),
            VM((2, A, SR, 128), F32),
            VM((5, D, W), F32),
            VM((5, D, W), BF),
            VM((A - 1, 5, PA, W), BF),
            VM((5, PA, W), F32),
            VM((B - 1, 5, PB, W), F32),
            VM((max(C - 1, 1), 5, PB, W), F32),
            VM((3, 8, W), F32),
            VM((A, 8, W), F32),
            VM((B, 8, W), F32),
            VM((C, 8, W), F32),
            dma((15,)),
            dma((8,)),
            dma((2, 7)),
            dma((2,)),
            dma((2, 6)),
            dma((2, 2, 3)),
            dma((2, 2)),
            dma((2, 3, 4)),
            dma((2, 3)),
            dma((2, 3)),
        ],
        compiler_params=pltpu.CompilerParams(
            collective_id=0, has_side_effects=True, vmem_limit_bytes=63 << 20
        ),
    )(
        node_input,
        cotangent,
        norm_gain,
        norm_bias,
        query_weight,
        key_weight,
        value_weight,
        gate_weight,
        out_weight,
        adjacent_vertices.T,
        active_vertex_tally,
        training_period,
    )
    return pl.pallas_call(
        finish_kernel,
        name="finish_kernel",
        out_shape=(
            jax.ShapeDtypeStruct((R, W), BF),
            jax.ShapeDtypeStruct((R, W), BF),
            jax.ShapeDtypeStruct((W,), F32),
            jax.ShapeDtypeStruct((W,), F32),
        )
        + tuple(jax.ShapeDtypeStruct((D, W), F32) for _ in range(5)),
        in_specs=[hbm, hbm, vmem, vmem, hbm],
        out_specs=(hbm, hbm, vmem, vmem) + (hbm,) * 5,
        scratch_shapes=[VM((5, D, W), BF), VM((5, D, W), F32), VM((2, R, W), BF), dma((14,))],
    )(layer_output, input_grad, gain_grad, bias_grad, fin)


def finish_kernel(
    lo_in, ig_in, gain_in, bias_in, fin, lo, ig, gain, bias, gq, gk, gv, gg, go, low, full, wide, sems
):
    loads = []

    def begin(src, dst, into):
        copy = pltpu.make_async_copy(src, dst, sems.at[len(into) + (0 if into is loads else 7)])
        copy.start()
        into.append(copy)

    for i in range(5):
        begin(fin.at[i], low.at[i], loads)
    begin(lo_in, wide.at[0], loads)
    begin(ig_in, wide.at[1], loads)
    gain[...] = gain_in[...]
    bias[...] = bias_in[...]
    stores = []
    for i, out in enumerate((gq, gk, gv, gg, go)):
        loads[i].wait()
        full[i] = low[i].astype(F32)
        begin(full.at[i], out, stores)
    for i, out in enumerate((lo, ig)):
        loads[5 + i].wait()
        begin(wide.at[i], out, stores)
    for cp in stores:
        cp.wait()


def factors(count):
    a = 4 if count % 4 == 0 else count
    b = 4 if count % (a * 4) == 0 else count // a
    return a, b, count // (a * b)


def solution(mesh):
    rows = P("graph", "head")
    cols = P(None, "head")
    return jax.shard_map(
        functools.partial(shards, factors(mesh.shape["graph"])),
        mesh=mesh,
        in_specs=(rows, rows, P("head"), P("head"))
        + (cols,) * 5
        + (P("graph", None), P("graph"), P("graph")),
        out_specs=(rows, rows, P("head"), P("head")) + (cols,) * 5,
        check_vma=False,
    )
```

```python
import functools

import jax
import jax.numpy as jnp
from jax import lax
from jax.experimental import pallas as pl
from jax.experimental.pallas import tpu as pltpu
from jax.sharding import PartitionSpec as P

EPS = 1e-05
BETA = 0.9
LOG2E = 1.4426950408889634
BF = jnp.bfloat16
F32 = jnp.float32
MESH = pl.DeviceIdType.MESH
NODES = 128
QUERY, KEY, VALUE, GATE, OUT = 0, 1, 2, 3, 4


def nn(a, b):
    return lax.dot_general(a, b, (((1,), (0,)), ((), ())), preferred_element_type=F32)


def nt(a, b):
    return lax.dot_general(a, b, (((1,), (1,)), ((), ())), preferred_element_type=F32)


def tn(a, b):
    return lax.dot_general(a, b, (((0,), (0,)), ((), ())), preferred_element_type=F32)


def split(a):
    high = a.astype(BF)
    return high, (a - high.astype(F32)).astype(BF)


def rows_cat(*parts):
    return jnp.concatenate(parts, axis=0)


def lanes_cat(*parts):
    return jnp.concatenate(parts, axis=1)


def block(start, size):
    return pl.ds(pl.multiple_of(start * size, size), size)


def layer_kernel(
    groups,
    x_hbm,
    c_hbm,
    gain_hbm,
    bias_hbm,
    wq,
    wk,
    wv,
    wg,
    wo_hbm,
    adjacent_hbm,
    tally_hbm,
    period_hbm,
    layer_out,
    input_grad,
    gain_grad,
    bias_grad,
    fin_hbm,
    gain,
    bias,
    gain_out,
    bias_out,
    tally,
    period,
    x,
    xo,
    c,
    co,
    wo,
    adjacent,
    weight,
    fin,
    gbs,
    gbo,
    woo,
    wall,
    normed,
    mean_keep,
    rstd_keep,
    q_sig,
    k_sig,
    qh,
    ql,
    kh,
    kl,
    vh,
    vl,
    g,
    dmix,
    datt,
    att,
    prob,
    dq,
    low4,
    mix,
    mixo,
    dn_recv,
    st_send,
    st_recv,
    sum_part,
    sum_recv,
    sum_mid,
    sum_z,
    sum_hi,
    sum_full,
    part,
    psend,
    precv,
    zpart,
    zrecv,
    hrecv,
    gb_part,
    gb_recv,
    gb_z,
    gb_hi,
    load_sems,
    store_sems,
    core_sems,
    mix_sems,
    dn_sems,
    ar_sems,
    arh_sems,
    w_sems,
    wh_sems,
    gb_sems,
):
    A, B, C = groups
    L = A * B
    R, W = x.shape
    NB = R // NODES
    PAIRS = W // 128
    me = lax.axis_index("graph")
    head = lax.axis_index("head")
    other = 1 - head
    lo = lax.rem(me, L)
    hi = me // L
    al = lax.rem(lo, A)
    bl = lo // A

    def dev(h_, b_, a_):
        return (h_ * L + b_ * A + a_, head)

    a_peers = [(lax.rem(al + d, A), dev(hi, bl, lax.rem(al + d, A))) for d in range(1, A)]
    b_peers = [(lax.rem(bl + d, B), dev(hi, lax.rem(bl + d, B), al)) for d in range(1, B)]
    h_peers = [(lax.rem(hi + d, C), dev(lax.rem(hi + d, C), bl, al)) for d in range(1, C)]
    partner = (me, other)
    own_rows = block(head, W)
    oth_rows = block(other, W)

    def send(src, dst, send_sem, recv_sem, to):
        pltpu.make_async_remote_copy(
            src_ref=src,
            dst_ref=dst,
            send_sem=send_sem,
            recv_sem=recv_sem,
            device_id=to,
            device_id_type=MESH,
        ).start()

    def bytes_of(ref, sem):
        pltpu.make_async_copy(ref, ref, sem).wait()

    def wait_both(ref, sems, index):
        bytes_of(ref, sems.at[(0,) + index])
        bytes_of(ref, sems.at[(1,) + index])

    dk, dv, dn_own, dn_send = att, q_sig, g, dmix

    barrier = pltpu.get_barrier_semaphore()
    greeted = [partner] + [to for _, to in a_peers + b_peers + h_peers]
    for to in greeted:
        pl.semaphore_signal(barrier, inc=1, device_id=to, device_id_type=MESH)

    loads = []

    def load(src, dst):
        copy = pltpu.make_async_copy(src, dst, load_sems.at[len(loads)])
        copy.start()
        loads.append(copy)
        return copy

    RB = 1024
    NR = R // RB
    XC = NR
    adjacent_load = load(adjacent_hbm, adjacent)
    x_loads = []
    for i in range(XC):
        piece = pl.ds(i * (R // XC), R // XC)
        x_loads.append(load(x_hbm.at[piece], x.at[piece]))
    wo_load = load(wo_hbm, wo)
    c_load = load(c_hbm, c)
    w_loads = []
    for i, w in ((1, wk), (2, wv), (0, wq), (3, wg)):
        cols = pl.ds(i * W, W)
        w_loads.append(load(w.at[own_rows], wall.at[pl.ds(0, W), cols]))
        w_loads.append(load(w.at[oth_rows], wall.at[pl.ds(W, W), cols]))

    stores = []

    def store(src, dst):
        copy = pltpu.make_async_copy(src, dst, store_sems.at[len(stores)])
        copy.start()
        stores.append(copy)

    small_loads = [
        load(gain_hbm, gain),
        load(bias_hbm, bias),
        load(tally_hbm, tally),
        load(period_hbm, period),
    ]
    for cp in small_loads:
        cp.wait()
    gbs[0:8, :] = jnp.broadcast_to(gain[...].astype(F32).reshape(1, W), (8, W))
    gbs[8:16, :] = jnp.broadcast_to(bias[...].astype(F32).reshape(1, W), (8, W))
    node_of = lax.broadcasted_iota(jnp.int32, (NODES, 128), 0)
    def count_block(i, _):
        for s in (2 * i, 2 * i + 1):
            listed = adjacent[:, block(s, NODES)]
            count = jnp.zeros((NODES, NODES), F32)
            for j in range(listed.shape[0]):
                count = count + jnp.where(listed[j : j + 1, :] == node_of, 1.0, 0.0)
            weight[s] = jnp.where(
                count > 0.0, jnp.log(jnp.maximum(count, 1.0)) * LOG2E, -1e30
            )
        return 0

    pl.semaphore_wait(barrier, len(greeted))

    send(gbs, gbo, core_sems.at[0, 0], core_sems.at[1, 0], partner)
    pieces = [pl.ds(i * (R // XC), R // XC) for i in range(XC)]
    for i, piece in enumerate(pieces):
        x_loads[i].wait()
        send(x.at[piece], xo.at[piece], core_sems.at[0, 3], core_sems.at[1, 3 + i], partner)
    wo_load.wait()
    send(wo.at[oth_rows], woo, core_sems.at[0, 1], core_sems.at[1, 1], partner)
    c_load.wait()
    send(c, co, core_sems.at[0, 2], core_sems.at[1, 2], partner)

    def own_dmix(b, _):
        r = block(b, RB)
        dmix[r, :] = nt(c[r, :], wo[own_rows, :])
        return 0

    lax.fori_loop(0, NR, own_dmix, 0)


    sum_part[...] = jnp.zeros_like(sum_part)
    bytes_of(gbo, core_sems.at[1, 0])
    gain_own, bias_own = gbs[0:1, :], gbs[8:9, :]
    gain_oth, bias_oth = gbo[0:1, :], gbo[8:9, :]
    lane_half = lax.broadcasted_iota(jnp.int32, (1, 128), 1) < 64

    def live_rows(first, a, count):
        node = lax.broadcasted_iota(jnp.int32, (NODES, a.shape[1]), 0)
        return rows_cat(
            *[
                jnp.where(node < tally[first + i], a[i * NODES : (i + 1) * NODES], 0.0)
                for i in range(count)
            ]
        )

    def norm_block(b, carry):
        @pl.when(lax.rem(b, NR // XC) == 0)
        def _():
            i = b // (NR // XC)
            bytes_of(xo.at[block(i, R // XC)], core_sems.at[1, 3 + i])

        r = block(b, RB)
        xa = x[r, :].astype(F32)
        xb = xo[r, :].astype(F32)
        mean = (
            jnp.sum(xa, axis=1, keepdims=True) + jnp.sum(xb, axis=1, keepdims=True)
        ) * (1.0 / (2 * W))
        xa = xa - mean
        xb = xb - mean
        var = (
            jnp.sum(xa * xa, axis=1, keepdims=True) + jnp.sum(xb * xb, axis=1, keepdims=True)
        ) * (1.0 / (2 * W))
        rstd = lax.rsqrt(var + EPS)
        mean_keep[r, :] = jnp.broadcast_to(mean, (RB, 128))
        rstd_keep[r, :] = jnp.broadcast_to(rstd, (RB, 128))
        na = (xa * rstd * gain_own + bias_own).astype(BF)
        nb = (xb * rstd * gain_oth + bias_oth).astype(BF)
        normed[r, 0:W] = na
        normed[r, W : 2 * W] = nb
        kv = nn(lanes_cat(na, nb), wall[:, W : 3 * W])
        kk = kv[:, 0:W]
        vv = kv[:, W : 2 * W]
        kh[r, :], kl[r, :] = split(kk)
        vbf, vlow = split(vv)
        vh[r, :] = vbf
        vl[r, :] = vlow
        sig = jax.nn.sigmoid(kk)
        k_sig[r, :] = sig
        kp = live_rows(b * (RB // NODES), sig, RB // NODES)
        kpb = kp.astype(BF)
        sums, totals = carry
        new_sums, new_totals = [], []
        for p in range(PAIRS):
            ls = slice(p * 128, (p + 1) * 128)
            new_sums.append(sums[p] + tn(kpb[:, ls], vbf[:, ls]))
            new_totals.append(totals[p] + jnp.sum(kp[:, ls], axis=0, keepdims=True))
        return tuple(new_sums), tuple(new_totals)

    def zero_sums():
        return (
            tuple(jnp.zeros((128, 128), F32) for _ in range(PAIRS)),
            tuple(jnp.zeros((1, 128), F32) for _ in range(PAIRS)),
        )

    for cp in w_loads[0:4]:
        cp.wait()
    carry = lax.fori_loop(0, NR, norm_block, zero_sums())

    def pack_sums(slot, carry):
        sums, totals = carry
        packed = rows_cat(
            *[jnp.where(lane_half, sums[p][0:64], sums[p][64:128]) for p in range(PAIRS)]
        )
        for j in range(A):
            sum_part[slot, j, 0:SR, :] = packed[j * SR : (j + 1) * SR]
            for p in range(PAIRS):
                sum_part[slot, j, SR + p : SR + p + 1, :] = totals[p]

    SR = 64 * PAIRS // A

    def ar_scatter(slot):
        for i, (j, to) in enumerate(a_peers):
            send(
                sum_part.at[slot, j],
                sum_recv.at[slot, i],
                ar_sems.at[0, slot, 0],
                ar_sems.at[1, slot, 0],
                to,
            )

    def ar_middle(slot):
        wait_both(sum_recv.at[slot], ar_sems, (slot, 0))
        total = sum_part[slot, al]
        for i in range(A - 1):
            total = total + sum_recv[slot, i]
        sum_mid[slot] = total
        for i, (_, to) in enumerate(b_peers):
            send(
                sum_mid.at[slot],
                sum_z.at[slot, i],
                ar_sems.at[0, slot, 1],
                ar_sems.at[1, slot, 1],
                to,
            )

    def ar_gather(slot):
        wait_both(sum_z.at[slot], ar_sems, (slot, 1))
        total = sum_mid[slot]
        for i in range(B - 1):
            total = total + sum_z[slot, i]
        if C > 1:
            sum_mid[slot] = total
            for i, (_, to) in enumerate(h_peers):
                send(
                    sum_mid.at[slot],
                    sum_hi.at[slot, i],
                    arh_sems.at[0, slot],
                    arh_sems.at[1, slot],
                    to,
                )
            wait_both(sum_hi.at[slot], arh_sems, (slot,))
            for i in range(C - 1):
                total = total + sum_hi[slot, i]
        sum_full[slot, al] = total
        for i, (_, to) in enumerate(a_peers):
            send(
                sum_full.at[slot, al],
                sum_full.at[slot, al],
                ar_sems.at[0, slot, 2],
                ar_sems.at[1, slot, 2],
                to,
            )

    def ar_result(slot):
        wait_both(sum_recv.at[slot], ar_sems, (slot, 2))
        mats, totals = [], []
        packed = rows_cat(*[sum_full[slot, j, 0:SR, :] for j in range(A)])
        for p in range(PAIRS):
            own = packed[p * 64 : (p + 1) * 64]
            mats.append(rows_cat(jnp.where(lane_half, own, 0.0), jnp.where(lane_half, 0.0, own)))
            totals.append(sum_full[slot, 0, SR + p : SR + p + 1, :])
        return mats, totals

    pack_sums(0, carry)
    ar_scatter(0)

    for cp in w_loads[4:]:
        cp.wait()
    bytes_of(woo, core_sems.at[1, 1])
    bytes_of(co, core_sems.at[1, 2])

    def gate_block(b, _):
        r = block(b, RB)
        n = normed[r, :]
        qq = nn(n, wall[:, 0:W])
        q_sig[r, :] = jax.nn.sigmoid(qq)
        qh[r, :], ql[r, :] = split(qq * (0.125 * LOG2E))
        gg = nn(n, wall[:, 3 * W : 4 * W])
        g[r, :] = gg
        dm = dmix[r, :] + nt(co[r, :], woo[...])
        dmix[r, :] = dm
        datt[r, :] = dm * ((1.0 - BETA) * gg + BETA)
        return 0

    lax.fori_loop(0, NR, gate_block, 0)
    ar_middle(0)
    adjacent_load.wait()
    lax.fori_loop(0, NB // 2, count_block, 0)
    ar_gather(0)

    half_row = jnp.where(lane_half, 1.0, 0.0)
    half_a = jnp.broadcast_to(half_row, (NODES, 128)).astype(BF)
    half_b = jnp.broadcast_to(1.0 - half_row, (NODES, 128)).astype(BF)

    def apart(a):
        return rows_cat(a * half_a, a * half_b)

    def joined(a):
        return jnp.where(lane_half, a[0:NODES], a[NODES : 2 * NODES])

    FU = 8
    lanes = [slice(p * 128, (p + 1) * 128) for p in range(PAIRS)]

    def forward_block(i, _):
        chains = [(i * FU + u, p) for u in range(FU) for p in range(PAIRS)]
        scores = []
        for s, p in chains:
            r, ls = block(s, NODES), lanes[p]
            high, low = kh[r, ls], kl[r, ls]
            qbh = apart(qh[r, ls])
            scores.append(
                nt(lanes_cat(high, low, high), lanes_cat(qbh, qbh, apart(ql[r, ls])))
            )
        probs = []
        for j, score in enumerate(scores):
            bias = weight[chains[j][0]]
            score = score + lanes_cat(bias, bias)
            e = jnp.exp2(score - jnp.max(score, axis=0, keepdims=True))
            probs.append(split(e * (1.0 / jnp.sum(e, axis=0, keepdims=True))))
        for (s, p), (high, low) in zip(chains, probs):
            prob[s, p, 0] = high
            prob[s, p, 1] = low
        for (s, p), (high, low) in zip(chains, probs):
            r, ls = block(s, NODES), lanes[p]
            vhigh = vh[r, ls]
            o = tn(
                rows_cat(high, low),
                rows_cat(lanes_cat(vhigh, vl[r, ls]), lanes_cat(vhigh, jnp.zeros_like(vhigh))),
            )
            att[r, ls] = joined(o[:, 0:128] + o[:, 128:256])
        return 0

    lax.fori_loop(0, NB // FU, forward_block, 0)

    mats, totals = ar_result(0)
    square = (2, 128, 128)
    same_head = (lax.broadcasted_iota(jnp.int32, (128, 128), 0) < 64) == (
        lax.broadcasted_iota(jnp.int32, (128, 128), 1) < 64
    )
    ones_bd = jnp.where(same_head, 1.0, 0.0).astype(BF)
    num_w, den_w, back_w = [], [], []
    for p in range(PAIRS):
        sh, sl = split(mats[p])
        th, tl = split(jnp.where(same_head, jnp.broadcast_to(totals[p], (128, 128)), 0.0))
        num_w.append(lanes_cat(sh, sl))
        den_w.append(rows_cat(th, tl))
        back_w.append(lanes_cat(sh, sh, sl))

    GU = 8

    def glob_block(i, carry):
        r = block(i, GU * NODES)
        keep = [(1 - period[i * GU + u]).astype(F32) for u in range(GU)]
        sums, tots = carry
        new_sums, new_tots = [], []
        for p in range(PAIRS):
            ls = lanes[p]
            qp = q_sig[r, ls]
            qpb = qp.astype(BF)
            num = nn(qpb, num_w[p])
            den = nt(qpb, den_w[p])
            inv = 1.0 / (den[:, 0:128] + den[:, 128:256])
            glob = (num[:, 0:128] + num[:, 128:256]) * inv
            at = att[r, ls] + glob
            mix[r, ls] = ((1.0 - BETA) * g[r, ls] * at + BETA * at).astype(BF)
            low4[GATE, r, ls] = (dmix[r, ls] * (1.0 - BETA) * at).astype(BF)
            da = datt[r, ls]
            dnum = rows_cat(*[keep[u] * da[u * NODES : (u + 1) * NODES] for u in range(GU)]) * inv
            dh, dl = split(dnum)
            th, tl = split(dnum * glob)
            dden = -nn(lanes_cat(th, tl), rows_cat(ones_bd, ones_bd))
            dqp = nt(lanes_cat(dh, dl, dh), back_w[p]) + dden * totals[p]
            dq[r, ls] = dqp * qp * (1.0 - qp)
            new_sums.append(sums[p] + tn(qpb, dh))
            new_tots.append(tots[p] + jnp.sum(dden * qp, axis=0, keepdims=True))
        return tuple(new_sums), tuple(new_tots)

    carry = lax.fori_loop(0, NB // GU, glob_block, zero_sums())
    pack_sums(1, carry)
    ar_scatter(1)
    send(mix, mixo, mix_sems.at[0], mix_sems.at[1], partner)

    KB = 1024

    def weight_grads(kinds):
        def step(i, _):
            r = block(i, KB)
            n = normed[r, :]
            for kind in kinds:
                got = tn(n, low4[kind, r, :])
                part[kind, own_rows, :] += got[0:W]
                part[kind, oth_rows, :] += got[W : 2 * W]
            return 0

        for kind in kinds:
            part[kind] = jnp.zeros(part.shape[1:], F32)
        lax.fori_loop(0, R // KB, step, 0)

    def out_grads():
        def step(i, _):
            r = block(i, KB)
            cc = c[r, :]
            part[OUT, own_rows, :] += tn(mix[r, :], cc)
            part[OUT, oth_rows, :] += tn(mixo[r, :], cc)
            return 0

        part[OUT] = jnp.zeros(part.shape[1:], F32)
        lax.fori_loop(0, R // KB, step, 0)

    D = 2 * W
    PA = D // A
    PB = PA // B

    kinds_of = {w: (w,) for w in range(5)}
    span = {w: pl.ds(w, 1) for w in range(5)}

    def w_scatter(w):
        for kind in kinds_of[w]:
            psend[kind] = part[kind].astype(BF)
        for i, (j, to) in enumerate(a_peers):
            send(
                psend.at[span[w], block(j, PA)],
                precv.at[i, span[w]],
                w_sems.at[0, w, 0],
                w_sems.at[1, w, 0],
                to,
            )

    def w_middle(w):
        wait_both(precv.at[:, span[w]], w_sems, (w, 0))
        for kind in kinds_of[w]:
            total = part[kind, block(al, PA), :]
            for i in range(A - 1):
                total = total + precv[i, kind].astype(F32)
            zpart[kind] = total
        for i, (j, to) in enumerate(b_peers):
            send(
                zpart.at[span[w], block(j, PB)],
                zrecv.at[i, span[w]],
                w_sems.at[0, w, 1],
                w_sems.at[1, w, 1],
                to,
            )

    here = pl.ds(pl.multiple_of(al * PA + bl * PB, PB), PB)

    def w_spread(w):
        wait_both(zrecv.at[:, span[w]], w_sems, (w, 1))
        totals = {}
        for kind in kinds_of[w]:
            total = zpart[kind, block(bl, PB), :]
            for i in range(B - 1):
                total = total + zrecv[i, kind]
            totals[kind] = total
        if C > 1:
            for kind in kinds_of[w]:
                zpart[kind, block(bl, PB), :] = totals[kind]
            for i, (_, to) in enumerate(h_peers):
                send(
                    zpart.at[span[w], block(bl, PB)],
                    hrecv.at[i, span[w]],
                    wh_sems.at[0, w],
                    wh_sems.at[1, w],
                    to,
                )
            wait_both(hrecv.at[:, span[w]], wh_sems, (w,))
            for kind in kinds_of[w]:
                for i in range(C - 1):
                    totals[kind] = totals[kind] + hrecv[i, kind]
        for kind in kinds_of[w]:
            fin[kind, here, :] = totals[kind].astype(BF)
        for i, (_, to) in enumerate(b_peers):
            send(
                fin.at[span[w], here],
                fin.at[span[w], here],
                w_sems.at[0, w, 2],
                w_sems.at[1, w, 2],
                to,
            )

    def w_gather(w):
        wait_both(fin.at[span[w], pl.ds(0, (B - 1) * PB)], w_sems, (w, 2))
        for i, (_, to) in enumerate(a_peers):
            send(
                fin.at[span[w], block(al, PA)],
                fin.at[span[w], block(al, PA)],
                w_sems.at[0, w, 3],
                w_sems.at[1, w, 3],
                to,
            )

    def w_keep(w):
        wait_both(fin.at[span[w], pl.ds(0, (A - 1) * PA)], w_sems, (w, 3))
        store(fin.at[span[w]], fin_hbm.at[span[w]])

    weight_grads((GATE,))
    w_scatter(GATE)
    bytes_of(mixo, mix_sems.at[1])
    out_grads()
    w_scatter(OUT)

    BU = 4

    def backward_block(i, _):
        @pl.when(i == 1)
        def _():
            ar_middle(1)

        @pl.when(i == 2)
        def _():
            w_middle(GATE)

        @pl.when(i == 3)
        def _():
            ar_gather(1)

        chains = [(block(i * BU + u, NODES), i * BU + u, p) for u in range(BU) for p in range(PAIRS)]
        outs, dps = [], []
        for r, s, p in chains:
            ls = lanes[p]
            oh, ol = split(datt[r, ls])
            oh, ol = apart(oh), apart(ol)
            outs.append((oh, ol))
            high = vh[r, ls]
            dps.append(nt(lanes_cat(high, vl[r, ls], high), lanes_cat(oh, oh, ol)))
        dss = []
        for (r, s, p), dp in zip(chains, dps):
            pr = prob[s, p, 0].astype(F32) + prob[s, p, 1].astype(F32)
            dss.append(split(pr * (dp - jnp.sum(pr * dp, axis=0, keepdims=True))))
        for (r, s, p), (oh, ol) in zip(chains, outs):
            got = nn(prob[s, p, 0], lanes_cat(oh, ol))
            dv[r, lanes[p]] = got[:, 0:128] + got[:, 128:256] + nn(prob[s, p, 1], oh)
        for (r, s, p), (high, low) in zip(chains, dss):
            ls = lanes[p]
            qbh = apart(qh[r, ls])
            got = nn(high, lanes_cat(qbh, apart(ql[r, ls])))
            dk[r, ls] = (got[:, 0:128] + got[:, 128:256] + nn(low, qbh)) * (1.0 / LOG2E)
        for (r, s, p), (high, low) in zip(chains, dss):
            ls = lanes[p]
            khigh = kh[r, ls]
            got = tn(
                rows_cat(high, low),
                rows_cat(lanes_cat(khigh, kl[r, ls]), lanes_cat(khigh, jnp.zeros_like(khigh))),
            )
            got = joined(got[:, 0:128] + got[:, 128:256]) * 0.125
            low4[QUERY, r, ls] = (dq[r, ls] + got).astype(BF)
        return 0

    lax.fori_loop(0, NB // BU, backward_block, 0)
    w_middle(OUT)
    weight_grads((QUERY,))
    w_scatter(QUERY)
    w_spread(GATE)

    mats, totals = ar_result(1)
    dsum = [m.astype(BF) for m in mats]

    KU = 8

    def key_block(i, _):
        r = block(i, KU * NODES)
        for p in range(PAIRS):
            ls = lanes[p]
            sig = k_sig[r, ls]
            kp = live_rows(i * KU, sig, KU)
            dkp = nt(vh[r, ls], dsum[p]) + totals[p]
            low4[KEY, r, ls] = (dk[r, ls] + dkp * kp * (1.0 - sig)).astype(BF)
            low4[VALUE, r, ls] = (dv[r, ls] + nn(kp.astype(BF), dsum[p])).astype(BF)
        return 0

    lax.fori_loop(0, NB // KU, key_block, 0)
    weight_grads((KEY,))
    w_scatter(KEY)
    weight_grads((VALUE,))
    w_scatter(VALUE)
    w_spread(OUT)

    DC = NR

    def normed_block(b, _):
        r = block(b, RB)
        grads = lanes_cat(*[low4[kind, r, :] for kind in (QUERY, KEY, VALUE, GATE)])
        dn = nt(grads, wall[...])
        dn_own[r, :] = dn[:, 0:W]
        dn_send[r, :] = dn[:, W : 2 * W]
        mean = mean_keep[r, 0:1]
        rstd = rstd_keep[r, 0:1]
        sa = dn[:, 0:W] * gain_own
        sb = dn[:, W : 2 * W] * gain_oth
        ha = (x[r, :].astype(F32) - mean) * rstd
        hb = (xo[r, :].astype(F32) - mean) * rstd
        s1 = jnp.sum(sa, axis=1, keepdims=True) + jnp.sum(sb, axis=1, keepdims=True)
        s2 = jnp.sum(sa * ha, axis=1, keepdims=True) + jnp.sum(sb * hb, axis=1, keepdims=True)
        st_send[r, :] = jnp.where(lane_half, s1, s2)

        @pl.when(lax.rem(b, NR // DC) == NR // DC - 1)
        def _():
            i = b // (NR // DC)
            piece = block(i, R // DC)
            send(dn_send.at[piece], dn_recv.at[piece], dn_sems.at[0, 0], dn_sems.at[0, 2 + i], partner)
            send(st_send.at[piece], st_recv.at[piece], dn_sems.at[0, 1], dn_sems.at[1, 2 + i], partner)

        @pl.when(b == NR // 2)
        def _():
            w_middle(QUERY)

        return 0

    lax.fori_loop(0, NR, normed_block, 0)
    w_middle(KEY)

    def out_block(b, _):
        r = block(b, RB)
        got = nn(mix[r, :], wo[own_rows, :]) + nn(mixo[r, :], wo[oth_rows, :])
        mixo[r, :] = (x[r, :].astype(F32) + got).astype(BF)
        return 0

    lax.fori_loop(0, NR, out_block, 0)
    store(mixo, layer_out)
    w_middle(VALUE)
    w_gather(GATE)
    w_gather(OUT)
    w_spread(QUERY)
    w_spread(KEY)

    def input_block(b, carry):
        @pl.when(lax.rem(b, NR // DC) == 0)
        def _():
            i = b // (NR // DC)
            piece = block(i, R // DC)
            bytes_of(dn_recv.at[piece], dn_sems.at[0, 2 + i])
            bytes_of(st_recv.at[piece], dn_sems.at[1, 2 + i])

        gain_sum, bias_sum = carry
        r = block(b, RB)
        dn = dn_own[r, :] + dn_recv[r, :]
        st = st_send[r, :] + st_recv[r, :]
        mean = mean_keep[r, 0:1]
        rstd = rstd_keep[r, 0:1]
        s1 = st[:, 0:1] * (1.0 / (2 * W))
        s2 = st[:, 64:65] * (1.0 / (2 * W))
        ha = (x[r, :].astype(F32) - mean) * rstd
        inner = rstd * (dn * gain_own - s1 - ha * s2)
        co[r, :] = (c[r, :].astype(F32) + inner).astype(BF)
        return (
            gain_sum + jnp.sum(dn * ha, axis=0, keepdims=True),
            bias_sum + jnp.sum(dn, axis=0, keepdims=True),
        )

    carry = (jnp.zeros((1, W), F32), jnp.zeros((1, W), F32))
    carry = lax.fori_loop(0, NR, input_block, carry)
    store(co, input_grad)
    w_spread(VALUE)
    w_gather(QUERY)
    w_gather(KEY)

    row = lax.broadcasted_iota(jnp.int32, (8, W), 0)
    total = jnp.where(row == 0, carry[0], jnp.where(row == 1, carry[1], 0.0))

    def in_order(total, step, held, index, count, peers):
        gb_part[step] = total
        held[pl.ds(index, 1)] = total[None]
        for _, to in peers:
            send(gb_part.at[step], held.at[index], gb_sems.at[0, step], gb_sems.at[1, step], to)
        return count

    def added(step, held, count):
        wait_both(held.at[pl.ds(0, count - 1)], gb_sems, (step,))
        total = held[0]
        for i in range(1, count):
            total = total + held[i]
        return total

    in_order(total, 0, gb_recv, al, A, a_peers)
    w_gather(VALUE)
    in_order(added(0, gb_recv, A), 1, gb_z, bl, B, b_peers)
    w_keep(GATE)
    w_keep(OUT)
    w_keep(QUERY)
    total = added(1, gb_z, B)
    if C > 1:
        in_order(total, 2, gb_hi, hi, C, h_peers)
        total = added(2, gb_hi, C)
    gain_out[...] = total[0:1].reshape(W)
    bias_out[...] = total[1:2].reshape(W)
    store(gain_out, gain_grad)
    store(bias_out, bias_grad)
    w_keep(KEY)
    w_keep(VALUE)
    for cp in stores:
        cp.wait()
    bytes_of(gbs, core_sems.at[0, 0])
    bytes_of(woo, core_sems.at[0, 1])
    bytes_of(c, core_sems.at[0, 2])
    bytes_of(x, core_sems.at[0, 3])
    bytes_of(mix, mix_sems.at[0])
    bytes_of(dn_send, dn_sems.at[0, 0])
    bytes_of(st_send, dn_sems.at[0, 1])


def shards(
    groups,
    node_input,
    cotangent,
    norm_gain,
    norm_bias,
    query_weight,
    key_weight,
    value_weight,
    gate_weight,
    out_weight,
    adjacent_vertices,
    active_vertex_tally,
    training_period,
):
    A, B, C = groups
    R, W = node_input.shape
    D = 2 * W
    NB = R // NODES
    PAIRS = W // 128
    SR = 64 * PAIRS // A + 8
    PA = D // A
    PB = PA // B
    VM = pltpu.VMEM
    dma = pltpu.SemaphoreType.DMA
    hbm = pl.BlockSpec(memory_space=pl.ANY)
    layer_output, input_grad, gain_grad, bias_grad, fin = pl.pallas_call(
        functools.partial(layer_kernel, groups),
        name="layer_kernel",
        out_shape=(
            jax.ShapeDtypeStruct((R, W), BF),
            jax.ShapeDtypeStruct((R, W), BF),
            jax.ShapeDtypeStruct((W,), F32),
            jax.ShapeDtypeStruct((W,), F32),
            jax.ShapeDtypeStruct((5, D, W), BF),
        ),
        in_specs=[hbm] * 12,
        out_specs=(hbm,) * 5,
        scratch_shapes=[
            VM((W,), BF),
            VM((W,), BF),
            VM((W,), F32),
            VM((W,), F32),
            pltpu.SMEM((NB,), jnp.int32),
            pltpu.SMEM((NB,), jnp.int32),
            VM((R, W), BF),
            VM((R, W), BF),
            VM((R, W), BF),
            VM((R, W), BF),
            VM((D, W), BF),
            VM((adjacent_vertices.shape[1], R), jnp.int32),
            VM((NB, NODES, NODES), F32),
            VM((5, D, W), BF),
            VM((16, W), F32),
            VM((16, W), F32),
            VM((W, W), BF),
            VM((D, 4 * W), BF),
            VM((R, D), BF),
            VM((R, 128), F32),
            VM((R, 128), F32),
            VM((R, W), F32),
            VM((R, W), F32),
            VM((R, W), BF),
            VM((R, W), BF),
            VM((R, W), BF),
            VM((R, W), BF),
            VM((R, W), BF),
            VM((R, W), BF),
            VM((R, W), F32),
            VM((R, W), F32),
            VM((R, W), F32),
            VM((R, W), F32),
            VM((NB, PAIRS, 2, NODES, 2 * NODES), BF),
            VM((R, W), F32),
            VM((4, R, W), BF),
            VM((R, W), BF),
            VM((R, W), BF),
            VM((R, W), F32),
            VM((R, 128), F32),
            VM((R, 128), F32),
            VM((2, A, SR, 128), F32),
            VM((2, A - 1, SR, 128), F32),
            VM((2, SR, 128), F32),
            VM((2, B - 1, SR, 128), F32),
            VM((2, max(C - 1, 1), SR, 128), F32),
            VM((2, A, SR, 128), F32),
            VM((5, D, W), F32),
            VM((5, D, W), BF),
            VM((A - 1, 5, PA, W), BF),
            VM((5, PA, W), F32),
            VM((B - 1, 5, PB, W), F32),
            VM((max(C - 1, 1), 5, PB, W), F32),
            VM((3, 8, W), F32),
            VM((A, 8, W), F32),
            VM((B, 8, W), F32),
            VM((C, 8, W), F32),
            dma((20,)),
            dma((10,)),
            dma((2, 7)),
            dma((2,)),
            dma((2, 6)),
            dma((2, 2, 3)),
            dma((2, 2)),
            dma((2, 5, 4)),
            dma((2, 5)),
            dma((2, 3)),
        ],
        compiler_params=pltpu.CompilerParams(
            collective_id=0, has_side_effects=True, vmem_limit_bytes=63 << 20
        ),
    )(
        node_input,
        cotangent,
        norm_gain,
        norm_bias,
        query_weight,
        key_weight,
        value_weight,
        gate_weight,
        out_weight,
        adjacent_vertices.T,
        active_vertex_tally,
        training_period,
    )
    return pl.pallas_call(
        finish_kernel,
        name="finish_kernel",
        out_shape=(
            jax.ShapeDtypeStruct((R, W), BF),
            jax.ShapeDtypeStruct((R, W), BF),
            jax.ShapeDtypeStruct((W,), F32),
            jax.ShapeDtypeStruct((W,), F32),
        )
        + tuple(jax.ShapeDtypeStruct((D, W), F32) for _ in range(5)),
        in_specs=[hbm] * 5,
        out_specs=(hbm,) * 9,
        scratch_shapes=[
            VM((5, D, W), BF),
            VM((5, D, W), F32),
            VM((2, R, W), BF),
            VM((W,), F32),
            VM((W,), F32),
            dma((18,)),
        ],
    )(layer_output, input_grad, gain_grad, bias_grad, fin)


def finish_kernel(
    lo_in, ig_in, gain_in, bias_in, fin, lo, ig, gain, bias, gq, gk, gv, gg, go, *scratch
):
    low, full, wide, gain_here, bias_here, sems = scratch
    loads, stores = [], []

    def begin(src, dst, into):
        copy = pltpu.make_async_copy(src, dst, sems.at[len(into) + (0 if into is loads else 9)])
        copy.start()
        into.append(copy)

    for i in range(5):
        begin(fin.at[i], low.at[i], loads)
    straight = (
        (lo_in, wide.at[0], lo),
        (ig_in, wide.at[1], ig),
        (gain_in, gain_here, gain),
        (bias_in, bias_here, bias),
    )
    for src, here, _ in straight:
        begin(src, here, loads)
    for i, out in enumerate((gq, gk, gv, gg, go)):
        loads[i].wait()
        full[i] = low[i].astype(F32)
        begin(full.at[i], out, stores)
    for i, (_, here, out) in enumerate(straight):
        loads[5 + i].wait()
        begin(here, out, stores)
    for cp in stores:
        cp.wait()


def factors(count):
    a = 4 if count % 4 == 0 else count
    b = 4 if count % (a * 4) == 0 else count // a
    return a, b, count // (a * b)


def solution(mesh):
    rows = P("graph", "head")
    cols = P(None, "head")
    return jax.shard_map(
        functools.partial(shards, factors(mesh.shape["graph"])),
        mesh=mesh,
        in_specs=(rows, rows, P("head"), P("head"))
        + (cols,) * 5
        + (P("graph", None), P("graph"), P("graph")),
        out_specs=(rows, rows, P("head"), P("head")) + (cols,) * 5,
        check_vma=False,
    )
```

```python
import functools

import jax
import jax.numpy as jnp
from jax import lax
from jax.experimental import pallas as pl
from jax.experimental.pallas import tpu as pltpu
from jax.sharding import PartitionSpec as P

EPS = 1e-05
BETA = 0.9
LOG2E = 1.4426950408889634
BF = jnp.bfloat16
F32 = jnp.float32
MESH = pl.DeviceIdType.MESH
NODES = 128
QUERY, KEY, VALUE, GATE, OUT = 0, 1, 2, 3, 4


def nn(a, b):
    return lax.dot_general(a, b, (((1,), (0,)), ((), ())), preferred_element_type=F32)


def nt(a, b):
    return lax.dot_general(a, b, (((1,), (1,)), ((), ())), preferred_element_type=F32)


def tn(a, b):
    return lax.dot_general(a, b, (((0,), (0,)), ((), ())), preferred_element_type=F32)


def split(a):
    high = a.astype(BF)
    return high, (a - high.astype(F32)).astype(BF)


def rows_cat(*parts):
    return jnp.concatenate(parts, axis=0)


def lanes_cat(*parts):
    return jnp.concatenate(parts, axis=1)


def block(start, size):
    return pl.ds(pl.multiple_of(start * size, size), size)


def layer_kernel(
    groups,
    x_hbm,
    c_hbm,
    gain_hbm,
    bias_hbm,
    wq,
    wk,
    wv,
    wg,
    wo_hbm,
    adjacent_hbm,
    tally_hbm,
    period_hbm,
    layer_out,
    input_grad,
    gain_grad,
    bias_grad,
    fin_hbm,
    gain,
    bias,
    gain_out,
    bias_out,
    tally,
    period,
    x,
    xo,
    c,
    co,
    wo,
    adjacent,
    weight,
    fin,
    gbs,
    gbo,
    woo,
    wall,
    normed,
    mean_keep,
    rstd_keep,
    q_sig,
    k_sig,
    qh,
    ql,
    kh,
    kl,
    vh,
    vl,
    g,
    dmix,
    datt,
    att,
    prob,
    dq,
    low4,
    mix,
    mixo,
    dn_recv,
    st_send,
    st_recv,
    sum_part,
    sum_recv,
    sum_mid,
    sum_z,
    sum_hi,
    sum_full,
    part,
    psend,
    precv,
    zpart,
    zrecv,
    hrecv,
    gb_part,
    gb_recv,
    gb_z,
    gb_hi,
    load_sems,
    store_sems,
    core_sems,
    mix_sems,
    dn_sems,
    ar_sems,
    arh_sems,
    w_sems,
    wh_sems,
    gb_sems,
):
    A, B, C = groups
    L = A * B
    R, W = x.shape
    NB = R // NODES
    PAIRS = W // 128
    me = lax.axis_index("graph")
    head = lax.axis_index("head")
    other = 1 - head
    lo = lax.rem(me, L)
    hi = me // L
    al = lax.rem(lo, A)
    bl = lo // A

    def dev(h_, b_, a_):
        return (h_ * L + b_ * A + a_, head)

    a_peers = [(lax.rem(al + d, A), dev(hi, bl, lax.rem(al + d, A))) for d in range(1, A)]
    b_peers = [(lax.rem(bl + d, B), dev(hi, lax.rem(bl + d, B), al)) for d in range(1, B)]
    h_peers = [(lax.rem(hi + d, C), dev(lax.rem(hi + d, C), bl, al)) for d in range(1, C)]
    partner = (me, other)
    own_rows = block(head, W)
    oth_rows = block(other, W)

    def send(src, dst, send_sem, recv_sem, to):
        pltpu.make_async_remote_copy(
            src_ref=src,
            dst_ref=dst,
            send_sem=send_sem,
            recv_sem=recv_sem,
            device_id=to,
            device_id_type=MESH,
        ).start()

    def bytes_of(ref, sem):
        pltpu.make_async_copy(ref, ref, sem).wait()

    def wait_both(ref, sems, index):
        bytes_of(ref, sems.at[(0,) + index])
        bytes_of(ref, sems.at[(1,) + index])

    dk, dv, dn_own, dn_send = att, q_sig, g, dmix

    barrier = pltpu.get_barrier_semaphore()
    greeted = [partner] + [to for _, to in a_peers + b_peers + h_peers]
    for to in greeted:
        pl.semaphore_signal(barrier, inc=1, device_id=to, device_id_type=MESH)

    loads = []

    def load(src, dst):
        copy = pltpu.make_async_copy(src, dst, load_sems.at[len(loads)])
        copy.start()
        loads.append(copy)
        return copy

    RB = 1024
    NR = R // RB
    XC = NR
    adjacent_load = load(adjacent_hbm, adjacent)
    x_loads = []
    for i in range(XC):
        piece = pl.ds(i * (R // XC), R // XC)
        x_loads.append(load(x_hbm.at[piece], x.at[piece]))
    wo_load = load(wo_hbm, wo)
    c_load = load(c_hbm, c)
    w_loads = []
    for i, w in ((1, wk), (2, wv), (0, wq), (3, wg)):
        cols = pl.ds(i * W, W)
        w_loads.append(load(w.at[own_rows], wall.at[pl.ds(0, W), cols]))
        w_loads.append(load(w.at[oth_rows], wall.at[pl.ds(W, W), cols]))

    stores = []

    def store(src, dst):
        copy = pltpu.make_async_copy(src, dst, store_sems.at[len(stores)])
        copy.start()
        stores.append(copy)

    small_loads = [
        load(gain_hbm, gain),
        load(bias_hbm, bias),
        load(tally_hbm, tally),
        load(period_hbm, period),
    ]
    for cp in small_loads:
        cp.wait()
    gbs[0:8, :] = jnp.broadcast_to(gain[...].astype(F32).reshape(1, W), (8, W))
    gbs[8:16, :] = jnp.broadcast_to(bias[...].astype(F32).reshape(1, W), (8, W))
    node_of = lax.broadcasted_iota(jnp.int32, (NODES, 128), 0)
    def count_block(i, _):
        node = node_of.astype(F32).astype(BF)
        one = jnp.ones((NODES, NODES), BF)
        zero = jnp.zeros((NODES, NODES), BF)
        for s in (2 * i, 2 * i + 1):
            listed = adjacent[:, block(s, NODES)].astype(F32).astype(BF)
            count = zero
            for j in range(listed.shape[0]):
                same = jnp.broadcast_to(listed[j : j + 1, :], (NODES, NODES)) == node
                count = count + jnp.where(same, one, zero)
            count = count.astype(F32)
            weight[s] = jnp.where(
                count > 0.0, jnp.log(jnp.maximum(count, 1.0)) * LOG2E, -1e30
            )
        return 0

    pl.semaphore_wait(barrier, len(greeted))

    send(gbs, gbo, core_sems.at[0, 0], core_sems.at[1, 0], partner)
    pieces = [pl.ds(i * (R // XC), R // XC) for i in range(XC)]
    for i, piece in enumerate(pieces):
        x_loads[i].wait()
        send(x.at[piece], xo.at[piece], core_sems.at[0, 3], core_sems.at[1, 3 + i], partner)
    wo_load.wait()
    send(wo.at[oth_rows], woo, core_sems.at[0, 1], core_sems.at[1, 1], partner)
    c_load.wait()
    send(c, co, core_sems.at[0, 2], core_sems.at[1, 2], partner)

    adjacent_load.wait()
    lax.fori_loop(0, NB // 2, count_block, 0)

    sum_part[...] = jnp.zeros_like(sum_part)
    bytes_of(gbo, core_sems.at[1, 0])
    gain_own, bias_own = gbs[0:1, :], gbs[8:9, :]
    gain_oth, bias_oth = gbo[0:1, :], gbo[8:9, :]
    lane_half = lax.broadcasted_iota(jnp.int32, (1, 128), 1) < 64

    def live_rows(first, a, count):
        node = lax.broadcasted_iota(jnp.int32, (NODES, a.shape[1]), 0)
        return rows_cat(
            *[
                jnp.where(node < tally[first + i], a[i * NODES : (i + 1) * NODES], 0.0)
                for i in range(count)
            ]
        )

    def norm_block(b, carry):
        @pl.when(lax.rem(b, NR // XC) == 0)
        def _():
            i = b // (NR // XC)
            bytes_of(xo.at[block(i, R // XC)], core_sems.at[1, 3 + i])

        r = block(b, RB)
        xa = x[r, :].astype(F32)
        xb = xo[r, :].astype(F32)
        mean = (
            jnp.sum(xa, axis=1, keepdims=True) + jnp.sum(xb, axis=1, keepdims=True)
        ) * (1.0 / (2 * W))
        xa = xa - mean
        xb = xb - mean
        var = (
            jnp.sum(xa * xa, axis=1, keepdims=True) + jnp.sum(xb * xb, axis=1, keepdims=True)
        ) * (1.0 / (2 * W))
        rstd = lax.rsqrt(var + EPS)
        mean_keep[r, :] = jnp.broadcast_to(mean, (RB, 128))
        rstd_keep[r, :] = jnp.broadcast_to(rstd, (RB, 128))
        na = (xa * rstd * gain_own + bias_own).astype(BF)
        nb = (xb * rstd * gain_oth + bias_oth).astype(BF)
        normed[r, 0:W] = na
        normed[r, W : 2 * W] = nb
        kv = nn(lanes_cat(na, nb), wall[:, W : 3 * W])
        kk = kv[:, 0:W]
        vv = kv[:, W : 2 * W]
        kh[r, :], kl[r, :] = split(kk)
        vbf, vlow = split(vv)
        vh[r, :] = vbf
        vl[r, :] = vlow
        sig = jax.nn.sigmoid(kk)
        k_sig[r, :] = sig
        kp = live_rows(b * (RB // NODES), sig, RB // NODES)
        kpb = kp.astype(BF)
        sums, totals = carry
        new_sums, new_totals = [], []
        for p in range(PAIRS):
            ls = slice(p * 128, (p + 1) * 128)
            new_sums.append(sums[p] + tn(kpb[:, ls], vbf[:, ls]))
            new_totals.append(totals[p] + jnp.sum(kp[:, ls], axis=0, keepdims=True))
        return tuple(new_sums), tuple(new_totals)

    def zero_sums():
        return (
            tuple(jnp.zeros((128, 128), F32) for _ in range(PAIRS)),
            tuple(jnp.zeros((1, 128), F32) for _ in range(PAIRS)),
        )

    for cp in w_loads[0:4]:
        cp.wait()
    carry = lax.fori_loop(0, NR, norm_block, zero_sums())

    def pack_sums(slot, carry):
        sums, totals = carry
        packed = rows_cat(
            *[jnp.where(lane_half, sums[p][0:64], sums[p][64:128]) for p in range(PAIRS)]
        )
        for j in range(A):
            sum_part[slot, j, 0:SR, :] = packed[j * SR : (j + 1) * SR]
            for p in range(PAIRS):
                sum_part[slot, j, SR + p : SR + p + 1, :] = totals[p]

    SR = 64 * PAIRS // A

    def ar_scatter(slot):
        for i, (j, to) in enumerate(a_peers):
            send(
                sum_part.at[slot, j],
                sum_recv.at[slot, i],
                ar_sems.at[0, slot, 0],
                ar_sems.at[1, slot, 0],
                to,
            )

    def ar_middle(slot):
        wait_both(sum_recv.at[slot], ar_sems, (slot, 0))
        total = sum_part[slot, al]
        for i in range(A - 1):
            total = total + sum_recv[slot, i]
        sum_mid[slot] = total
        for i, (_, to) in enumerate(b_peers):
            send(
                sum_mid.at[slot],
                sum_z.at[slot, i],
                ar_sems.at[0, slot, 1],
                ar_sems.at[1, slot, 1],
                to,
            )

    def ar_gather(slot):
        wait_both(sum_z.at[slot], ar_sems, (slot, 1))
        total = sum_mid[slot]
        for i in range(B - 1):
            total = total + sum_z[slot, i]
        if C > 1:
            sum_mid[slot] = total
            for i, (_, to) in enumerate(h_peers):
                send(
                    sum_mid.at[slot],
                    sum_hi.at[slot, i],
                    arh_sems.at[0, slot],
                    arh_sems.at[1, slot],
                    to,
                )
            wait_both(sum_hi.at[slot], arh_sems, (slot,))
            for i in range(C - 1):
                total = total + sum_hi[slot, i]
        sum_full[slot, al] = total
        for i, (_, to) in enumerate(a_peers):
            send(
                sum_full.at[slot, al],
                sum_full.at[slot, al],
                ar_sems.at[0, slot, 2],
                ar_sems.at[1, slot, 2],
                to,
            )

    def ar_result(slot):
        wait_both(sum_recv.at[slot], ar_sems, (slot, 2))
        mats, totals = [], []
        packed = rows_cat(*[sum_full[slot, j, 0:SR, :] for j in range(A)])
        for p in range(PAIRS):
            own = packed[p * 64 : (p + 1) * 64]
            mats.append(rows_cat(jnp.where(lane_half, own, 0.0), jnp.where(lane_half, 0.0, own)))
            totals.append(sum_full[slot, 0, SR + p : SR + p + 1, :])
        return mats, totals

    pack_sums(0, carry)
    ar_scatter(0)

    for cp in w_loads[4:]:
        cp.wait()
    bytes_of(woo, core_sems.at[1, 1])
    bytes_of(co, core_sems.at[1, 2])

    def gate_block(b, _):
        r = block(b, RB)
        n = normed[r, :]
        qq = nn(n, wall[:, 0:W])
        q_sig[r, :] = jax.nn.sigmoid(qq)
        qh[r, :], ql[r, :] = split(qq * (0.125 * LOG2E))
        gg = nn(n, wall[:, 3 * W : 4 * W])
        g[r, :] = gg
        dm = nt(lanes_cat(c[r, :], co[r, :]), lanes_cat(wo[own_rows, :], woo[...]))
        dmix[r, :] = dm
        datt[r, :] = dm * ((1.0 - BETA) * gg + BETA)
        return 0

    lax.fori_loop(0, NR, gate_block, 0)
    ar_middle(0)

    half_row = jnp.where(lane_half, 1.0, 0.0)
    half_a = jnp.broadcast_to(half_row, (NODES, 128)).astype(BF)
    half_b = jnp.broadcast_to(1.0 - half_row, (NODES, 128)).astype(BF)

    def apart(a):
        return rows_cat(a * half_a, a * half_b)

    def joined(a):
        return jnp.where(lane_half, a[0:NODES], a[NODES : 2 * NODES])

    FU = 4
    lanes = [slice(p * 128, (p + 1) * 128) for p in range(PAIRS)]

    def forward_block(i, _):
        @pl.when(i == 3)
        def _():
            ar_gather(0)

        chains = [(i * FU + u, p) for u in range(FU) for p in range(PAIRS)]
        scores = []
        for s, p in chains:
            r, ls = block(s, NODES), lanes[p]
            high, low = kh[r, ls], kl[r, ls]
            qbh = apart(qh[r, ls])
            scores.append(
                nt(lanes_cat(high, low, high), lanes_cat(qbh, qbh, apart(ql[r, ls])))
            )
        probs = []
        for j, score in enumerate(scores):
            bias = weight[chains[j][0]]
            score = score + lanes_cat(bias, bias)
            e = jnp.exp2(score - jnp.max(score, axis=0, keepdims=True))
            probs.append(split(e * (1.0 / jnp.sum(e, axis=0, keepdims=True))))
        for (s, p), (high, low) in zip(chains, probs):
            prob[s, p, 0] = high
            prob[s, p, 1] = low
        for (s, p), (high, low) in zip(chains, probs):
            r, ls = block(s, NODES), lanes[p]
            vhigh = vh[r, ls]
            o = tn(
                rows_cat(high, low),
                rows_cat(lanes_cat(vhigh, vl[r, ls]), lanes_cat(vhigh, jnp.zeros_like(vhigh))),
            )
            att[r, ls] = joined(o[:, 0:128] + o[:, 128:256])
        return 0

    lax.fori_loop(0, NB // FU, forward_block, 0)

    mats, totals = ar_result(0)
    square = (2, 128, 128)
    same_head = (lax.broadcasted_iota(jnp.int32, (128, 128), 0) < 64) == (
        lax.broadcasted_iota(jnp.int32, (128, 128), 1) < 64
    )
    ones_bd = jnp.where(same_head, 1.0, 0.0).astype(BF)
    num_w, den_w, back_w = [], [], []
    for p in range(PAIRS):
        sh, sl = split(mats[p])
        th, tl = split(jnp.where(same_head, jnp.broadcast_to(totals[p], (128, 128)), 0.0))
        num_w.append(lanes_cat(sh, sl))
        den_w.append(rows_cat(th, tl))
        back_w.append(lanes_cat(sh, sh, sl))

    GU = 8

    def glob_block(i, carry):
        r = block(i, GU * NODES)
        keep = [(1 - period[i * GU + u]).astype(F32) for u in range(GU)]
        sums, tots = carry
        new_sums, new_tots = [], []
        for p in range(PAIRS):
            ls = lanes[p]
            qp = q_sig[r, ls]
            qpb = qp.astype(BF)
            num = nn(qpb, num_w[p])
            den = nt(qpb, den_w[p])
            inv = 1.0 / (den[:, 0:128] + den[:, 128:256])
            glob = (num[:, 0:128] + num[:, 128:256]) * inv
            at = att[r, ls] + glob
            mix[r, ls] = ((1.0 - BETA) * g[r, ls] * at + BETA * at).astype(BF)
            low4[GATE, r, ls] = (dmix[r, ls] * (1.0 - BETA) * at).astype(BF)
            da = datt[r, ls]
            dnum = rows_cat(*[keep[u] * da[u * NODES : (u + 1) * NODES] for u in range(GU)]) * inv
            dh, dl = split(dnum)
            th, tl = split(dnum * glob)
            dden = -nn(lanes_cat(th, tl), rows_cat(ones_bd, ones_bd))
            dqp = nt(lanes_cat(dh, dl, dh), back_w[p]) + dden * totals[p]
            dq[r, ls] = dqp * qp * (1.0 - qp)
            new_sums.append(sums[p] + tn(qpb, dh))
            new_tots.append(tots[p] + jnp.sum(dden * qp, axis=0, keepdims=True))
        return tuple(new_sums), tuple(new_tots)

    carry = lax.fori_loop(0, NB // GU, glob_block, zero_sums())
    pack_sums(1, carry)
    ar_scatter(1)
    send(mix, mixo, mix_sems.at[0], mix_sems.at[1], partner)

    KB = 1024

    def weight_grads(kinds):
        def step(i, _):
            r = block(i, KB)
            n = normed[r, :]
            for kind in kinds:
                got = tn(n, low4[kind, r, :])
                part[kind, own_rows, :] += got[0:W]
                part[kind, oth_rows, :] += got[W : 2 * W]
            return 0

        for kind in kinds:
            part[kind] = jnp.zeros(part.shape[1:], F32)
        lax.fori_loop(0, R // KB, step, 0)

    def out_grads():
        def step(i, _):
            r = block(i, KB)
            cc = c[r, :]
            part[OUT, own_rows, :] += tn(mix[r, :], cc)
            part[OUT, oth_rows, :] += tn(mixo[r, :], cc)
            return 0

        part[OUT] = jnp.zeros(part.shape[1:], F32)
        lax.fori_loop(0, R // KB, step, 0)

    D = 2 * W
    PA = D // A
    PB = PA // B

    B_FIRST = (QUERY,) if A == B else ()

    def order(w):
        first, second = (al, a_peers), (bl, b_peers)
        return (second, first) if w in B_FIRST else (first, second)

    def w_scatter(w):
        psend[w] = part[w].astype(BF)
        for i, (j, to) in enumerate(order(w)[0][1]):
            send(
                psend.at[w, block(j, PA)],
                precv.at[w, i],
                w_sems.at[0, w, 0],
                w_sems.at[1, w, 0],
                to,
            )

    def w_middle(w):
        (mine, _), (_, peers) = order(w)
        wait_both(precv.at[w], w_sems, (w, 0))
        total = part[w, block(mine, PA), :]
        for i in range(A - 1):
            total = total + precv[w, i].astype(F32)
        zpart[w] = total
        for i, (j, to) in enumerate(peers):
            send(
                zpart.at[w, block(j, PB)],
                zrecv.at[w, i],
                w_sems.at[0, w, 1],
                w_sems.at[1, w, 1],
                to,
            )

    def share(w):
        (first, _), (second, _) = order(w)
        return pl.ds(pl.multiple_of(first * PA + second * PB, PB), PB)

    def w_spread(w):
        _, (mine, peers) = order(w)
        wait_both(zrecv.at[w], w_sems, (w, 1))
        total = zpart[w, block(mine, PB), :]
        for i in range(B - 1):
            total = total + zrecv[w, i]
        if C > 1:
            zpart[w, block(mine, PB), :] = total
            for i, (_, to) in enumerate(h_peers):
                send(
                    zpart.at[w, block(mine, PB)],
                    hrecv.at[w, i],
                    wh_sems.at[0, w],
                    wh_sems.at[1, w],
                    to,
                )
            wait_both(hrecv.at[w], wh_sems, (w,))
            for i in range(C - 1):
                total = total + hrecv[w, i]
        fin[w, share(w), :] = total.astype(BF)
        for _, to in peers:
            send(
                fin.at[w, share(w)],
                fin.at[w, share(w)],
                w_sems.at[0, w, 2],
                w_sems.at[1, w, 2],
                to,
            )

    def w_gather(w):
        mine, peers = order(w)[0]
        wait_both(fin.at[w, pl.ds(0, (B - 1) * PB)], w_sems, (w, 2))
        for _, to in peers:
            send(
                fin.at[w, block(mine, PA)],
                fin.at[w, block(mine, PA)],
                w_sems.at[0, w, 3],
                w_sems.at[1, w, 3],
                to,
            )

    def w_keep(w):
        wait_both(fin.at[w, pl.ds(0, (A - 1) * PA)], w_sems, (w, 3))
        store(fin.at[w], fin_hbm.at[w])

    weight_grads((GATE,))
    w_scatter(GATE)
    bytes_of(mixo, mix_sems.at[1])
    out_grads()
    w_scatter(OUT)

    BU = 4

    def backward_block(i, _):
        @pl.when(i == 1)
        def _():
            ar_middle(1)

        @pl.when(i == 2)
        def _():
            w_middle(GATE)

        @pl.when(i == 3)
        def _():
            ar_gather(1)

        chains = [(block(i * BU + u, NODES), i * BU + u, p) for u in range(BU) for p in range(PAIRS)]
        outs, dps = [], []
        for r, s, p in chains:
            ls = lanes[p]
            oh, ol = split(datt[r, ls])
            oh, ol = apart(oh), apart(ol)
            outs.append((oh, ol))
            high = vh[r, ls]
            dps.append(nt(lanes_cat(high, vl[r, ls], high), lanes_cat(oh, oh, ol)))
        dss = []
        for (r, s, p), dp in zip(chains, dps):
            pr = prob[s, p, 0].astype(F32) + prob[s, p, 1].astype(F32)
            dss.append(split(pr * (dp - jnp.sum(pr * dp, axis=0, keepdims=True))))
        for (r, s, p), (oh, ol) in zip(chains, outs):
            got = nn(prob[s, p, 0], lanes_cat(oh, ol))
            dv[r, lanes[p]] = got[:, 0:128] + got[:, 128:256] + nn(prob[s, p, 1], oh)
        for (r, s, p), (high, low) in zip(chains, dss):
            ls = lanes[p]
            qbh = apart(qh[r, ls])
            got = nn(high, lanes_cat(qbh, apart(ql[r, ls])))
            dk[r, ls] = (got[:, 0:128] + got[:, 128:256] + nn(low, qbh)) * (1.0 / LOG2E)
        for (r, s, p), (high, low) in zip(chains, dss):
            ls = lanes[p]
            khigh = kh[r, ls]
            got = tn(
                rows_cat(high, low),
                rows_cat(lanes_cat(khigh, kl[r, ls]), lanes_cat(khigh, jnp.zeros_like(khigh))),
            )
            got = joined(got[:, 0:128] + got[:, 128:256]) * 0.125
            low4[QUERY, r, ls] = (dq[r, ls] + got).astype(BF)
        return 0

    lax.fori_loop(0, NB // BU, backward_block, 0)
    w_middle(OUT)
    weight_grads((QUERY,))
    w_scatter(QUERY)
    w_spread(GATE)

    mats, totals = ar_result(1)
    dsum = [m.astype(BF) for m in mats]

    KU = 8

    def key_block(i, _):
        r = block(i, KU * NODES)
        for p in range(PAIRS):
            ls = lanes[p]
            sig = k_sig[r, ls]
            kp = live_rows(i * KU, sig, KU)
            dkp = nt(vh[r, ls], dsum[p]) + totals[p]
            low4[KEY, r, ls] = (dk[r, ls] + dkp * kp * (1.0 - sig)).astype(BF)
            low4[VALUE, r, ls] = (dv[r, ls] + nn(kp.astype(BF), dsum[p])).astype(BF)
        return 0

    lax.fori_loop(0, NB // KU, key_block, 0)
    weight_grads((KEY,))
    w_scatter(KEY)
    weight_grads((VALUE,))
    w_scatter(VALUE)
    w_spread(OUT)

    DC = NR

    def normed_block(b, _):
        r = block(b, RB)
        grads = lanes_cat(*[low4[kind, r, :] for kind in (QUERY, KEY, VALUE, GATE)])
        dn = nt(grads, wall[...])
        dn_own[r, :] = dn[:, 0:W]
        dn_send[r, :] = dn[:, W : 2 * W]
        mean = mean_keep[r, 0:1]
        rstd = rstd_keep[r, 0:1]
        sa = dn[:, 0:W] * gain_own
        sb = dn[:, W : 2 * W] * gain_oth
        ha = (x[r, :].astype(F32) - mean) * rstd
        hb = (xo[r, :].astype(F32) - mean) * rstd
        s1 = jnp.sum(sa, axis=1, keepdims=True) + jnp.sum(sb, axis=1, keepdims=True)
        s2 = jnp.sum(sa * ha, axis=1, keepdims=True) + jnp.sum(sb * hb, axis=1, keepdims=True)
        st_send[r, :] = jnp.where(lane_half, s1, s2)

        @pl.when(lax.rem(b, NR // DC) == NR // DC - 1)
        def _():
            i = b // (NR // DC)
            piece = block(i, R // DC)
            send(dn_send.at[piece], dn_recv.at[piece], dn_sems.at[0, 0], dn_sems.at[0, 2 + i], partner)
            send(st_send.at[piece], st_recv.at[piece], dn_sems.at[0, 1], dn_sems.at[1, 2 + i], partner)

        return 0

    lax.fori_loop(0, NR, normed_block, 0)
    w_middle(KEY)
    w_middle(QUERY)

    def out_block(b, _):
        r = block(b, RB)
        got = nn(mix[r, :], wo[own_rows, :]) + nn(mixo[r, :], wo[oth_rows, :])
        mixo[r, :] = (x[r, :].astype(F32) + got).astype(BF)
        return 0

    lax.fori_loop(0, NR, out_block, 0)
    store(mixo, layer_out)
    w_middle(VALUE)
    w_gather(GATE)
    w_gather(OUT)
    w_spread(KEY)
    w_spread(QUERY)

    def input_block(b, carry):
        @pl.when(lax.rem(b, NR // DC) == 0)
        def _():
            i = b // (NR // DC)
            piece = block(i, R // DC)
            bytes_of(dn_recv.at[piece], dn_sems.at[0, 2 + i])
            bytes_of(st_recv.at[piece], dn_sems.at[1, 2 + i])

        gain_sum, bias_sum = carry
        r = block(b, RB)
        dn = dn_own[r, :] + dn_recv[r, :]
        st = st_send[r, :] + st_recv[r, :]
        mean = mean_keep[r, 0:1]
        rstd = rstd_keep[r, 0:1]
        s1 = st[:, 0:1] * (1.0 / (2 * W))
        s2 = st[:, 64:65] * (1.0 / (2 * W))
        ha = (x[r, :].astype(F32) - mean) * rstd
        inner = rstd * (dn * gain_own - s1 - ha * s2)
        co[r, :] = (c[r, :].astype(F32) + inner).astype(BF)
        return (
            gain_sum + jnp.sum(dn * ha, axis=0, keepdims=True),
            bias_sum + jnp.sum(dn, axis=0, keepdims=True),
        )

    carry = (jnp.zeros((1, W), F32), jnp.zeros((1, W), F32))
    carry = lax.fori_loop(0, NR, input_block, carry)
    store(co, input_grad)
    w_spread(VALUE)
    w_gather(KEY)

    row = lax.broadcasted_iota(jnp.int32, (8, W), 0)
    total = jnp.where(row == 0, carry[0], jnp.where(row == 1, carry[1], 0.0))

    def in_order(total, step, held, index, count, peers):
        gb_part[step] = total
        held[pl.ds(index, 1)] = total[None]
        for _, to in peers:
            send(gb_part.at[step], held.at[index], gb_sems.at[0, step], gb_sems.at[1, step], to)
        return count

    def added(step, held, count):
        wait_both(held.at[pl.ds(0, count - 1)], gb_sems, (step,))
        total = held[0]
        for i in range(1, count):
            total = total + held[i]
        return total

    in_order(total, 0, gb_recv, al, A, a_peers)
    w_gather(VALUE)
    w_gather(QUERY)
    in_order(added(0, gb_recv, A), 1, gb_z, bl, B, b_peers)
    w_keep(GATE)
    w_keep(OUT)
    w_keep(QUERY)
    total = added(1, gb_z, B)
    if C > 1:
        in_order(total, 2, gb_hi, hi, C, h_peers)
        total = added(2, gb_hi, C)
    gain_out[...] = total[0:1].reshape(W)
    bias_out[...] = total[1:2].reshape(W)
    store(gain_out, gain_grad)
    store(bias_out, bias_grad)
    w_keep(KEY)
    w_keep(VALUE)
    for cp in stores:
        cp.wait()
    bytes_of(gbs, core_sems.at[0, 0])
    bytes_of(woo, core_sems.at[0, 1])
    bytes_of(c, core_sems.at[0, 2])
    bytes_of(x, core_sems.at[0, 3])
    bytes_of(mix, mix_sems.at[0])
    bytes_of(dn_send, dn_sems.at[0, 0])
    bytes_of(st_send, dn_sems.at[0, 1])


def shards(
    groups,
    node_input,
    cotangent,
    norm_gain,
    norm_bias,
    query_weight,
    key_weight,
    value_weight,
    gate_weight,
    out_weight,
    adjacent_vertices,
    active_vertex_tally,
    training_period,
):
    A, B, C = groups
    R, W = node_input.shape
    D = 2 * W
    NB = R // NODES
    PAIRS = W // 128
    SR = 64 * PAIRS // A + 8
    PA = D // A
    PB = PA // B
    VM = pltpu.VMEM
    dma = pltpu.SemaphoreType.DMA
    hbm = pl.BlockSpec(memory_space=pl.ANY)
    layer_output, input_grad, gain_grad, bias_grad, fin = pl.pallas_call(
        functools.partial(layer_kernel, groups),
        name="layer_kernel",
        out_shape=(
            jax.ShapeDtypeStruct((R, W), BF),
            jax.ShapeDtypeStruct((R, W), BF),
            jax.ShapeDtypeStruct((W,), F32),
            jax.ShapeDtypeStruct((W,), F32),
            jax.ShapeDtypeStruct((5, D, W), BF),
        ),
        in_specs=[hbm] * 12,
        out_specs=(hbm,) * 5,
        scratch_shapes=[
            VM((W,), BF),
            VM((W,), BF),
            VM((W,), F32),
            VM((W,), F32),
            pltpu.SMEM((NB,), jnp.int32),
            pltpu.SMEM((NB,), jnp.int32),
            VM((R, W), BF),
            VM((R, W), BF),
            VM((R, W), BF),
            VM((R, W), BF),
            VM((D, W), BF),
            VM((adjacent_vertices.shape[1], R), jnp.int32),
            VM((NB, NODES, NODES), F32),
            VM((5, D, W), BF),
            VM((16, W), F32),
            VM((16, W), F32),
            VM((W, W), BF),
            VM((D, 4 * W), BF),
            VM((R, D), BF),
            VM((R, 128), F32),
            VM((R, 128), F32),
            VM((R, W), F32),
            VM((R, W), F32),
            VM((R, W), BF),
            VM((R, W), BF),
            VM((R, W), BF),
            VM((R, W), BF),
            VM((R, W), BF),
            VM((R, W), BF),
            VM((R, W), F32),
            VM((R, W), F32),
            VM((R, W), F32),
            VM((R, W), F32),
            VM((NB, PAIRS, 2, NODES, 2 * NODES), BF),
            VM((R, W), F32),
            VM((4, R, W), BF),
            VM((R, W), BF),
            VM((R, W), BF),
            VM((R, W), F32),
            VM((R, 128), F32),
            VM((R, 128), F32),
            VM((2, A, SR, 128), F32),
            VM((2, A - 1, SR, 128), F32),
            VM((2, SR, 128), F32),
            VM((2, B - 1, SR, 128), F32),
            VM((2, max(C - 1, 1), SR, 128), F32),
            VM((2, A, SR, 128), F32),
            VM((5, D, W), F32),
            VM((5, D, W), BF),
            VM((5, A - 1, PA, W), BF),
            VM((5, PA, W), F32),
            VM((5, B - 1, PB, W), F32),
            VM((5, max(C - 1, 1), PB, W), F32),
            VM((3, 8, W), F32),
            VM((A, 8, W), F32),
            VM((B, 8, W), F32),
            VM((C, 8, W), F32),
            dma((20,)),
            dma((10,)),
            dma((2, 7)),
            dma((2,)),
            dma((2, 6)),
            dma((2, 2, 3)),
            dma((2, 2)),
            dma((2, 5, 4)),
            dma((2, 5)),
            dma((2, 3)),
        ],
        compiler_params=pltpu.CompilerParams(
            collective_id=0, has_side_effects=True, vmem_limit_bytes=63 << 20
        ),
    )(
        node_input,
        cotangent,
        norm_gain,
        norm_bias,
        query_weight,
        key_weight,
        value_weight,
        gate_weight,
        out_weight,
        adjacent_vertices.T,
        active_vertex_tally,
        training_period,
    )
    return pl.pallas_call(
        finish_kernel,
        name="finish_kernel",
        out_shape=(
            jax.ShapeDtypeStruct((R, W), BF),
            jax.ShapeDtypeStruct((R, W), BF),
            jax.ShapeDtypeStruct((W,), F32),
            jax.ShapeDtypeStruct((W,), F32),
        )
        + tuple(jax.ShapeDtypeStruct((D, W), F32) for _ in range(5)),
        in_specs=[hbm] * 5,
        out_specs=(hbm,) * 9,
        scratch_shapes=[
            VM((5, D, W), BF),
            VM((5, D, W), F32),
            VM((2, R, W), BF),
            VM((W,), F32),
            VM((W,), F32),
            dma((18,)),
        ],
    )(layer_output, input_grad, gain_grad, bias_grad, fin)


def finish_kernel(
    lo_in, ig_in, gain_in, bias_in, fin, lo, ig, gain, bias, gq, gk, gv, gg, go, *scratch
):
    low, full, wide, gain_here, bias_here, sems = scratch
    loads, stores = [], []

    def begin(src, dst, into):
        copy = pltpu.make_async_copy(src, dst, sems.at[len(into) + (0 if into is loads else 9)])
        copy.start()
        into.append(copy)

    for i in range(5):
        begin(fin.at[i], low.at[i], loads)
    straight = (
        (lo_in, wide.at[0], lo),
        (ig_in, wide.at[1], ig),
        (gain_in, gain_here, gain),
        (bias_in, bias_here, bias),
    )
    for src, here, _ in straight:
        begin(src, here, loads)
    for i, out in enumerate((gq, gk, gv, gg, go)):
        loads[i].wait()
        full[i] = low[i].astype(F32)
        begin(full.at[i], out, stores)
    for i, (_, here, out) in enumerate(straight):
        loads[5 + i].wait()
        begin(here, out, stores)
    for cp in stores:
        cp.wait()


def factors(count):
    a = 4 if count % 4 == 0 else count
    b = 4 if count % (a * 4) == 0 else count // a
    return a, b, count // (a * b)


def solution(mesh):
    rows = P("graph", "head")
    cols = P(None, "head")
    return jax.shard_map(
        functools.partial(shards, factors(mesh.shape["graph"])),
        mesh=mesh,
        in_specs=(rows, rows, P("head"), P("head"))
        + (cols,) * 5
        + (P("graph", None), P("graph"), P("graph")),
        out_specs=(rows, rows, P("head"), P("head")) + (cols,) * 5,
        check_vma=False,
    )
```

```python
import functools

import jax
import jax.numpy as jnp
from jax import lax
from jax.experimental import pallas as pl
from jax.experimental.pallas import tpu as pltpu
from jax.sharding import PartitionSpec as P

EPS = 1e-05
BETA = 0.9
LOG2E = 1.4426950408889634
BF = jnp.bfloat16
F32 = jnp.float32
MESH = pl.DeviceIdType.MESH
NODES = 128
QUERY, KEY, VALUE, GATE, OUT = 0, 1, 2, 3, 4


def nn(a, b):
    return lax.dot_general(a, b, (((1,), (0,)), ((), ())), preferred_element_type=F32)


def nt(a, b):
    return lax.dot_general(a, b, (((1,), (1,)), ((), ())), preferred_element_type=F32)


def tn(a, b):
    return lax.dot_general(a, b, (((0,), (0,)), ((), ())), preferred_element_type=F32)


def split(a):
    high = a.astype(BF)
    return high, (a - high.astype(F32)).astype(BF)


def rows_cat(*parts):
    return jnp.concatenate(parts, axis=0)


def lanes_cat(*parts):
    return jnp.concatenate(parts, axis=1)


def block(start, size):
    return pl.ds(pl.multiple_of(start * size, size), size)


def layer_kernel(
    groups,
    x_hbm,
    c_hbm,
    gain_hbm,
    bias_hbm,
    wq,
    wk,
    wv,
    wg,
    wo_hbm,
    adjacent_hbm,
    tally_hbm,
    period_hbm,
    layer_out,
    input_grad,
    gain_grad,
    bias_grad,
    fin_hbm,
    gain,
    bias,
    gain_out,
    bias_out,
    tally,
    period,
    x,
    xo,
    c,
    co,
    wo,
    adjacent,
    weight,
    fin,
    gbs,
    gbo,
    woo,
    wall,
    normed,
    mean_keep,
    rstd_keep,
    q_sig,
    k_sig,
    qh,
    ql,
    kh,
    kl,
    vh,
    vl,
    g,
    dmix,
    datt,
    att,
    prob,
    dq,
    dv,
    low4,
    mix,
    mixo,
    dn_recv,
    st_send,
    st_recv,
    sum_part,
    sum_recv,
    sum_mid,
    sum_z,
    sum_hi,
    sum_full,
    part,
    psend,
    precv,
    zpart,
    zrecv,
    hrecv,
    gb_part,
    gb_recv,
    gb_z,
    gb_hi,
    load_sems,
    store_sems,
    core_sems,
    mix_sems,
    dn_sems,
    ar_sems,
    arh_sems,
    w_sems,
    wh_sems,
    gb_sems,
):
    A, B, C = groups
    L = A * B
    R, W = x.shape
    NB = R // NODES
    PAIRS = W // 128
    me = lax.axis_index("graph")
    head = lax.axis_index("head")
    other = 1 - head
    lo = lax.rem(me, L)
    hi = me // L
    al = lax.rem(lo, A)
    bl = lo // A

    def dev(h_, b_, a_):
        return (h_ * L + b_ * A + a_, head)

    a_peers = [(lax.rem(al + d, A), dev(hi, bl, lax.rem(al + d, A))) for d in range(1, A)]
    b_peers = [(lax.rem(bl + d, B), dev(hi, lax.rem(bl + d, B), al)) for d in range(1, B)]
    h_peers = [(lax.rem(hi + d, C), dev(lax.rem(hi + d, C), bl, al)) for d in range(1, C)]
    partner = (me, other)
    own_rows = block(head, W)
    oth_rows = block(other, W)

    def send(src, dst, send_sem, recv_sem, to):
        pltpu.make_async_remote_copy(
            src_ref=src,
            dst_ref=dst,
            send_sem=send_sem,
            recv_sem=recv_sem,
            device_id=to,
            device_id_type=MESH,
        ).start()

    def bytes_of(ref, sem):
        pltpu.make_async_copy(ref, ref, sem).wait()

    def wait_both(ref, sems, index):
        bytes_of(ref, sems.at[(0,) + index])
        bytes_of(ref, sems.at[(1,) + index])

    dk, dn_own, dn_send = att, g, dmix

    barrier = pltpu.get_barrier_semaphore()
    greeted = [partner] + [to for _, to in a_peers + b_peers + h_peers]
    for to in greeted:
        pl.semaphore_signal(barrier, inc=1, device_id=to, device_id_type=MESH)

    loads = []

    def load(src, dst):
        copy = pltpu.make_async_copy(src, dst, load_sems.at[len(loads)])
        copy.start()
        loads.append(copy)
        return copy

    RB = 1024
    NR = R // RB
    XC = NR
    adjacent_load = load(adjacent_hbm, adjacent)
    x_loads = []
    for i in range(XC):
        piece = pl.ds(i * (R // XC), R // XC)
        x_loads.append(load(x_hbm.at[piece], x.at[piece]))
    wo_load = load(wo_hbm, wo)
    c_load = load(c_hbm, c)
    w_loads = []
    for i, w in ((1, wk), (2, wv), (0, wq), (3, wg)):
        cols = pl.ds(i * W, W)
        w_loads.append(load(w.at[own_rows], wall.at[pl.ds(0, W), cols]))
        w_loads.append(load(w.at[oth_rows], wall.at[pl.ds(W, W), cols]))

    stores = []

    def store(src, dst):
        copy = pltpu.make_async_copy(src, dst, store_sems.at[len(stores)])
        copy.start()
        stores.append(copy)

    small_loads = [
        load(gain_hbm, gain),
        load(bias_hbm, bias),
        load(tally_hbm, tally),
        load(period_hbm, period),
    ]
    for cp in small_loads:
        cp.wait()
    gbs[0:8, :] = jnp.broadcast_to(gain[...].astype(F32).reshape(1, W), (8, W))
    gbs[8:16, :] = jnp.broadcast_to(bias[...].astype(F32).reshape(1, W), (8, W))
    node_of = lax.broadcasted_iota(jnp.int32, (NODES, 128), 0)
    def count_block(i, _):
        node = node_of.astype(F32).astype(BF)
        one = jnp.ones((NODES, NODES), BF)
        zero = jnp.zeros((NODES, NODES), BF)
        for s in (2 * i, 2 * i + 1):
            listed = adjacent[:, block(s, NODES)].astype(F32).astype(BF)
            count = zero
            for j in range(listed.shape[0]):
                same = jnp.broadcast_to(listed[j : j + 1, :], (NODES, NODES)) == node
                count = count + jnp.where(same, one, zero)
            count = count.astype(F32)
            weight[s] = jnp.where(
                count > 0.0, jnp.log(jnp.maximum(count, 1.0)) * LOG2E, -1e30
            )
        return 0

    pl.semaphore_wait(barrier, len(greeted))

    send(gbs, gbo, core_sems.at[0, 0], core_sems.at[1, 0], partner)
    pieces = [pl.ds(i * (R // XC), R // XC) for i in range(XC)]
    for i, piece in enumerate(pieces):
        x_loads[i].wait()
        send(x.at[piece], xo.at[piece], core_sems.at[0, 3], core_sems.at[1, 3 + i], partner)
    wo_load.wait()
    send(wo.at[oth_rows], woo, core_sems.at[0, 1], core_sems.at[1, 1], partner)
    c_load.wait()
    send(c, co, core_sems.at[0, 2], core_sems.at[1, 2], partner)

    adjacent_load.wait()
    lax.fori_loop(0, NB // 2, count_block, 0)

    sum_part[...] = jnp.zeros_like(sum_part)
    bytes_of(gbo, core_sems.at[1, 0])
    gain_own, bias_own = gbs[0:1, :], gbs[8:9, :]
    gain_oth, bias_oth = gbo[0:1, :], gbo[8:9, :]
    lane_half = lax.broadcasted_iota(jnp.int32, (1, 128), 1) < 64

    def live_rows(first, a, count):
        node = lax.broadcasted_iota(jnp.int32, (NODES, a.shape[1]), 0)
        return rows_cat(
            *[
                jnp.where(node < tally[first + i], a[i * NODES : (i + 1) * NODES], 0.0)
                for i in range(count)
            ]
        )

    def norm_block(b, carry):
        @pl.when(lax.rem(b, NR // XC) == 0)
        def _():
            i = b // (NR // XC)
            bytes_of(xo.at[block(i, R // XC)], core_sems.at[1, 3 + i])

        r = block(b, RB)
        xa = x[r, :].astype(F32)
        xb = xo[r, :].astype(F32)
        mean = (
            jnp.sum(xa, axis=1, keepdims=True) + jnp.sum(xb, axis=1, keepdims=True)
        ) * (1.0 / (2 * W))
        xa = xa - mean
        xb = xb - mean
        var = (
            jnp.sum(xa * xa, axis=1, keepdims=True) + jnp.sum(xb * xb, axis=1, keepdims=True)
        ) * (1.0 / (2 * W))
        rstd = lax.rsqrt(var + EPS)
        mean_keep[r, :] = jnp.broadcast_to(mean, (RB, 128))
        rstd_keep[r, :] = jnp.broadcast_to(rstd, (RB, 128))
        na = (xa * rstd * gain_own + bias_own).astype(BF)
        nb = (xb * rstd * gain_oth + bias_oth).astype(BF)
        normed[r, 0:W] = na
        normed[r, W : 2 * W] = nb
        kv = nn(lanes_cat(na, nb), wall[:, W : 3 * W])
        kk = kv[:, 0:W]
        vv = kv[:, W : 2 * W]
        kh[r, :], kl[r, :] = split(kk)
        vbf, vlow = split(vv)
        vh[r, :] = vbf
        vl[r, :] = vlow
        sig = jax.nn.sigmoid(kk)
        k_sig[r, :] = sig
        kp = live_rows(b * (RB // NODES), sig, RB // NODES)
        kpb = kp.astype(BF)
        sums, totals = carry
        new_sums, new_totals = [], []
        for p in range(PAIRS):
            ls = slice(p * 128, (p + 1) * 128)
            new_sums.append(sums[p] + tn(kpb[:, ls], vbf[:, ls]))
            new_totals.append(totals[p] + jnp.sum(kp[:, ls], axis=0, keepdims=True))
        return tuple(new_sums), tuple(new_totals)

    def zero_sums():
        return (
            tuple(jnp.zeros((128, 128), F32) for _ in range(PAIRS)),
            tuple(jnp.zeros((1, 128), F32) for _ in range(PAIRS)),
        )

    for cp in w_loads[0:4]:
        cp.wait()
    carry = lax.fori_loop(0, NR, norm_block, zero_sums())

    def pack_sums(slot, carry):
        sums, totals = carry
        packed = rows_cat(
            *[jnp.where(lane_half, sums[p][0:64], sums[p][64:128]) for p in range(PAIRS)]
        )
        for j in range(A):
            sum_part[slot, j, 0:SR, :] = packed[j * SR : (j + 1) * SR]
            for p in range(PAIRS):
                sum_part[slot, j, SR + p : SR + p + 1, :] = totals[p]

    SR = 64 * PAIRS // A

    def ar_scatter(slot):
        for i, (j, to) in enumerate(a_peers):
            send(
                sum_part.at[slot, j],
                sum_recv.at[slot, i],
                ar_sems.at[0, slot, 0],
                ar_sems.at[1, slot, 0],
                to,
            )

    def ar_middle(slot):
        wait_both(sum_recv.at[slot], ar_sems, (slot, 0))
        total = sum_part[slot, al]
        for i in range(A - 1):
            total = total + sum_recv[slot, i]
        sum_mid[slot] = total
        for i, (_, to) in enumerate(b_peers):
            send(
                sum_mid.at[slot],
                sum_z.at[slot, i],
                ar_sems.at[0, slot, 1],
                ar_sems.at[1, slot, 1],
                to,
            )

    def ar_gather(slot):
        wait_both(sum_z.at[slot], ar_sems, (slot, 1))
        total = sum_mid[slot]
        for i in range(B - 1):
            total = total + sum_z[slot, i]
        if C > 1:
            sum_mid[slot] = total
            for i, (_, to) in enumerate(h_peers):
                send(
                    sum_mid.at[slot],
                    sum_hi.at[slot, i],
                    arh_sems.at[0, slot],
                    arh_sems.at[1, slot],
                    to,
                )
            wait_both(sum_hi.at[slot], arh_sems, (slot,))
            for i in range(C - 1):
                total = total + sum_hi[slot, i]
        sum_full[slot, al] = total
        for i, (_, to) in enumerate(a_peers):
            send(
                sum_full.at[slot, al],
                sum_full.at[slot, al],
                ar_sems.at[0, slot, 2],
                ar_sems.at[1, slot, 2],
                to,
            )

    def ar_result(slot):
        wait_both(sum_recv.at[slot], ar_sems, (slot, 2))
        mats, totals = [], []
        packed = rows_cat(*[sum_full[slot, j, 0:SR, :] for j in range(A)])
        for p in range(PAIRS):
            own = packed[p * 64 : (p + 1) * 64]
            mats.append(rows_cat(jnp.where(lane_half, own, 0.0), jnp.where(lane_half, 0.0, own)))
            totals.append(sum_full[slot, 0, SR + p : SR + p + 1, :])
        return mats, totals

    pack_sums(0, carry)
    ar_scatter(0)

    for cp in w_loads[4:]:
        cp.wait()
    bytes_of(woo, core_sems.at[1, 1])
    bytes_of(co, core_sems.at[1, 2])

    def gate_block(b, _):
        r = block(b, RB)
        n = normed[r, :]
        qq = nn(n, wall[:, 0:W])
        q_sig[r, :] = jax.nn.sigmoid(qq)
        qh[r, :], ql[r, :] = split(qq * (0.125 * LOG2E))
        gg = nn(n, wall[:, 3 * W : 4 * W])
        g[r, :] = gg
        dm = nt(lanes_cat(c[r, :], co[r, :]), lanes_cat(wo[own_rows, :], woo[...]))
        dmix[r, :] = dm
        datt[r, :] = dm * ((1.0 - BETA) * gg + BETA)
        return 0

    lax.fori_loop(0, NR, gate_block, 0)
    ar_middle(0)

    half_row = jnp.where(lane_half, 1.0, 0.0)
    half_a = jnp.broadcast_to(half_row, (NODES, 128)).astype(BF)
    half_b = jnp.broadcast_to(1.0 - half_row, (NODES, 128)).astype(BF)

    def apart(a):
        return rows_cat(a * half_a, a * half_b)

    def joined(a):
        return jnp.where(lane_half, a[0:NODES], a[NODES : 2 * NODES])

    FU = 4
    lanes = [slice(p * 128, (p + 1) * 128) for p in range(PAIRS)]

    def forward_block(i, _):
        @pl.when(i == 3)
        def _():
            ar_gather(0)

        chains = [(i * FU + u, p) for u in range(FU) for p in range(PAIRS)]
        scores = []
        for s, p in chains:
            r, ls = block(s, NODES), lanes[p]
            high, low = kh[r, ls], kl[r, ls]
            qbh = apart(qh[r, ls])
            scores.append(
                nt(lanes_cat(high, low, high), lanes_cat(qbh, qbh, apart(ql[r, ls])))
            )
        probs = []
        for j, score in enumerate(scores):
            bias = weight[chains[j][0]]
            score = score + lanes_cat(bias, bias)
            e = jnp.exp2(score - jnp.max(score, axis=0, keepdims=True))
            probs.append(split(e * (1.0 / jnp.sum(e, axis=0, keepdims=True))))
        for (s, p), (high, low) in zip(chains, probs):
            prob[s, p, 0] = high
            prob[s, p, 1] = low
        for (s, p), (high, low) in zip(chains, probs):
            r, ls = block(s, NODES), lanes[p]
            vhigh = vh[r, ls]
            o = tn(
                rows_cat(high, low),
                rows_cat(lanes_cat(vhigh, vl[r, ls]), lanes_cat(vhigh, jnp.zeros_like(vhigh))),
            )
            att[r, ls] = joined(o[:, 0:128] + o[:, 128:256])
        return 0

    lax.fori_loop(0, NB // FU, forward_block, 0)

    def value_block(i, _):
        chains = [(i * BU + u, p) for u in range(BU) for p in range(PAIRS)]
        outs = []
        for s, p in chains:
            oh, ol = split(datt[block(s, NODES), lanes[p]])
            outs.append((apart(oh), apart(ol)))
        for (s, p), (oh, ol) in zip(chains, outs):
            got = nn(prob[s, p, 0], lanes_cat(oh, ol))
            got = got[:, 0:128] + got[:, 128:256] + nn(prob[s, p, 1], oh)
            dv[block(s, NODES), lanes[p]] = got
        return 0

    BU = 4
    lax.fori_loop(0, NB // BU, value_block, 0)

    mats, totals = ar_result(0)
    square = (2, 128, 128)
    same_head = (lax.broadcasted_iota(jnp.int32, (128, 128), 0) < 64) == (
        lax.broadcasted_iota(jnp.int32, (128, 128), 1) < 64
    )
    ones_bd = jnp.where(same_head, 1.0, 0.0).astype(BF)
    num_w, den_w, back_w = [], [], []
    for p in range(PAIRS):
        sh, sl = split(mats[p])
        th, tl = split(jnp.where(same_head, jnp.broadcast_to(totals[p], (128, 128)), 0.0))
        num_w.append(lanes_cat(sh, sl))
        den_w.append(rows_cat(th, tl))
        back_w.append(lanes_cat(sh, sh, sl))

    GU = 8

    def glob_block(i, carry):
        r = block(i, GU * NODES)
        keep = [(1 - period[i * GU + u]).astype(F32) for u in range(GU)]
        sums, tots = carry
        new_sums, new_tots = [], []
        for p in range(PAIRS):
            ls = lanes[p]
            qp = q_sig[r, ls]
            qpb = qp.astype(BF)
            num = nn(qpb, num_w[p])
            den = nt(qpb, den_w[p])
            inv = 1.0 / (den[:, 0:128] + den[:, 128:256])
            glob = (num[:, 0:128] + num[:, 128:256]) * inv
            at = att[r, ls] + glob
            mix[r, ls] = ((1.0 - BETA) * g[r, ls] * at + BETA * at).astype(BF)
            low4[GATE, r, ls] = (dmix[r, ls] * (1.0 - BETA) * at).astype(BF)
            da = datt[r, ls]
            dnum = rows_cat(*[keep[u] * da[u * NODES : (u + 1) * NODES] for u in range(GU)]) * inv
            dh, dl = split(dnum)
            th, tl = split(dnum * glob)
            dden = -nn(lanes_cat(th, tl), rows_cat(ones_bd, ones_bd))
            dqp = nt(lanes_cat(dh, dl, dh), back_w[p]) + dden * totals[p]
            dq[r, ls] = dqp * qp * (1.0 - qp)
            new_sums.append(sums[p] + tn(qpb, dh))
            new_tots.append(tots[p] + jnp.sum(dden * qp, axis=0, keepdims=True))
        return tuple(new_sums), tuple(new_tots)

    carry = lax.fori_loop(0, NB // GU, glob_block, zero_sums())
    pack_sums(1, carry)
    ar_scatter(1)
    send(mix, mixo, mix_sems.at[0], mix_sems.at[1], partner)

    KB = 1024

    def weight_grads(kinds):
        def step(i, _):
            r = block(i, KB)
            n = normed[r, :]
            for kind in kinds:
                got = tn(n, low4[kind, r, :])
                part[kind, own_rows, :] += got[0:W]
                part[kind, oth_rows, :] += got[W : 2 * W]
            return 0

        for kind in kinds:
            part[kind] = jnp.zeros(part.shape[1:], F32)
        lax.fori_loop(0, R // KB, step, 0)

    def out_grads():
        def step(i, _):
            r = block(i, KB)
            cc = c[r, :]
            part[OUT, own_rows, :] += tn(mix[r, :], cc)
            part[OUT, oth_rows, :] += tn(mixo[r, :], cc)
            return 0

        part[OUT] = jnp.zeros(part.shape[1:], F32)
        lax.fori_loop(0, R // KB, step, 0)

    D = 2 * W
    PA = D // A
    PB = PA // B

    B_FIRST = (QUERY,) if A == B else ()

    def order(w):
        first, second = (al, a_peers), (bl, b_peers)
        return (second, first) if w in B_FIRST else (first, second)

    def w_scatter(w):
        psend[w] = part[w].astype(BF)
        for i, (j, to) in enumerate(order(w)[0][1]):
            send(
                psend.at[w, block(j, PA)],
                precv.at[w, i],
                w_sems.at[0, w, 0],
                w_sems.at[1, w, 0],
                to,
            )

    def w_middle(w):
        (mine, _), (_, peers) = order(w)
        wait_both(precv.at[w], w_sems, (w, 0))
        total = part[w, block(mine, PA), :]
        for i in range(A - 1):
            total = total + precv[w, i].astype(F32)
        zpart[w] = total
        for i, (j, to) in enumerate(peers):
            send(
                zpart.at[w, block(j, PB)],
                zrecv.at[w, i],
                w_sems.at[0, w, 1],
                w_sems.at[1, w, 1],
                to,
            )

    def share(w):
        (first, _), (second, _) = order(w)
        return pl.ds(pl.multiple_of(first * PA + second * PB, PB), PB)

    def w_spread(w):
        _, (mine, peers) = order(w)
        wait_both(zrecv.at[w], w_sems, (w, 1))
        total = zpart[w, block(mine, PB), :]
        for i in range(B - 1):
            total = total + zrecv[w, i]
        if C > 1:
            zpart[w, block(mine, PB), :] = total
            for i, (_, to) in enumerate(h_peers):
                send(
                    zpart.at[w, block(mine, PB)],
                    hrecv.at[w, i],
                    wh_sems.at[0, w],
                    wh_sems.at[1, w],
                    to,
                )
            wait_both(hrecv.at[w], wh_sems, (w,))
            for i in range(C - 1):
                total = total + hrecv[w, i]
        fin[w, share(w), :] = total.astype(BF)
        for _, to in peers:
            send(
                fin.at[w, share(w)],
                fin.at[w, share(w)],
                w_sems.at[0, w, 2],
                w_sems.at[1, w, 2],
                to,
            )

    def w_gather(w):
        mine, peers = order(w)[0]
        wait_both(fin.at[w, pl.ds(0, (B - 1) * PB)], w_sems, (w, 2))
        for _, to in peers:
            send(
                fin.at[w, block(mine, PA)],
                fin.at[w, block(mine, PA)],
                w_sems.at[0, w, 3],
                w_sems.at[1, w, 3],
                to,
            )

    def w_keep(w):
        wait_both(fin.at[w, pl.ds(0, (A - 1) * PA)], w_sems, (w, 3))
        store(fin.at[w], fin_hbm.at[w])

    weight_grads((GATE,))
    w_scatter(GATE)
    bytes_of(mixo, mix_sems.at[1])
    out_grads()
    w_scatter(OUT)

    def backward_block(i, _):
        @pl.when(i == 1)
        def _():
            ar_middle(1)

        @pl.when(i == 2)
        def _():
            w_middle(GATE)

        @pl.when(i == 3)
        def _():
            ar_gather(1)

        chains = [(block(i * BU + u, NODES), i * BU + u, p) for u in range(BU) for p in range(PAIRS)]
        dps = []
        for r, s, p in chains:
            ls = lanes[p]
            oh, ol = split(datt[r, ls])
            oh, ol = apart(oh), apart(ol)
            high = vh[r, ls]
            dps.append(nt(lanes_cat(high, vl[r, ls], high), lanes_cat(oh, oh, ol)))
        dss = []
        for (r, s, p), dp in zip(chains, dps):
            pr = prob[s, p, 0].astype(F32) + prob[s, p, 1].astype(F32)
            dss.append(split(pr * (dp - jnp.sum(pr * dp, axis=0, keepdims=True))))
        for (r, s, p), (high, low) in zip(chains, dss):
            ls = lanes[p]
            qbh = apart(qh[r, ls])
            got = nn(high, lanes_cat(qbh, apart(ql[r, ls])))
            dk[r, ls] = (got[:, 0:128] + got[:, 128:256] + nn(low, qbh)) * (1.0 / LOG2E)
        for (r, s, p), (high, low) in zip(chains, dss):
            ls = lanes[p]
            khigh = kh[r, ls]
            got = tn(
                rows_cat(high, low),
                rows_cat(lanes_cat(khigh, kl[r, ls]), lanes_cat(khigh, jnp.zeros_like(khigh))),
            )
            got = joined(got[:, 0:128] + got[:, 128:256]) * 0.125
            low4[QUERY, r, ls] = (dq[r, ls] + got).astype(BF)
        return 0

    lax.fori_loop(0, NB // BU, backward_block, 0)
    w_middle(OUT)
    weight_grads((QUERY,))
    w_scatter(QUERY)
    w_spread(GATE)

    mats, totals = ar_result(1)
    dsum = [m.astype(BF) for m in mats]

    KU = 8

    def key_block(i, _):
        r = block(i, KU * NODES)
        for p in range(PAIRS):
            ls = lanes[p]
            sig = k_sig[r, ls]
            kp = live_rows(i * KU, sig, KU)
            dkp = nt(vh[r, ls], dsum[p]) + totals[p]
            low4[KEY, r, ls] = (dk[r, ls] + dkp * kp * (1.0 - sig)).astype(BF)
            low4[VALUE, r, ls] = (dv[r, ls] + nn(kp.astype(BF), dsum[p])).astype(BF)
        return 0

    lax.fori_loop(0, NB // KU, key_block, 0)
    weight_grads((KEY,))
    w_scatter(KEY)
    weight_grads((VALUE,))
    w_scatter(VALUE)
    w_spread(OUT)

    DC = NR

    def normed_block(b, _):
        r = block(b, RB)
        grads = lanes_cat(*[low4[kind, r, :] for kind in (QUERY, KEY, VALUE, GATE)])
        dn = nt(grads, wall[...])
        dn_own[r, :] = dn[:, 0:W]
        dn_send[r, :] = dn[:, W : 2 * W]
        mean = mean_keep[r, 0:1]
        rstd = rstd_keep[r, 0:1]
        sa = dn[:, 0:W] * gain_own
        sb = dn[:, W : 2 * W] * gain_oth
        ha = (x[r, :].astype(F32) - mean) * rstd
        hb = (xo[r, :].astype(F32) - mean) * rstd
        s1 = jnp.sum(sa, axis=1, keepdims=True) + jnp.sum(sb, axis=1, keepdims=True)
        s2 = jnp.sum(sa * ha, axis=1, keepdims=True) + jnp.sum(sb * hb, axis=1, keepdims=True)
        st_send[r, :] = jnp.where(lane_half, s1, s2)

        @pl.when(lax.rem(b, NR // DC) == NR // DC - 1)
        def _():
            i = b // (NR // DC)
            piece = block(i, R // DC)
            send(dn_send.at[piece], dn_recv.at[piece], dn_sems.at[0, 0], dn_sems.at[0, 2 + i], partner)
            send(st_send.at[piece], st_recv.at[piece], dn_sems.at[0, 1], dn_sems.at[1, 2 + i], partner)

        return 0

    lax.fori_loop(0, NR, normed_block, 0)
    w_middle(KEY)
    w_middle(QUERY)

    def out_block(b, _):
        r = block(b, RB)
        got = nn(mix[r, :], wo[own_rows, :]) + nn(mixo[r, :], wo[oth_rows, :])
        mixo[r, :] = (x[r, :].astype(F32) + got).astype(BF)
        return 0

    w_middle(VALUE)
    lax.fori_loop(0, NR, out_block, 0)
    store(mixo, layer_out)
    w_gather(GATE)
    w_gather(OUT)
    w_spread(KEY)
    w_spread(QUERY)

    def input_block(b, carry):
        @pl.when(lax.rem(b, NR // DC) == 0)
        def _():
            i = b // (NR // DC)
            piece = block(i, R // DC)
            bytes_of(dn_recv.at[piece], dn_sems.at[0, 2 + i])
            bytes_of(st_recv.at[piece], dn_sems.at[1, 2 + i])

        gain_sum, bias_sum = carry
        r = block(b, RB)
        dn = dn_own[r, :] + dn_recv[r, :]
        st = st_send[r, :] + st_recv[r, :]
        mean = mean_keep[r, 0:1]
        rstd = rstd_keep[r, 0:1]
        s1 = st[:, 0:1] * (1.0 / (2 * W))
        s2 = st[:, 64:65] * (1.0 / (2 * W))
        ha = (x[r, :].astype(F32) - mean) * rstd
        inner = rstd * (dn * gain_own - s1 - ha * s2)
        co[r, :] = (c[r, :].astype(F32) + inner).astype(BF)
        return (
            gain_sum + jnp.sum(dn * ha, axis=0, keepdims=True),
            bias_sum + jnp.sum(dn, axis=0, keepdims=True),
        )

    carry = (jnp.zeros((1, W), F32), jnp.zeros((1, W), F32))
    carry = lax.fori_loop(0, NR, input_block, carry)
    store(co, input_grad)
    w_spread(VALUE)
    w_gather(KEY)

    row = lax.broadcasted_iota(jnp.int32, (8, W), 0)
    total = jnp.where(row == 0, carry[0], jnp.where(row == 1, carry[1], 0.0))

    def in_order(total, step, held, index, count, peers):
        gb_part[step] = total
        held[pl.ds(index, 1)] = total[None]
        for _, to in peers:
            send(gb_part.at[step], held.at[index], gb_sems.at[0, step], gb_sems.at[1, step], to)
        return count

    def added(step, held, count):
        wait_both(held.at[pl.ds(0, count - 1)], gb_sems, (step,))
        total = held[0]
        for i in range(1, count):
            total = total + held[i]
        return total

    in_order(total, 0, gb_recv, al, A, a_peers)
    w_gather(VALUE)
    w_gather(QUERY)
    in_order(added(0, gb_recv, A), 1, gb_z, bl, B, b_peers)
    w_keep(GATE)
    w_keep(OUT)
    w_keep(QUERY)
    total = added(1, gb_z, B)
    if C > 1:
        in_order(total, 2, gb_hi, hi, C, h_peers)
        total = added(2, gb_hi, C)
    gain_out[...] = total[0:1].reshape(W)
    bias_out[...] = total[1:2].reshape(W)
    store(gain_out, gain_grad)
    store(bias_out, bias_grad)
    w_keep(KEY)
    w_keep(VALUE)
    for cp in stores:
        cp.wait()
    bytes_of(gbs, core_sems.at[0, 0])
    bytes_of(woo, core_sems.at[0, 1])
    bytes_of(c, core_sems.at[0, 2])
    bytes_of(x, core_sems.at[0, 3])
    bytes_of(mix, mix_sems.at[0])
    bytes_of(dn_send, dn_sems.at[0, 0])
    bytes_of(st_send, dn_sems.at[0, 1])


def shards(
    groups,
    node_input,
    cotangent,
    norm_gain,
    norm_bias,
    query_weight,
    key_weight,
    value_weight,
    gate_weight,
    out_weight,
    adjacent_vertices,
    active_vertex_tally,
    training_period,
):
    A, B, C = groups
    R, W = node_input.shape
    D = 2 * W
    NB = R // NODES
    PAIRS = W // 128
    SR = 64 * PAIRS // A + 8
    PA = D // A
    PB = PA // B
    VM = pltpu.VMEM
    dma = pltpu.SemaphoreType.DMA
    hbm = pl.BlockSpec(memory_space=pl.ANY)
    layer_output, input_grad, gain_grad, bias_grad, fin = pl.pallas_call(
        functools.partial(layer_kernel, groups),
        name="layer_kernel",
        out_shape=(
            jax.ShapeDtypeStruct((R, W), BF),
            jax.ShapeDtypeStruct((R, W), BF),
            jax.ShapeDtypeStruct((W,), F32),
            jax.ShapeDtypeStruct((W,), F32),
            jax.ShapeDtypeStruct((5, D, W), BF),
        ),
        in_specs=[hbm] * 12,
        out_specs=(hbm,) * 5,
        scratch_shapes=[
            VM((W,), BF),
            VM((W,), BF),
            VM((W,), F32),
            VM((W,), F32),
            pltpu.SMEM((NB,), jnp.int32),
            pltpu.SMEM((NB,), jnp.int32),
            VM((R, W), BF),
            VM((R, W), BF),
            VM((R, W), BF),
            VM((R, W), BF),
            VM((D, W), BF),
            VM((adjacent_vertices.shape[1], R), jnp.int32),
            VM((NB, NODES, NODES), F32),
            VM((5, D, W), BF),
            VM((16, W), F32),
            VM((16, W), F32),
            VM((W, W), BF),
            VM((D, 4 * W), BF),
            VM((R, D), BF),
            VM((R, 128), F32),
            VM((R, 128), F32),
            VM((R, W), F32),
            VM((R, W), F32),
            VM((R, W), BF),
            VM((R, W), BF),
            VM((R, W), BF),
            VM((R, W), BF),
            VM((R, W), BF),
            VM((R, W), BF),
            VM((R, W), F32),
            VM((R, W), F32),
            VM((R, W), F32),
            VM((R, W), F32),
            VM((NB, PAIRS, 2, NODES, 2 * NODES), BF),
            VM((R, W), F32),
            VM((R, W), F32),
            VM((4, R, W), BF),
            VM((R, W), BF),
            VM((R, W), BF),
            VM((R, W), F32),
            VM((R, 128), F32),
            VM((R, 128), F32),
            VM((2, A, SR, 128), F32),
            VM((2, A - 1, SR, 128), F32),
            VM((2, SR, 128), F32),
            VM((2, B - 1, SR, 128), F32),
            VM((2, max(C - 1, 1), SR, 128), F32),
            VM((2, A, SR, 128), F32),
            VM((5, D, W), F32),
            VM((5, D, W), BF),
            VM((5, A - 1, PA, W), BF),
            VM((5, PA, W), F32),
            VM((5, B - 1, PB, W), F32),
            VM((5, max(C - 1, 1), PB, W), F32),
            VM((3, 8, W), F32),
            VM((A, 8, W), F32),
            VM((B, 8, W), F32),
            VM((C, 8, W), F32),
            dma((20,)),
            dma((10,)),
            dma((2, 7)),
            dma((2,)),
            dma((2, 6)),
            dma((2, 2, 3)),
            dma((2, 2)),
            dma((2, 5, 4)),
            dma((2, 5)),
            dma((2, 3)),
        ],
        compiler_params=pltpu.CompilerParams(
            collective_id=0, has_side_effects=True, vmem_limit_bytes=63 << 20
        ),
    )(
        node_input,
        cotangent,
        norm_gain,
        norm_bias,
        query_weight,
        key_weight,
        value_weight,
        gate_weight,
        out_weight,
        adjacent_vertices.T,
        active_vertex_tally,
        training_period,
    )
    return pl.pallas_call(
        finish_kernel,
        name="finish_kernel",
        out_shape=(
            jax.ShapeDtypeStruct((R, W), BF),
            jax.ShapeDtypeStruct((R, W), BF),
            jax.ShapeDtypeStruct((W,), F32),
            jax.ShapeDtypeStruct((W,), F32),
        )
        + tuple(jax.ShapeDtypeStruct((D, W), F32) for _ in range(5)),
        in_specs=[hbm] * 5,
        out_specs=(hbm,) * 9,
        scratch_shapes=[
            VM((5, D, W), BF),
            VM((5, D, W), F32),
            VM((2, R, W), BF),
            VM((W,), F32),
            VM((W,), F32),
            dma((18,)),
        ],
    )(layer_output, input_grad, gain_grad, bias_grad, fin)


def finish_kernel(
    lo_in, ig_in, gain_in, bias_in, fin, lo, ig, gain, bias, gq, gk, gv, gg, go, *scratch
):
    low, full, wide, gain_here, bias_here, sems = scratch
    loads, stores = [], []

    def begin(src, dst, into):
        copy = pltpu.make_async_copy(src, dst, sems.at[len(into) + (0 if into is loads else 9)])
        copy.start()
        into.append(copy)

    for i in range(5):
        begin(fin.at[i], low.at[i], loads)
    straight = (
        (lo_in, wide.at[0], lo),
        (ig_in, wide.at[1], ig),
        (gain_in, gain_here, gain),
        (bias_in, bias_here, bias),
    )
    for src, here, _ in straight:
        begin(src, here, loads)
    for i, out in enumerate((gq, gk, gv, gg, go)):
        loads[i].wait()
        full[i] = low[i].astype(F32)
        begin(full.at[i], out, stores)
    for i, (_, here, out) in enumerate(straight):
        loads[5 + i].wait()
        begin(here, out, stores)
    for cp in stores:
        cp.wait()


def factors(count):
    a = 4 if count % 4 == 0 else count
    b = 4 if count % (a * 4) == 0 else count // a
    return a, b, count // (a * b)


def solution(mesh):
    rows = P("graph", "head")
    cols = P(None, "head")
    return jax.shard_map(
        functools.partial(shards, factors(mesh.shape["graph"])),
        mesh=mesh,
        in_specs=(rows, rows, P("head"), P("head"))
        + (cols,) * 5
        + (P("graph", None), P("graph"), P("graph")),
        out_specs=(rows, rows, P("head"), P("head")) + (cols,) * 5,
        check_vma=False,
    )
```

```python
import functools

import jax
import jax.numpy as jnp
from jax import lax
from jax.experimental import pallas as pl
from jax.experimental.pallas import tpu as pltpu
from jax.sharding import PartitionSpec as P

EPS = 1e-05
BETA = 0.9
LOG2E = 1.4426950408889634
BF = jnp.bfloat16
F32 = jnp.float32
MESH = pl.DeviceIdType.MESH
NODES = 128
QUERY, KEY, VALUE, GATE, OUT = 0, 1, 2, 3, 4


def nn(a, b):
    return lax.dot_general(a, b, (((1,), (0,)), ((), ())), preferred_element_type=F32)


def nt(a, b):
    return lax.dot_general(a, b, (((1,), (1,)), ((), ())), preferred_element_type=F32)


def tn(a, b):
    return lax.dot_general(a, b, (((0,), (0,)), ((), ())), preferred_element_type=F32)


def split(a):
    high = a.astype(BF)
    return high, (a - high.astype(F32)).astype(BF)


def rows_cat(*parts):
    return jnp.concatenate(parts, axis=0)


def lanes_cat(*parts):
    return jnp.concatenate(parts, axis=1)


def block(start, size):
    return pl.ds(pl.multiple_of(start * size, size), size)


def layer_kernel(
    groups,
    x_hbm,
    c_hbm,
    gain_hbm,
    bias_hbm,
    wq,
    wk,
    wv,
    wg,
    wo_hbm,
    adjacent_hbm,
    tally_hbm,
    period_hbm,
    layer_out,
    input_grad,
    gain_grad,
    bias_grad,
    fin_hbm,
    gain,
    bias,
    gain_out,
    bias_out,
    tally,
    period,
    x,
    xo,
    c,
    co,
    wo,
    adjacent,
    weight,
    fin,
    gbs,
    gbo,
    woo,
    wall,
    normed,
    mean_keep,
    rstd_keep,
    q_sig,
    k_sig,
    qh,
    ql,
    kh,
    kl,
    vh,
    vl,
    g,
    dmix,
    datt,
    att,
    prob,
    dq,
    dv,
    low4,
    mix,
    mixo,
    dn_recv,
    st_send,
    st_recv,
    sum_part,
    sum_recv,
    sum_mid,
    sum_z,
    sum_hi,
    sum_full,
    part,
    psend,
    precv,
    zpart,
    zrecv,
    hrecv,
    gb_part,
    gb_recv,
    gb_z,
    gb_hi,
    load_sems,
    store_sems,
    core_sems,
    mix_sems,
    dn_sems,
    ar_sems,
    arh_sems,
    w_sems,
    wh_sems,
    gb_sems,
):
    A, B, C = groups
    L = A * B
    R, W = x.shape
    NB = R // NODES
    PAIRS = W // 128
    me = lax.axis_index("graph")
    head = lax.axis_index("head")
    other = 1 - head
    lo = lax.rem(me, L)
    hi = me // L
    al = lax.rem(lo, A)
    bl = lo // A

    def dev(h_, b_, a_):
        return (h_ * L + b_ * A + a_, head)

    a_peers = [(lax.rem(al + d, A), dev(hi, bl, lax.rem(al + d, A))) for d in range(1, A)]
    b_peers = [(lax.rem(bl + d, B), dev(hi, lax.rem(bl + d, B), al)) for d in range(1, B)]
    h_peers = [(lax.rem(hi + d, C), dev(lax.rem(hi + d, C), bl, al)) for d in range(1, C)]
    partner = (me, other)
    own_rows = block(head, W)
    oth_rows = block(other, W)

    def send(src, dst, send_sem, recv_sem, to):
        pltpu.make_async_remote_copy(
            src_ref=src,
            dst_ref=dst,
            send_sem=send_sem,
            recv_sem=recv_sem,
            device_id=to,
            device_id_type=MESH,
        ).start()

    def bytes_of(ref, sem):
        pltpu.make_async_copy(ref, ref, sem).wait()

    def wait_both(ref, sems, index):
        bytes_of(ref, sems.at[(0,) + index])
        bytes_of(ref, sems.at[(1,) + index])

    dk, dn_own, dn_send = att, g, dmix

    barrier = pltpu.get_barrier_semaphore()
    greeted = [partner] + [to for _, to in a_peers + b_peers + h_peers]
    for to in greeted:
        pl.semaphore_signal(barrier, inc=1, device_id=to, device_id_type=MESH)

    loads = []

    def load(src, dst):
        copy = pltpu.make_async_copy(src, dst, load_sems.at[len(loads)])
        copy.start()
        loads.append(copy)
        return copy

    RB = 1024
    NR = R // RB
    XC = NR
    adjacent_load = load(adjacent_hbm, adjacent)
    x_loads = []
    for i in range(XC):
        piece = pl.ds(i * (R // XC), R // XC)
        x_loads.append(load(x_hbm.at[piece], x.at[piece]))
    wo_load = load(wo_hbm, wo)
    c_load = load(c_hbm, c)
    w_loads = []
    for i, w in ((1, wk), (2, wv), (0, wq), (3, wg)):
        cols = pl.ds(i * W, W)
        w_loads.append(load(w.at[own_rows], wall.at[pl.ds(0, W), cols]))
        w_loads.append(load(w.at[oth_rows], wall.at[pl.ds(W, W), cols]))

    stores = []

    def store(src, dst):
        copy = pltpu.make_async_copy(src, dst, store_sems.at[len(stores)])
        copy.start()
        stores.append(copy)

    small_loads = [
        load(gain_hbm, gain),
        load(bias_hbm, bias),
        load(tally_hbm, tally),
        load(period_hbm, period),
    ]
    for cp in small_loads:
        cp.wait()
    gbs[0:8, :] = jnp.broadcast_to(gain[...].astype(F32).reshape(1, W), (8, W))
    gbs[8:16, :] = jnp.broadcast_to(bias[...].astype(F32).reshape(1, W), (8, W))
    node_of = lax.broadcasted_iota(jnp.int32, (NODES, 128), 0)
    def count_block(i, _):
        node = node_of.astype(F32).astype(BF)
        one = jnp.ones((NODES, NODES), BF)
        zero = jnp.zeros((NODES, NODES), BF)
        for s in (2 * i, 2 * i + 1):
            listed = adjacent[:, block(s, NODES)].astype(F32).astype(BF)
            count = zero
            for j in range(listed.shape[0]):
                same = jnp.broadcast_to(listed[j : j + 1, :], (NODES, NODES)) == node
                count = count + jnp.where(same, one, zero)
            count = count.astype(F32)
            weight[s] = jnp.where(
                count > 0.0, jnp.log(jnp.maximum(count, 1.0)) * LOG2E, -1e30
            )
        return 0

    pl.semaphore_wait(barrier, len(greeted))

    send(gbs, gbo, core_sems.at[0, 0], core_sems.at[1, 0], partner)
    pieces = [pl.ds(i * (R // XC), R // XC) for i in range(XC)]
    for i, piece in enumerate(pieces):
        x_loads[i].wait()
        send(x.at[piece], xo.at[piece], core_sems.at[0, 3], core_sems.at[1, 3 + i], partner)
    wo_load.wait()
    send(wo.at[oth_rows], woo, core_sems.at[0, 1], core_sems.at[1, 1], partner)
    c_load.wait()
    send(c, co, core_sems.at[0, 2], core_sems.at[1, 2], partner)

    adjacent_load.wait()
    lax.fori_loop(0, NB // 2, count_block, 0)

    sum_part[...] = jnp.zeros_like(sum_part)
    bytes_of(gbo, core_sems.at[1, 0])
    gain_own, bias_own = gbs[0:1, :], gbs[8:9, :]
    gain_oth, bias_oth = gbo[0:1, :], gbo[8:9, :]
    lane_half = lax.broadcasted_iota(jnp.int32, (1, 128), 1) < 64

    def live_rows(first, a, count):
        node = lax.broadcasted_iota(jnp.int32, (NODES, a.shape[1]), 0)
        return rows_cat(
            *[
                jnp.where(node < tally[first + i], a[i * NODES : (i + 1) * NODES], 0.0)
                for i in range(count)
            ]
        )

    def norm_block(b, carry):
        @pl.when(lax.rem(b, NR // XC) == 0)
        def _():
            i = b // (NR // XC)
            bytes_of(xo.at[block(i, R // XC)], core_sems.at[1, 3 + i])

        r = block(b, RB)
        xa = x[r, :].astype(F32)
        xb = xo[r, :].astype(F32)
        mean = (
            jnp.sum(xa, axis=1, keepdims=True) + jnp.sum(xb, axis=1, keepdims=True)
        ) * (1.0 / (2 * W))
        xa = xa - mean
        xb = xb - mean
        var = (
            jnp.sum(xa * xa, axis=1, keepdims=True) + jnp.sum(xb * xb, axis=1, keepdims=True)
        ) * (1.0 / (2 * W))
        rstd = lax.rsqrt(var + EPS)
        mean_keep[r, :] = jnp.broadcast_to(mean, (RB, 128))
        rstd_keep[r, :] = jnp.broadcast_to(rstd, (RB, 128))
        na = (xa * rstd * gain_own + bias_own).astype(BF)
        nb = (xb * rstd * gain_oth + bias_oth).astype(BF)
        normed[r, 0:W] = na
        normed[r, W : 2 * W] = nb
        kv = nn(lanes_cat(na, nb), wall[:, W : 3 * W])
        kk = kv[:, 0:W]
        vv = kv[:, W : 2 * W]
        kh[r, :], kl[r, :] = split(kk)
        vbf, vlow = split(vv)
        vh[r, :] = vbf
        vl[r, :] = vlow
        sig = jax.nn.sigmoid(kk)
        k_sig[r, :] = sig
        kp = live_rows(b * (RB // NODES), sig, RB // NODES)
        kpb = kp.astype(BF)
        sums, totals = carry
        new_sums, new_totals = [], []
        for p in range(PAIRS):
            ls = slice(p * 128, (p + 1) * 128)
            new_sums.append(sums[p] + tn(kpb[:, ls], vbf[:, ls]))
            new_totals.append(totals[p] + jnp.sum(kp[:, ls], axis=0, keepdims=True))
        return tuple(new_sums), tuple(new_totals)

    def zero_sums():
        return (
            tuple(jnp.zeros((128, 128), F32) for _ in range(PAIRS)),
            tuple(jnp.zeros((1, 128), F32) for _ in range(PAIRS)),
        )

    for cp in w_loads[0:4]:
        cp.wait()
    carry = lax.fori_loop(0, NR, norm_block, zero_sums())

    def pack_sums(slot, carry):
        sums, totals = carry
        packed = rows_cat(
            *[jnp.where(lane_half, sums[p][0:64], sums[p][64:128]) for p in range(PAIRS)]
        )
        for j in range(A):
            sum_part[slot, j, 0:SR, :] = packed[j * SR : (j + 1) * SR]
            for p in range(PAIRS):
                sum_part[slot, j, SR + p : SR + p + 1, :] = totals[p]

    SR = 64 * PAIRS // A

    def ar_scatter(slot):
        for i, (j, to) in enumerate(a_peers):
            send(
                sum_part.at[slot, j],
                sum_recv.at[slot, i],
                ar_sems.at[0, slot, 0],
                ar_sems.at[1, slot, 0],
                to,
            )

    def ar_middle(slot):
        wait_both(sum_recv.at[slot], ar_sems, (slot, 0))
        total = sum_part[slot, al]
        for i in range(A - 1):
            total = total + sum_recv[slot, i]
        sum_mid[slot] = total
        for i, (_, to) in enumerate(b_peers):
            send(
                sum_mid.at[slot],
                sum_z.at[slot, i],
                ar_sems.at[0, slot, 1],
                ar_sems.at[1, slot, 1],
                to,
            )

    def ar_gather(slot):
        wait_both(sum_z.at[slot], ar_sems, (slot, 1))
        total = sum_mid[slot]
        for i in range(B - 1):
            total = total + sum_z[slot, i]
        if C > 1:
            sum_mid[slot] = total
            for i, (_, to) in enumerate(h_peers):
                send(
                    sum_mid.at[slot],
                    sum_hi.at[slot, i],
                    arh_sems.at[0, slot],
                    arh_sems.at[1, slot],
                    to,
                )
            wait_both(sum_hi.at[slot], arh_sems, (slot,))
            for i in range(C - 1):
                total = total + sum_hi[slot, i]
        sum_full[slot, al] = total
        for i, (_, to) in enumerate(a_peers):
            send(
                sum_full.at[slot, al],
                sum_full.at[slot, al],
                ar_sems.at[0, slot, 2],
                ar_sems.at[1, slot, 2],
                to,
            )

    def ar_result(slot):
        wait_both(sum_recv.at[slot], ar_sems, (slot, 2))
        mats, totals = [], []
        packed = rows_cat(*[sum_full[slot, j, 0:SR, :] for j in range(A)])
        for p in range(PAIRS):
            own = packed[p * 64 : (p + 1) * 64]
            mats.append(rows_cat(jnp.where(lane_half, own, 0.0), jnp.where(lane_half, 0.0, own)))
            totals.append(sum_full[slot, 0, SR + p : SR + p + 1, :])
        return mats, totals

    pack_sums(0, carry)
    ar_scatter(0)

    for cp in w_loads[4:]:
        cp.wait()
    bytes_of(woo, core_sems.at[1, 1])
    bytes_of(co, core_sems.at[1, 2])

    def gate_block(b, _):
        r = block(b, RB)
        n = normed[r, :]
        qq = nn(n, wall[:, 0:W])
        q_sig[r, :] = jax.nn.sigmoid(qq)
        qh[r, :], ql[r, :] = split(qq * (0.125 * LOG2E))
        gg = nn(n, wall[:, 3 * W : 4 * W])
        g[r, :] = gg
        dm = nt(lanes_cat(c[r, :], co[r, :]), lanes_cat(wo[own_rows, :], woo[...]))
        dmix[r, :] = dm
        datt[r, :] = dm * ((1.0 - BETA) * gg + BETA)
        return 0

    lax.fori_loop(0, NR, gate_block, 0)
    ar_middle(0)

    half_row = jnp.where(lane_half, 1.0, 0.0)
    half_a = jnp.broadcast_to(half_row, (NODES, 128)).astype(BF)
    half_b = jnp.broadcast_to(1.0 - half_row, (NODES, 128)).astype(BF)

    def apart(a):
        return rows_cat(a * half_a, a * half_b)

    def joined(a):
        return jnp.where(lane_half, a[0:NODES], a[NODES : 2 * NODES])

    FU = 4
    lanes = [slice(p * 128, (p + 1) * 128) for p in range(PAIRS)]

    def forward_block(i, _):
        @pl.when(i == 3)
        def _():
            ar_gather(0)

        chains = [(i * FU + u, p) for u in range(FU) for p in range(PAIRS)]
        scores = []
        for s, p in chains:
            r, ls = block(s, NODES), lanes[p]
            high, low = kh[r, ls], kl[r, ls]
            qbh = apart(qh[r, ls])
            scores.append(
                nt(lanes_cat(high, low, high), lanes_cat(qbh, qbh, apart(ql[r, ls])))
            )
        probs = []
        for j, score in enumerate(scores):
            bias = weight[chains[j][0]]
            score = score + lanes_cat(bias, bias)
            e = jnp.exp2(score - jnp.max(score, axis=0, keepdims=True))
            probs.append(split(e * (1.0 / jnp.sum(e, axis=0, keepdims=True))))
        for (s, p), (high, low) in zip(chains, probs):
            prob[s, p, 0] = high
            prob[s, p, 1] = low
        for (s, p), (high, low) in zip(chains, probs):
            r, ls = block(s, NODES), lanes[p]
            vhigh = vh[r, ls]
            o = tn(
                rows_cat(high, low),
                rows_cat(lanes_cat(vhigh, vl[r, ls]), lanes_cat(vhigh, jnp.zeros_like(vhigh))),
            )
            att[r, ls] = joined(o[:, 0:128] + o[:, 128:256])
        return 0

    lax.fori_loop(0, NB // FU, forward_block, 0)

    def value_block(i, _):
        chains = [(i * BU + u, p) for u in range(BU) for p in range(PAIRS)]
        outs = []
        for s, p in chains:
            oh, ol = split(datt[block(s, NODES), lanes[p]])
            outs.append((apart(oh), apart(ol)))
        for (s, p), (oh, ol) in zip(chains, outs):
            got = nn(prob[s, p, 0], lanes_cat(oh, ol))
            got = got[:, 0:128] + got[:, 128:256] + nn(prob[s, p, 1], oh)
            dv[block(s, NODES), lanes[p]] = got
        return 0

    BU = 4
    lax.fori_loop(0, NB // BU, value_block, 0)

    mats, totals = ar_result(0)
    square = (2, 128, 128)
    same_head = (lax.broadcasted_iota(jnp.int32, (128, 128), 0) < 64) == (
        lax.broadcasted_iota(jnp.int32, (128, 128), 1) < 64
    )
    ones_bd = jnp.where(same_head, 1.0, 0.0).astype(BF)
    num_w, den_w, back_w = [], [], []
    for p in range(PAIRS):
        sh, sl = split(mats[p])
        th, tl = split(jnp.where(same_head, jnp.broadcast_to(totals[p], (128, 128)), 0.0))
        num_w.append(lanes_cat(sh, sl))
        den_w.append(rows_cat(th, tl))
        back_w.append(lanes_cat(sh, sh, sl))

    GU = 8

    def glob_block(i, carry):
        r = block(i, GU * NODES)
        keep = [(1 - period[i * GU + u]).astype(F32) for u in range(GU)]
        sums, tots = carry
        new_sums, new_tots = [], []
        for p in range(PAIRS):
            ls = lanes[p]
            qp = q_sig[r, ls]
            qpb = qp.astype(BF)
            num = nn(qpb, num_w[p])
            den = nt(qpb, den_w[p])
            inv = 1.0 / (den[:, 0:128] + den[:, 128:256])
            glob = (num[:, 0:128] + num[:, 128:256]) * inv
            at = att[r, ls] + glob
            mix[r, ls] = ((1.0 - BETA) * g[r, ls] * at + BETA * at).astype(BF)
            low4[GATE, r, ls] = (dmix[r, ls] * (1.0 - BETA) * at).astype(BF)
            da = datt[r, ls]
            dnum = rows_cat(*[keep[u] * da[u * NODES : (u + 1) * NODES] for u in range(GU)]) * inv
            dh, dl = split(dnum)
            th, tl = split(dnum * glob)
            dden = -nn(lanes_cat(th, tl), rows_cat(ones_bd, ones_bd))
            dqp = nt(lanes_cat(dh, dl, dh), back_w[p]) + dden * totals[p]
            dq[r, ls] = dqp * qp * (1.0 - qp)
            new_sums.append(sums[p] + tn(qpb, dh))
            new_tots.append(tots[p] + jnp.sum(dden * qp, axis=0, keepdims=True))
        return tuple(new_sums), tuple(new_tots)

    carry = lax.fori_loop(0, NB // GU, glob_block, zero_sums())
    pack_sums(1, carry)
    ar_scatter(1)
    send(mix, mixo, mix_sems.at[0], mix_sems.at[1], partner)


    def keep_part(kind, rows, got):
        part[kind, rows, :] = got
        psend[kind, rows, :] = got.astype(BF)

    def weight_grads(kind):
        got = tn(normed[...], low4[kind])
        keep_part(kind, own_rows, got[0:W])
        keep_part(kind, oth_rows, got[W : 2 * W])

    def out_grads():
        keep_part(OUT, own_rows, tn(mix[...], c[...]))
        keep_part(OUT, oth_rows, tn(mixo[...], c[...]))

    D = 2 * W
    PA = D // A
    PB = PA // B

    B_FIRST = (QUERY,) if A == B else ()

    def order(w):
        first, second = (al, a_peers), (bl, b_peers)
        return (second, first) if w in B_FIRST else (first, second)

    def w_scatter(w):
        for i, (j, to) in enumerate(order(w)[0][1]):
            send(
                psend.at[w, block(j, PA)],
                precv.at[w, i],
                w_sems.at[0, w, 0],
                w_sems.at[1, w, 0],
                to,
            )

    def w_middle(w):
        (mine, _), (_, peers) = order(w)
        wait_both(precv.at[w], w_sems, (w, 0))
        total = part[w, block(mine, PA), :]
        for i in range(A - 1):
            total = total + precv[w, i].astype(F32)
        zpart[w] = total
        for i, (j, to) in enumerate(peers):
            send(
                zpart.at[w, block(j, PB)],
                zrecv.at[w, i],
                w_sems.at[0, w, 1],
                w_sems.at[1, w, 1],
                to,
            )

    def share(w):
        (first, _), (second, _) = order(w)
        return pl.ds(pl.multiple_of(first * PA + second * PB, PB), PB)

    def w_spread(w):
        _, (mine, peers) = order(w)
        wait_both(zrecv.at[w], w_sems, (w, 1))
        total = zpart[w, block(mine, PB), :]
        for i in range(B - 1):
            total = total + zrecv[w, i]
        if C > 1:
            zpart[w, block(mine, PB), :] = total
            for i, (_, to) in enumerate(h_peers):
                send(
                    zpart.at[w, block(mine, PB)],
                    hrecv.at[w, i],
                    wh_sems.at[0, w],
                    wh_sems.at[1, w],
                    to,
                )
            wait_both(hrecv.at[w], wh_sems, (w,))
            for i in range(C - 1):
                total = total + hrecv[w, i]
        fin[w, share(w), :] = total.astype(BF)
        for _, to in peers:
            send(
                fin.at[w, share(w)],
                fin.at[w, share(w)],
                w_sems.at[0, w, 2],
                w_sems.at[1, w, 2],
                to,
            )

    def w_gather(w):
        mine, peers = order(w)[0]
        wait_both(fin.at[w, pl.ds(0, (B - 1) * PB)], w_sems, (w, 2))
        for _, to in peers:
            send(
                fin.at[w, block(mine, PA)],
                fin.at[w, block(mine, PA)],
                w_sems.at[0, w, 3],
                w_sems.at[1, w, 3],
                to,
            )

    def w_keep(w):
        wait_both(fin.at[w, pl.ds(0, (A - 1) * PA)], w_sems, (w, 3))
        store(fin.at[w], fin_hbm.at[w])

    weight_grads(GATE)
    w_scatter(GATE)
    bytes_of(mixo, mix_sems.at[1])
    out_grads()
    w_scatter(OUT)

    def backward_block(i, _):
        @pl.when(i == 1)
        def _():
            ar_middle(1)

        @pl.when(i == 2)
        def _():
            w_middle(GATE)

        @pl.when(i == 3)
        def _():
            ar_gather(1)

        chains = [(block(i * BU + u, NODES), i * BU + u, p) for u in range(BU) for p in range(PAIRS)]
        dps = []
        for r, s, p in chains:
            ls = lanes[p]
            oh, ol = split(datt[r, ls])
            oh, ol = apart(oh), apart(ol)
            high = vh[r, ls]
            dps.append(nt(lanes_cat(high, vl[r, ls], high), lanes_cat(oh, oh, ol)))
        dss = []
        for (r, s, p), dp in zip(chains, dps):
            pr = prob[s, p, 0].astype(F32) + prob[s, p, 1].astype(F32)
            dss.append(split(pr * (dp - jnp.sum(pr * dp, axis=0, keepdims=True))))
        for (r, s, p), (high, low) in zip(chains, dss):
            ls = lanes[p]
            qbh = apart(qh[r, ls])
            got = nn(high, lanes_cat(qbh, apart(ql[r, ls])))
            dk[r, ls] = (got[:, 0:128] + got[:, 128:256] + nn(low, qbh)) * (1.0 / LOG2E)
        for (r, s, p), (high, low) in zip(chains, dss):
            ls = lanes[p]
            khigh = kh[r, ls]
            got = tn(
                rows_cat(high, low),
                rows_cat(lanes_cat(khigh, kl[r, ls]), lanes_cat(khigh, jnp.zeros_like(khigh))),
            )
            got = joined(got[:, 0:128] + got[:, 128:256]) * 0.125
            low4[QUERY, r, ls] = (dq[r, ls] + got).astype(BF)
        return 0

    lax.fori_loop(0, NB // BU, backward_block, 0)
    w_middle(OUT)
    weight_grads(QUERY)
    w_scatter(QUERY)
    w_spread(GATE)

    mats, totals = ar_result(1)
    dsum = [m.astype(BF) for m in mats]

    KU = 8

    def key_block(i, _):
        r = block(i, KU * NODES)
        for p in range(PAIRS):
            ls = lanes[p]
            sig = k_sig[r, ls]
            kp = live_rows(i * KU, sig, KU)
            dkp = nt(vh[r, ls], dsum[p]) + totals[p]
            low4[KEY, r, ls] = (dk[r, ls] + dkp * kp * (1.0 - sig)).astype(BF)
            low4[VALUE, r, ls] = (dv[r, ls] + nn(kp.astype(BF), dsum[p])).astype(BF)
        return 0

    lax.fori_loop(0, NB // KU, key_block, 0)
    weight_grads(KEY)
    w_scatter(KEY)
    weight_grads(VALUE)
    w_scatter(VALUE)
    w_spread(OUT)

    DC = NR

    def normed_block(b, _):
        r = block(b, RB)
        grads = lanes_cat(*[low4[kind, r, :] for kind in (QUERY, KEY, VALUE, GATE)])
        dn = nt(grads, wall[...])
        dn_own[r, :] = dn[:, 0:W]
        dn_send[r, :] = dn[:, W : 2 * W]
        mean = mean_keep[r, 0:1]
        rstd = rstd_keep[r, 0:1]
        sa = dn[:, 0:W] * gain_own
        sb = dn[:, W : 2 * W] * gain_oth
        ha = (x[r, :].astype(F32) - mean) * rstd
        hb = (xo[r, :].astype(F32) - mean) * rstd
        s1 = jnp.sum(sa, axis=1, keepdims=True) + jnp.sum(sb, axis=1, keepdims=True)
        s2 = jnp.sum(sa * ha, axis=1, keepdims=True) + jnp.sum(sb * hb, axis=1, keepdims=True)
        st_send[r, :] = jnp.where(lane_half, s1, s2)

        @pl.when(lax.rem(b, NR // DC) == NR // DC - 1)
        def _():
            i = b // (NR // DC)
            piece = block(i, R // DC)
            send(dn_send.at[piece], dn_recv.at[piece], dn_sems.at[0, 0], dn_sems.at[0, 2 + i], partner)
            send(st_send.at[piece], st_recv.at[piece], dn_sems.at[0, 1], dn_sems.at[1, 2 + i], partner)

        return 0

    lax.fori_loop(0, NR, normed_block, 0)
    w_middle(KEY)
    w_middle(QUERY)

    def out_block(b, _):
        r = block(b, RB)
        got = nn(mix[r, :], wo[own_rows, :]) + nn(mixo[r, :], wo[oth_rows, :])
        mixo[r, :] = (x[r, :].astype(F32) + got).astype(BF)
        return 0

    w_middle(VALUE)
    lax.fori_loop(0, NR, out_block, 0)
    store(mixo, layer_out)
    w_gather(GATE)
    w_gather(OUT)
    w_spread(KEY)
    w_spread(QUERY)

    def input_block(b, carry):
        @pl.when(lax.rem(b, NR // DC) == 0)
        def _():
            i = b // (NR // DC)
            piece = block(i, R // DC)
            bytes_of(dn_recv.at[piece], dn_sems.at[0, 2 + i])
            bytes_of(st_recv.at[piece], dn_sems.at[1, 2 + i])

        gain_sum, bias_sum = carry
        r = block(b, RB)
        dn = dn_own[r, :] + dn_recv[r, :]
        st = st_send[r, :] + st_recv[r, :]
        mean = mean_keep[r, 0:1]
        rstd = rstd_keep[r, 0:1]
        s1 = st[:, 0:1] * (1.0 / (2 * W))
        s2 = st[:, 64:65] * (1.0 / (2 * W))
        ha = (x[r, :].astype(F32) - mean) * rstd
        inner = rstd * (dn * gain_own - s1 - ha * s2)
        co[r, :] = (c[r, :].astype(F32) + inner).astype(BF)
        return (
            gain_sum + jnp.sum(dn * ha, axis=0, keepdims=True),
            bias_sum + jnp.sum(dn, axis=0, keepdims=True),
        )

    carry = (jnp.zeros((1, W), F32), jnp.zeros((1, W), F32))
    carry = lax.fori_loop(0, NR, input_block, carry)
    store(co, input_grad)
    w_spread(VALUE)
    w_gather(KEY)
    w_gather(QUERY)

    row = lax.broadcasted_iota(jnp.int32, (8, W), 0)
    total = jnp.where(row == 0, carry[0], jnp.where(row == 1, carry[1], 0.0))

    def in_order(total, step, held, index, count, peers):
        gb_part[step] = total
        held[pl.ds(index, 1)] = total[None]
        for _, to in peers:
            send(gb_part.at[step], held.at[index], gb_sems.at[0, step], gb_sems.at[1, step], to)
        return count

    def added(step, held, count):
        wait_both(held.at[pl.ds(0, count - 1)], gb_sems, (step,))
        total = held[0]
        for i in range(1, count):
            total = total + held[i]
        return total

    in_order(total, 0, gb_recv, al, A, a_peers)
    w_gather(VALUE)
    in_order(added(0, gb_recv, A), 1, gb_z, bl, B, b_peers)
    w_keep(GATE)
    w_keep(OUT)
    w_keep(QUERY)
    total = added(1, gb_z, B)
    if C > 1:
        in_order(total, 2, gb_hi, hi, C, h_peers)
        total = added(2, gb_hi, C)
    gain_out[...] = total[0:1].reshape(W)
    bias_out[...] = total[1:2].reshape(W)
    store(gain_out, gain_grad)
    store(bias_out, bias_grad)
    w_keep(KEY)
    w_keep(VALUE)
    for cp in stores:
        cp.wait()
    bytes_of(gbs, core_sems.at[0, 0])
    bytes_of(woo, core_sems.at[0, 1])
    bytes_of(c, core_sems.at[0, 2])
    bytes_of(x, core_sems.at[0, 3])
    bytes_of(mix, mix_sems.at[0])
    bytes_of(dn_send, dn_sems.at[0, 0])
    bytes_of(st_send, dn_sems.at[0, 1])


def shards(
    groups,
    node_input,
    cotangent,
    norm_gain,
    norm_bias,
    query_weight,
    key_weight,
    value_weight,
    gate_weight,
    out_weight,
    adjacent_vertices,
    active_vertex_tally,
    training_period,
):
    A, B, C = groups
    R, W = node_input.shape
    D = 2 * W
    NB = R // NODES
    PAIRS = W // 128
    SR = 64 * PAIRS // A + 8
    PA = D // A
    PB = PA // B
    VM = pltpu.VMEM
    dma = pltpu.SemaphoreType.DMA
    hbm = pl.BlockSpec(memory_space=pl.ANY)
    layer_output, input_grad, gain_grad, bias_grad, fin = pl.pallas_call(
        functools.partial(layer_kernel, groups),
        name="layer_kernel",
        out_shape=(
            jax.ShapeDtypeStruct((R, W), BF),
            jax.ShapeDtypeStruct((R, W), BF),
            jax.ShapeDtypeStruct((W,), F32),
            jax.ShapeDtypeStruct((W,), F32),
            jax.ShapeDtypeStruct((5, D, W), BF),
        ),
        in_specs=[hbm] * 12,
        out_specs=(hbm,) * 5,
        scratch_shapes=[
            VM((W,), BF),
            VM((W,), BF),
            VM((W,), F32),
            VM((W,), F32),
            pltpu.SMEM((NB,), jnp.int32),
            pltpu.SMEM((NB,), jnp.int32),
            VM((R, W), BF),
            VM((R, W), BF),
            VM((R, W), BF),
            VM((R, W), BF),
            VM((D, W), BF),
            VM((adjacent_vertices.shape[1], R), jnp.int32),
            VM((NB, NODES, NODES), F32),
            VM((5, D, W), BF),
            VM((16, W), F32),
            VM((16, W), F32),
            VM((W, W), BF),
            VM((D, 4 * W), BF),
            VM((R, D), BF),
            VM((R, 128), F32),
            VM((R, 128), F32),
            VM((R, W), F32),
            VM((R, W), F32),
            VM((R, W), BF),
            VM((R, W), BF),
            VM((R, W), BF),
            VM((R, W), BF),
            VM((R, W), BF),
            VM((R, W), BF),
            VM((R, W), F32),
            VM((R, W), F32),
            VM((R, W), F32),
            VM((R, W), F32),
            VM((NB, PAIRS, 2, NODES, 2 * NODES), BF),
            VM((R, W), F32),
            VM((R, W), F32),
            VM((4, R, W), BF),
            VM((R, W), BF),
            VM((R, W), BF),
            VM((R, W), F32),
            VM((R, 128), F32),
            VM((R, 128), F32),
            VM((2, A, SR, 128), F32),
            VM((2, A - 1, SR, 128), F32),
            VM((2, SR, 128), F32),
            VM((2, B - 1, SR, 128), F32),
            VM((2, max(C - 1, 1), SR, 128), F32),
            VM((2, A, SR, 128), F32),
            VM((5, D, W), F32),
            VM((5, D, W), BF),
            VM((5, A - 1, PA, W), BF),
            VM((5, PA, W), F32),
            VM((5, B - 1, PB, W), F32),
            VM((5, max(C - 1, 1), PB, W), F32),
            VM((3, 8, W), F32),
            VM((A, 8, W), F32),
            VM((B, 8, W), F32),
            VM((C, 8, W), F32),
            dma((20,)),
            dma((10,)),
            dma((2, 7)),
            dma((2,)),
            dma((2, 6)),
            dma((2, 2, 3)),
            dma((2, 2)),
            dma((2, 5, 4)),
            dma((2, 5)),
            dma((2, 3)),
        ],
        compiler_params=pltpu.CompilerParams(
            collective_id=0, has_side_effects=True, vmem_limit_bytes=63 << 20
        ),
    )(
        node_input,
        cotangent,
        norm_gain,
        norm_bias,
        query_weight,
        key_weight,
        value_weight,
        gate_weight,
        out_weight,
        adjacent_vertices.T,
        active_vertex_tally,
        training_period,
    )
    return pl.pallas_call(
        finish_kernel,
        name="finish_kernel",
        out_shape=(
            jax.ShapeDtypeStruct((R, W), BF),
            jax.ShapeDtypeStruct((R, W), BF),
            jax.ShapeDtypeStruct((W,), F32),
            jax.ShapeDtypeStruct((W,), F32),
        )
        + tuple(jax.ShapeDtypeStruct((D, W), F32) for _ in range(5)),
        in_specs=[hbm] * 5,
        out_specs=(hbm,) * 9,
        scratch_shapes=[
            VM((5, D, W), BF),
            VM((5, D, W), F32),
            VM((2, R, W), BF),
            VM((W,), F32),
            VM((W,), F32),
            dma((18,)),
        ],
    )(layer_output, input_grad, gain_grad, bias_grad, fin)


def finish_kernel(
    lo_in, ig_in, gain_in, bias_in, fin, lo, ig, gain, bias, gq, gk, gv, gg, go, *scratch
):
    low, full, wide, gain_here, bias_here, sems = scratch
    loads, stores = [], []

    def begin(src, dst, into):
        copy = pltpu.make_async_copy(src, dst, sems.at[len(into) + (0 if into is loads else 9)])
        copy.start()
        into.append(copy)

    for i in range(5):
        begin(fin.at[i], low.at[i], loads)
    straight = (
        (lo_in, wide.at[0], lo),
        (ig_in, wide.at[1], ig),
        (gain_in, gain_here, gain),
        (bias_in, bias_here, bias),
    )
    for src, here, _ in straight:
        begin(src, here, loads)
    for i, out in enumerate((gq, gk, gv, gg, go)):
        loads[i].wait()
        full[i] = low[i].astype(F32)
        begin(full.at[i], out, stores)
    for i, (_, here, out) in enumerate(straight):
        loads[5 + i].wait()
        begin(here, out, stores)
    for cp in stores:
        cp.wait()


def factors(count):
    a = 4 if count % 4 == 0 else count
    b = 4 if count % (a * 4) == 0 else count // a
    return a, b, count // (a * b)


def solution(mesh):
    rows = P("graph", "head")
    cols = P(None, "head")
    return jax.shard_map(
        functools.partial(shards, factors(mesh.shape["graph"])),
        mesh=mesh,
        in_specs=(rows, rows, P("head"), P("head"))
        + (cols,) * 5
        + (P("graph", None), P("graph"), P("graph")),
        out_specs=(rows, rows, P("head"), P("head")) + (cols,) * 5,
        check_vma=False,
    )
```
